128 devices in a mesh: tex: 8 (over x, core), view: 16 (over y, z).
Axes of the slice: x: 4, y: 4, z: 4, core: 2. Of those that a mesh axis runs over, the one named last changes fastest.
Arguments:
- texel_atlas: float32 [128, 10, 4096], P(('tex', 'view'))
- observed: float32 [128, 3, 768], P('view'), may hold values from -5 to 5
- geometry: float32 [128, 6, 768], P('view'), may hold values from -1 to 1
- block_ids: int32 [128, 8, 4], P('view', 'tex'), may hold values from -1 to 15, as said below
- pixel_slot: int32 [128, 768], P('view'), may hold values from 0 to 31, as said below
- corner: int32 [128, 768], P('view'), may hold values from 0 to 3968
- bilinear_frac: float32 [128, 2, 768], P('view'), may hold values from 0 to 1
Outputs:
- update: float32 [128, 10, 4096], P(('tex', 'view'))
- solve_residual: float32 [128, 10, 4096], P(('tex', 'view'))
The draws below stay inside these ranges and needn't reach their ends.
Inputs may be any that keep to these rules, and one draw needn't show every extreme that they name: `block_ids`: -1 marks an empty slot; for each image tile and owner the live slots come first, one to 4 of them. `pixel_slot`: always names a live slot of the pixel's own tile.
All inputs are finite; a program needn't handle non-finite values.
Results may differ from the reference program's by a relative error of at most 0.0023.
Values sent between devices are 32-bit elements; how exact they have to be, the bound alone decides.
A program may use at most 128 MiB of HBM per device.

```python
import math
import jax
import jax.numpy as jnp
from jax import lax

C = 10
BSIDE = 64
BT = 4096
SLOTS = 4
P_SIZE = 768
ITERS = 2
OWNERS = 8
RANGE = 16
NBLK = 128
NTILE = 128


low_ends = [0.05, 0.05, 0.05, 0.02, 0.02, 0.02, 0.4, -0.3, -0.3, 0.3]


high_ends = [0.9, 0.9, 0.9, 0.5, 0.5, 0.5, 0.9, 0.3, 0.3, 1.0]


def tile_counts(key):
    key = jax.random.fold_in(key, 100)
    counts = jax.random.randint(key, (NTILE, OWNERS), 1, SLOTS + 1)
    counts = counts.at[0].set(SLOTS)
    return counts.at[1, 0].set(1)


def draw_texel_atlas(key, part):
    key = jax.random.fold_in(key, 11)
    unit = jax.random.uniform(key, (NBLK, C, BT), jnp.float32)
    lower = jnp.array(low_ends, jnp.float32)[None, :, None]
    upper = jnp.array(high_ends, jnp.float32)[None, :, None]
    return lower + (upper - lower) * unit


def direction_draw(key):
    height_key, angle_key = jax.random.split(key)
    height = jax.random.uniform(height_key, (NTILE, 1, P_SIZE), jnp.float32, 0.72, 1.0)
    angle = jax.random.uniform(angle_key, (NTILE, 1, P_SIZE), jnp.float32, -math.pi, math.pi)
    radial = jnp.sqrt(1.0 - height * height)
    return jnp.concatenate([radial * jnp.cos(angle), radial * jnp.sin(angle), height], axis=1)


def draw_geometry(key, part):
    key = jax.random.fold_in(key, 12)
    light_key, view_key = jax.random.split(key)
    return jnp.concatenate([direction_draw(light_key), direction_draw(view_key)], axis=1)


def draw_block_ids(key, part):
    counts = tile_counts(key)
    key = jax.random.fold_in(key, 13)
    within = jax.random.randint(key, (NTILE, OWNERS, SLOTS), 0, RANGE)
    within = within.at[0, :, 0].set(RANGE - 1).at[0, :, 1].set(0)
    live = jnp.arange(SLOTS, dtype=jnp.int32)[None, None, :] < counts[:, :, None]
    return jnp.where(live, within, -1).astype(jnp.int32)


def draw_pixel_slot(key, part):
    counts = tile_counts(key)
    key = jax.random.fold_in(key, 14)
    owner_key, slot_key = jax.random.split(key)
    owner_pick = jax.random.randint(owner_key, (NTILE, P_SIZE), 0, OWNERS)
    limit = jnp.take_along_axis(counts, owner_pick, axis=1)
    slot_within = jax.random.randint(slot_key, (NTILE, P_SIZE), 0, limit)
    slots_drawn = owner_pick * SLOTS + slot_within
    return slots_drawn.at[0, 0].set(OWNERS * SLOTS - 1).at[0, 1].set(0).astype(jnp.int32)


def set_ends(values, own_key, least, largest):
    extent = values.shape
    spot = [jax.random.randint(jax.random.fold_in(own_key, axis), (), 0, extent[axis]) for axis in range(len(extent))]
    values = values.at[tuple(spot)].set(least)
    longest = extent.index(max(extent))
    spot[longest] = (spot[longest] + 1) % extent[longest]
    return values.at[tuple(spot)].set(largest)


def steps_of(stream_key, extent, pieces, smallest, high):
    factor_of = 1.0
    for dim, shards_of in pieces:
        steps = jax.random.uniform(jax.random.fold_in(jax.random.fold_in(stream_key, 6), dim), (shards_of,), jnp.float32, smallest / len(pieces), high / len(pieces))
        factor_of = factor_of * jnp.repeat(jnp.exp(steps), extent[dim] // shards_of).reshape((-1,) + (1,) * (len(extent) - 1 - dim))
    return factor_of


def gaussian(key, shape, scale, most, cuts=(), kind=jnp.bfloat16):
    values = jax.random.normal(key, shape, jnp.float32) * scale
    if len(cuts) > 0:
        values = steps_of(key, shape, cuts, -0.22, 0.18) * values
    return jnp.clip(values, min=-most, max=most).astype(kind)


def setup_inputs(seed: int = 0) -> dict:
    key_of = jax.random.split(jax.random.key(seed), 8)
    texel_atlas = draw_texel_atlas(jax.random.fold_in(key_of[7], 71), 0)
    observed = gaussian(key_of[1], (NTILE, 3, P_SIZE), 1.0, 5.0, ((0, 16),), jnp.float32)
    geometry = draw_geometry(jax.random.fold_in(key_of[7], 71), 0)
    block_ids = draw_block_ids(jax.random.fold_in(key_of[7], 71), 0)
    pixel_slot = draw_pixel_slot(jax.random.fold_in(key_of[7], 71), 0)
    corner = set_ends(jax.random.randint(key_of[5], (NTILE, P_SIZE), 0, (BSIDE - 1) * (BSIDE - 1)), jax.random.fold_in(key_of[5], 1), 0, ((BSIDE - 1) * (BSIDE - 1)) - 1).astype(jnp.int32)
    bilinear_frac = jnp.clip(1.0 * jax.random.uniform(key_of[6], (NTILE, 2, P_SIZE), jnp.float32) ** steps_of(key_of[6], (NTILE, 2, P_SIZE), ((0, 16),), -0.2, 0.2), 0.0, 1.0)
    return {"texel_atlas": texel_atlas, "observed": observed, "geometry": geometry, "block_ids": block_ids, "pixel_slot": pixel_slot, "corner": corner, "bilinear_frac": bilinear_frac}


DAMPING = 0.1

def shade(params, geometry):
    albedo = params[:, 0:3]
    specular = params[:, 3:6]
    roughness = params[:, 6]
    tilt_x = params[:, 7]
    tilt_y = params[:, 8]
    occlusion = params[:, 9]
    inverse_len = lax.rsqrt(1.0 + tilt_x * tilt_x + tilt_y * tilt_y)
    normal_x = tilt_x * inverse_len
    normal_y = tilt_y * inverse_len
    light_dir = geometry[:, 0:3]
    viewer = geometry[:, 3:6]
    halfway = light_dir + viewer
    halfway = halfway * lax.rsqrt(lax.optimization_barrier(jnp.sum(halfway * halfway, axis=1, keepdims=True)))

    def facing(vector):
        return normal_x * vector[:, 0] + normal_y * vector[:, 1] + inverse_len * vector[:, 2]
    cosine_light = facing(light_dir)
    cosine_view = facing(viewer)
    cosine_half = facing(halfway)
    view_half = lax.optimization_barrier(jnp.sum(viewer * halfway, axis=1))
    rough_square = roughness * roughness
    rough_fourth = rough_square * rough_square
    denominator = cosine_half * cosine_half * (rough_fourth - 1.0) + 1.0
    distribution = rough_fourth / (math.pi * denominator * denominator)
    smith_k = 0.5 * rough_square
    masking = cosine_light / (cosine_light * (1.0 - smith_k) + smith_k)
    masking = masking * cosine_view / (cosine_view * (1.0 - smith_k) + smith_k)
    fresnel = specular + (1.0 - specular) * ((1.0 - view_half) ** 5)[:, None]
    reflected = (distribution * masking / (4.0 * cosine_light * cosine_view))[:, None] * fresnel
    return (occlusion * cosine_light)[:, None] * (albedo + math.pi * reflected)

def footprint(block_ids, pixel_slot, corner):
    slot_table = block_ids.reshape(NTILE, OWNERS * SLOTS)
    within = jnp.take_along_axis(slot_table, pixel_slot, axis=1)
    block_number = pixel_slot // SLOTS * RANGE + within
    return (block_number * BT + corner // (BSIDE - 1) * BSIDE + corner % (BSIDE - 1)).astype(jnp.int32)

def corner_weights(bilinear_frac):
    across = bilinear_frac[:, 0]
    frac_down = bilinear_frac[:, 1]
    return ((1.0 - across) * (1.0 - frac_down), across * (1.0 - frac_down), (1.0 - across) * frac_down, across * frac_down)

def sample(field, anchor, weights):
    flattened = jnp.transpose(field, (1, 0, 2)).reshape(C, NBLK * BT)
    offsets = (0, 1, BSIDE, BSIDE + 1)
    summed = jnp.zeros((C, NTILE, P_SIZE), jnp.float32)
    for offset, weight in zip(offsets, weights):
        summed = summed + weight[None] * flattened[:, anchor + offset]
    return jnp.transpose(summed, (1, 0, 2))

def spread(cotangent, anchor, weights):
    turned = jnp.transpose(cotangent, (1, 0, 2))
    flattened = jnp.zeros((C, NBLK * BT), jnp.float32)
    offsets = (0, 1, BSIDE, BSIDE + 1)
    for offset, weight in zip(offsets, weights):
        flattened = flattened.at[:, anchor + offset].add(weight[None] * turned)
    return jnp.transpose(flattened.reshape(C, NBLK, BT), (1, 0, 2))

def reference(texel_atlas, observed, geometry, block_ids, pixel_slot, corner, bilinear_frac):
    anchor = footprint(block_ids, pixel_slot, corner)
    weights = corner_weights(bilinear_frac)
    base_params = sample(texel_atlas, anchor, weights)

    def render(params):
        return shade(params, geometry)
    colors, backward = jax.vjp(render, base_params)

    def pullback(cotangent):
        return backward(cotangent)[0]
    unused, pushed = jax.vjp(pullback, jnp.zeros_like(colors))

    def forward(tangent):
        return pushed(tangent)[0]
    gradient = spread(backward(colors - observed)[0], anchor, weights)

    def operator(vector):
        pixels = sample(vector, anchor, weights)
        return spread(backward(forward(pixels))[0], anchor, weights) + DAMPING * vector
    update = jnp.zeros_like(gradient)
    residual = -gradient
    direction = residual
    norm_now = jnp.sum(residual * residual)
    for iteration in range(ITERS):
        applied = operator(direction)
        step_size = norm_now / jnp.sum(direction * applied)
        update = update + step_size * direction
        residual = residual - step_size * applied
        norm_next = jnp.sum(residual * residual)
        direction = residual + norm_next / norm_now * direction
        norm_now = norm_next
    return (update, residual)
```

```python
import functools
import math

import jax
import jax.numpy as jnp
from jax import lax
from jax.experimental import pallas as pl
from jax.experimental.pallas import tpu as pltpu
from jax.sharding import PartitionSpec as P

BSIDE = 64
ITERS = 2


DAMPING = 0.1


def shade(params, geometry):
    albedo = params[:, 0:3]
    specular = params[:, 3:6]
    roughness = params[:, 6]
    tilt_x = params[:, 7]
    tilt_y = params[:, 8]
    occlusion = params[:, 9]
    inverse_len = lax.rsqrt(1.0 + tilt_x * tilt_x + tilt_y * tilt_y)
    normal_x = tilt_x * inverse_len
    normal_y = tilt_y * inverse_len
    light_dir = geometry[:, 0:3]
    viewer = geometry[:, 3:6]
    halfway = light_dir + viewer
    halfway = halfway * lax.rsqrt(jnp.sum(halfway * halfway, axis=1, keepdims=True))

    def facing(vector):
        return normal_x * vector[:, 0] + normal_y * vector[:, 1] + inverse_len * vector[:, 2]

    cosine_light = facing(light_dir)
    cosine_view = facing(viewer)
    cosine_half = facing(halfway)
    view_half = jnp.sum(viewer * halfway, axis=1)
    rough_square = roughness * roughness
    rough_fourth = rough_square * rough_square
    denominator = cosine_half * cosine_half * (rough_fourth - 1.0) + 1.0
    distribution = rough_fourth / (math.pi * denominator * denominator)
    smith_k = 0.5 * rough_square
    masking = cosine_light / (cosine_light * (1.0 - smith_k) + smith_k)
    masking = masking * cosine_view / (cosine_view * (1.0 - smith_k) + smith_k)
    fresnel = specular + (1.0 - specular) * ((1.0 - view_half) ** 5)[:, None]
    reflected = (distribution * masking / (4.0 * cosine_light * cosine_view))[:, None] * fresnel
    return (occlusion * cosine_light)[:, None] * (albedo + math.pi * reflected)


def tables(slot_part, corner_part, frac_part, owner_index, slots):
    in_range = slot_part // slots == owner_index
    slot_within = slot_part % slots
    row_start = corner_part // (BSIDE - 1)
    column_start = corner_part % (BSIDE - 1)
    across = frac_part[:, 0]
    frac_down = frac_part[:, 1]
    positions = jnp.arange(BSIDE, dtype=jnp.int32)[None, :, None]
    column_weight = jnp.where(positions == column_start[:, None], (1.0 - across)[:, None], 0.0)
    column_weight = column_weight + jnp.where(
        positions == column_start[:, None] + 1, across[:, None], 0.0
    )
    row_part = jnp.where(positions == row_start[:, None], (1.0 - frac_down)[:, None], 0.0)
    row_part = row_part + jnp.where(positions == row_start[:, None] + 1, frac_down[:, None], 0.0)
    picked = (jnp.arange(slots, dtype=jnp.int32)[None, :, None] == slot_within[:, None]) & in_range[
        :, None
    ]
    row_weight = jnp.where(picked[:, :, None], row_part[:, None], 0.0)
    return (row_weight, column_weight)


def general_step(texel_atlas, observed, geometry, block_ids, pixel_slot, corner, bilinear_frac):
    tex_count = lax.axis_size("tex")
    owner_index = lax.axis_index("tex")
    own_blocks, channels, texels = texel_atlas.shape
    tiles_all = observed.shape[0]
    tiles_own = tiles_all // tex_count
    slots = block_ids.shape[2]
    groups = tiles_all // tex_count
    slot_blocks = block_ids[:, 0, :]
    slot_list = slot_blocks.reshape(-1)
    exact_mode = lax.Precision.HIGHEST

    def grouped(source):
        return source.reshape((groups, tex_count) + source.shape[1:])

    pixel_tables = (grouped(pixel_slot), grouped(corner), grouped(bilinear_frac))

    def widen(own_shard):
        return lax.all_gather(own_shard, "view", axis=0, tiled=True)

    def pixels_of(whole_range):
        ranged = whole_range.shape[0]
        named = jnp.arange(ranged, dtype=jnp.int32)
        chooser = (jnp.clip(slot_list, 0, ranged - 1)[:, None] == named[None, :]).astype(jnp.float32)
        fetched = jnp.dot(chooser, whole_range.reshape(ranged, -1), precision=exact_mode)
        fetched = fetched.reshape(tiles_all, slots, channels, texels)

        def pixels_one_group(members):
            blocks, slot_part, corner_part, frac_part = members
            row_weight, column_weight = tables(
                slot_part, corner_part, frac_part, owner_index, slots
            )
            values = blocks.reshape(blocks.shape[0], slots, channels, BSIDE, BSIDE)
            middle = jnp.einsum("tjcyx,tjyp->tcxp", values, row_weight, precision=exact_mode)
            return jnp.sum(middle * column_weight[:, None], axis=2)

        partial_value = lax.map(pixels_one_group, (grouped(fetched),) + pixel_tables)
        partial_value = partial_value.reshape((tiles_all,) + partial_value.shape[2:])
        return lax.psum_scatter(partial_value, "tex", scatter_dimension=0, tiled=True)

    def texel_terms(cotangent):
        gathered = lax.all_gather(cotangent, "tex", axis=0, tiled=True)

        def texel_one_group(members):
            back_part, slot_part, corner_part, frac_part = members
            row_weight, column_weight = tables(
                slot_part, corner_part, frac_part, owner_index, slots
            )
            middle = back_part[:, :, None, :] * column_weight[:, None]
            values = jnp.einsum("tcxp,tjyp->tjcyx", middle, row_weight, precision=exact_mode)
            return values.reshape(values.shape[0] * slots, channels * texels)

        terms = lax.map(texel_one_group, (grouped(gathered),) + pixel_tables)
        return terms.reshape(tiles_all * slots, channels * texels)

    def owner_sums(terms):
        row_count = lax.axis_size("view") * own_blocks
        wanted = jnp.arange(row_count, dtype=jnp.int32)
        selector = (slot_list[None, :] == wanted[:, None]).astype(jnp.float32)
        summed = jnp.dot(selector, terms, precision=exact_mode, preferred_element_type=jnp.float32)
        return lax.psum_scatter(
            summed.reshape(row_count, channels, texels), "view", scatter_dimension=0, tiled=True
        )

    atlas_range = widen(texel_atlas)
    base_params = pixels_of(atlas_range)
    geometry_own = lax.dynamic_slice_in_dim(geometry, owner_index * tiles_own, tiles_own, 0)
    observed_own = lax.dynamic_slice_in_dim(observed, owner_index * tiles_own, tiles_own, 0)

    def render(params):
        return shade(params, geometry_own)

    colors, backward = jax.vjp(render, base_params)

    def pullback(cotangent):
        return backward(cotangent)[0]

    unused, pushed = jax.vjp(pullback, jnp.zeros_like(colors))
    first_terms = texel_terms(backward(colors - observed_own)[0])
    gradient = owner_sums(first_terms)

    def inner_sums(values):
        return lax.psum((values[0],), ("tex", "view"))

    update = jnp.zeros_like(gradient)
    residual = -gradient
    direction = residual
    norm_now = inner_sums((jnp.sum(residual * residual),))[0]
    for iteration in range(ITERS):
        applied = (
            owner_sums(texel_terms(backward(pushed(pixels_of(widen(direction)))[0])[0]))
            + DAMPING * direction
        )
        step_size = norm_now / inner_sums((jnp.sum(direction * applied),))[0]
        update = update + step_size * direction
        residual = residual - step_size * applied
        norm_next = inner_sums((jnp.sum(residual * residual),))[0]
        direction = residual + norm_next / norm_now * direction
        norm_now = norm_next
    return (update, residual)


MESH = pl.DeviceIdType.MESH
F32 = jnp.float32
BF16 = jnp.bfloat16
CHANNELS = 10
ROWS = 16
WINDOW = 384
PICKED = 256
SORTED = 1024
CHUNK = 256
NT = (((1,), (1,)), ((), ()))


def halves(values):
    high = values.astype(BF16)
    low = (values - high.astype(F32)).astype(BF16)
    return high, low


def iota(shape, axis):
    return lax.broadcasted_iota(jnp.int32, shape, axis)


def pack_kernel(ids, obs, geo, frac, slot, corner, out, spilled, picked, ordered):
    tiles, pixels = slot.shape
    slots = ids.shape[0]
    blocks = out.shape[0]
    owner = lax.axis_index("tex")
    lanes = pixels // 128

    slot_now = slot[...]
    corner_now = corner[...]
    row = corner_now // (BSIDE - 1)
    column = (corner_now - row * (BSIDE - 1)).astype(F32)
    row = row.astype(F32)
    tile_of = iota((tiles, 128), 0)
    target = jnp.zeros((tiles, pixels), jnp.int32)
    for s in range(slots):
        named = jnp.zeros((tiles, 128), jnp.int32)
        for t in range(tiles):
            named = jnp.where(tile_of == t, ids[s, t] + 1, named)
        target = jnp.where(
            slot_now == owner * slots + s, jnp.concatenate([named] * lanes, axis=1), target
        )
    mine = jnp.where(target > 0, 1.0, 0.0)
    before = jnp.where(iota((128, 128), 0) < iota((128, 128), 1), 1.0, 0.0).astype(BF16)

    stacked = jnp.concatenate([mine[:, c * 128 : c * 128 + 128] for c in range(lanes)], axis=0)
    ahead = jnp.dot(stacked.astype(BF16), before, preferred_element_type=F32)
    base = jnp.zeros((tiles, 1), F32)
    places = []
    for c in range(lanes):
        places.append(ahead[c * tiles : c * tiles + tiles] + base)
        base = base + jnp.sum(mine[:, c * 128 : c * 128 + 128], axis=1, keepdims=True)
    place = jnp.where(target > 0, jnp.concatenate(places, axis=1), -1.0).astype(jnp.int32)
    over = jnp.max(jnp.where(base > PICKED, 1.0, 0.0))
    total = jnp.sum(base)
    over = jnp.maximum(over, jnp.where(total > SORTED, 1.0, 0.0))

    target_f = target.astype(F32)
    wanted = iota((PICKED, pixels), 0)
    for t in range(tiles):
        numbers = jnp.concatenate(
            [
                obs[:, t, :],
                geo[:, t, :],
                frac[t],
                row[t : t + 1],
                column[t : t + 1],
                target_f[t : t + 1],
                jnp.zeros((2, pixels), F32),
            ],
            axis=0,
        )
        both = jnp.concatenate(halves(numbers), axis=0)
        hot = jnp.where(wanted == place[t : t + 1], 1.0, 0.0).astype(BF16)
        got = lax.dot_general(both, hot, NT, preferred_element_type=F32)
        picked[:, t * PICKED : t * PICKED + PICKED] = got[:ROWS] + got[ROWS:]

    listed = tiles * PICKED
    groups = listed // 128
    target_row = picked[13:14, :]
    member = jnp.where(
        iota((blocks, listed), 0).astype(F32) + 1.0 == target_row, 1.0, 0.0
    )
    stacked = jnp.concatenate([member[:, c * 128 : c * 128 + 128] for c in range(groups)], axis=0)
    ahead = jnp.dot(stacked.astype(BF16), before, preferred_element_type=F32)
    base = jnp.zeros((blocks, 1), F32)
    places = []
    for c in range(groups):
        places.append(ahead[c * blocks : c * blocks + blocks] + base)
        base = base + jnp.sum(member[:, c * 128 : c * 128 + 128], axis=1, keepdims=True)
    over = jnp.maximum(over, jnp.max(jnp.where(base > WINDOW, 1.0, 0.0)))
    earlier = jnp.where(iota((blocks, blocks), 1) < iota((blocks, blocks), 0), 1.0, 0.0)
    first = jnp.dot(
        earlier,
        jnp.broadcast_to(base, (blocks, 128)),
        precision=lax.Precision.HIGHEST,
        preferred_element_type=F32,
    )
    place = jnp.concatenate(places, axis=1) + first[:, 0:1]
    place = jnp.sum(member * place, axis=0, keepdims=True)
    place = jnp.where(target_row > 0.0, place, -1.0).astype(jnp.int32)
    both = jnp.concatenate(halves(picked[...]), axis=0)
    ordered[:, SORTED:] = jnp.zeros((ROWS, ordered.shape[1] - SORTED), F32)
    for q in range(SORTED // 256):
        hot = jnp.where(iota((256, listed), 0) + q * 256 == place, 1.0, 0.0).astype(BF16)
        got = lax.dot_general(both, hot, NT, preferred_element_type=F32)
        ordered[:, q * 256 : q * 256 + 256] = got[:ROWS] + got[ROWS:]

    first = jnp.minimum(first, float(SORTED)).astype(jnp.int32)
    wide = WINDOW + 128
    for k in range(blocks):
        begin = first[k, 0]
        aligned = pl.multiple_of(begin // 128 * 128, 128)
        window = ordered[:, pl.ds(aligned, wide)]
        shift = begin - aligned
        window = pltpu.roll(window, lax.rem(wide - shift, wide), axis=1)
        out[k] = window[:, :WINDOW]
    spilled[...] = jnp.full(spilled.shape, over, F32)


def exchange_kernel(windows, landed, own_sem, send_sem, recv_sem):
    tex = lax.axis_index("tex")
    view = lax.axis_index("view")
    views = windows.shape[0]
    barrier = pltpu.get_barrier_semaphore()
    for step in range(1, views):
        peer = lax.rem(view + step, views)
        pl.semaphore_signal(barrier, inc=1, device_id=(tex, peer), device_id_type=MESH)
    own = pltpu.make_async_copy(windows.at[view], landed.at[view], own_sem)
    own.start()
    pl.semaphore_wait(barrier, views - 1)
    copies = []
    for step in range(1, views):
        peer = lax.rem(view + step, views)
        copy = pltpu.make_async_remote_copy(
            src_ref=windows.at[peer],
            dst_ref=landed.at[view],
            send_sem=send_sem.at[step],
            recv_sem=recv_sem.at[step],
            device_id=(tex, peer),
            device_id_type=MESH,
        )
        copy.start()
        copies.append(copy)
    own.wait()
    for copy in copies:
        copy.wait()


def optics(params, geometry):
    roughness, tilt_x, tilt_y, occlusion = params[6], params[7], params[8], params[9]
    light, viewer = geometry[0:3], geometry[3:6]
    inverse_len = lax.rsqrt(1.0 + tilt_x * tilt_x + tilt_y * tilt_y)
    normal_x = tilt_x * inverse_len
    normal_y = tilt_y * inverse_len
    half = [a + b for a, b in zip(light, viewer)]
    scale = lax.rsqrt(half[0] * half[0] + half[1] * half[1] + half[2] * half[2])
    half = [a * scale for a in half]

    def facing(vector):
        cosine = normal_x * vector[0] + normal_y * vector[1] + inverse_len * vector[2]
        along_x = inverse_len * (vector[0] - normal_x * cosine)
        along_y = inverse_len * (vector[1] - normal_y * cosine)
        return cosine, along_x, along_y

    light_c, light_x, light_y = facing(light)
    view_c, view_x, view_y = facing(viewer)
    half_c, half_x, half_y = facing(half)
    miss = 1.0 - (viewer[0] * half[0] + viewer[1] * half[1] + viewer[2] * half[2])
    fifth = miss * miss
    fifth = fifth * fifth * miss
    square = roughness * roughness
    fourth = square * square
    inverse_d = 1.0 / (half_c * half_c * (fourth - 1.0) + 1.0)
    smith = 0.5 * square
    inverse_l = 1.0 / (light_c * (1.0 - smith) + smith)
    inverse_v = 1.0 / (view_c * (1.0 - smith) + smith)
    shape = 0.25 * inverse_d * inverse_d * inverse_l * inverse_v
    gloss = fourth * shape
    shape_slope = -4.0 * square * half_c * half_c * inverse_d
    shape_slope = shape_slope - 0.5 * (1.0 - light_c) * inverse_l - 0.5 * (1.0 - view_c) * inverse_v
    gloss_square = 2.0 * square * shape + gloss * shape_slope
    gloss_half = -4.0 * gloss * half_c * (fourth - 1.0) * inverse_d
    gloss_light = -gloss * (1.0 - smith) * inverse_l
    gloss_view = -gloss * (1.0 - smith) * inverse_v
    gloss_x = gloss_half * half_x + gloss_light * light_x + gloss_view * view_x
    gloss_y = gloss_half * half_y + gloss_light * light_y + gloss_view * view_y
    lit = occlusion * light_c
    fresnel = [params[3 + c] + (1.0 - params[3 + c]) * fifth for c in range(3)]
    total = [params[c] + gloss * fresnel[c] for c in range(3)]
    factors = [
        lit,
        lit * gloss * (1.0 - fifth),
        lit * gloss_square * 2.0 * roughness,
        occlusion * light_x,
        lit * gloss_x,
        occlusion * light_y,
        lit * gloss_y,
        light_c,
    ]
    return factors + total + fresnel, [lit * t for t in total]


def push(tangent, factors):
    albedo, specular, rough, ex, fx, ey, fy, shine = factors[:8]
    total, fresnel = factors[8:11], factors[11:14]
    on_total = ex * tangent[7] + ey * tangent[8] + shine * tangent[9]
    on_fresnel = rough * tangent[6] + fx * tangent[7] + fy * tangent[8]
    return [
        albedo * tangent[c] + specular * tangent[3 + c] + total[c] * on_total + fresnel[c] * on_fresnel
        for c in range(3)
    ]


def pull(colors, factors):
    albedo, specular, rough, ex, fx, ey, fy, shine = factors[:8]
    total, fresnel = factors[8:11], factors[11:14]
    e = total[0] * colors[0] + total[1] * colors[1] + total[2] * colors[2]
    f = fresnel[0] * colors[0] + fresnel[1] * colors[1] + fresnel[2] * colors[2]
    return (
        [albedo * c for c in colors]
        + [specular * c for c in colors]
        + [rough * f, ex * e + fx * f, ey * e + fy * f, shine * e]
    )


def solve_kernel(
    landed, spilled, atlas, start, first, second, sums, pixels, field, across, down, slopes, gathered
):
    senders = landed.shape[0]
    me = lax.axis_index("view")
    half_rows = CHANNELS * BSIDE // 2
    lane = iota((half_rows, 128), 1)

    pixels[...] = jnp.zeros(pixels.shape, F32)
    marks = landed[:, 13, :]
    live = jnp.where(marks == (me + 1).astype(F32), 1.0, 0.0)
    counts = jnp.sum(live, axis=1, keepdims=True)
    earlier = jnp.where(iota((senders, senders), 1) < iota((senders, senders), 0), 1.0, 0.0)
    begins = jnp.dot(
        earlier,
        jnp.broadcast_to(counts, (senders, 128)),
        precision=lax.Precision.HIGHEST,
        preferred_element_type=F32,
    ).astype(jnp.int32)
    wide = WINDOW + 128
    for j in range(senders):
        begin = begins[j, 0]
        aligned = pl.multiple_of(begin // 128 * 128, 128)
        window = jnp.where(live[j : j + 1] > 0.0, landed[j], 0.0)
        window = jnp.concatenate([window, jnp.zeros((ROWS, 128), F32)], axis=1)
        window = pltpu.roll(window, begin - aligned, axis=1)
        pixels[:, pl.ds(aligned, wide)] += window
    count = jnp.sum(counts).astype(jnp.int32)
    chunks = (count + CHUNK - 1) // CHUNK

    def hold(values):
        high, low = halves(values)
        high, low = high.astype(F32), low.astype(F32)
        left = jnp.where(lane < BSIDE, high, pltpu.roll(low, BSIDE, axis=1)).astype(BF16)
        right = jnp.where(lane < BSIDE, pltpu.roll(high, BSIDE, axis=1), low).astype(BF16)
        field[:half_rows, :128] = left
        field[:half_rows, 128:] = left
        field[half_rows:, :128] = right
        field[half_rows:, 128:] = right

    def sample(c, rows):
        seen = jnp.dot(field[...], across[c], preferred_element_type=F32)
        seen = seen.reshape(2, CHANNELS, BSIDE // 2, CHUNK) * rows
        seen = jnp.sum(seen[0] + seen[1], axis=1)
        return [seen[k : k + 1] for k in range(CHANNELS)]

    def spread(c, rows, back):
        back = jnp.concatenate(back, axis=0)
        terms = (back.reshape(1, CHANNELS, 1, CHUNK) * rows).reshape(2 * half_rows, CHUNK)
        high, low = halves(terms)
        columns = across[c, BSIDE : 3 * BSIDE, :]
        gathered[...] += lax.dot_general(high, columns, NT, preferred_element_type=F32)
        gathered[...] += lax.dot_general(low, columns, NT, preferred_element_type=F32)

    def collected():
        left, right = gathered[:half_rows], gathered[half_rows:]
        left = left + pltpu.roll(left, BSIDE, axis=1)
        right = right + pltpu.roll(right, BSIDE, axis=1)
        return jnp.where(lane < BSIDE, left, right)

    hold(atlas[...])
    gathered[...] = jnp.zeros(gathered.shape, F32)

    def first_pass(c, carry):
        numbers = pixels[:, pl.ds(pl.multiple_of(c * CHUNK, CHUNK), CHUNK)]
        numbers = [numbers[k : k + 1] for k in range(ROWS)]
        used = iota((1, CHUNK), 1) + c * CHUNK < count
        frac_x, frac_y, row, column = numbers[9:13]
        at = iota((BSIDE, CHUNK), 0).astype(F32)
        weight = jnp.where(at == column, 1.0 - frac_x, jnp.where(at == column + 1.0, frac_x, 0.0))
        high, low = halves(weight)
        across[c] = jnp.concatenate([high, high, low, low], axis=0)
        at = iota((BSIDE, CHUNK), 0)
        at = jnp.where(at < BSIDE // 2, 2 * at, 2 * at - (BSIDE - 1)).astype(F32)
        weight = jnp.where(at == row, 1.0 - frac_y, jnp.where(at == row + 1.0, frac_y, 0.0))
        weight = jnp.where(used, weight, 0.0)
        down[c] = weight
        rows = weight.reshape(2, 1, BSIDE // 2, CHUNK)
        factors, colors = optics(sample(c, rows), numbers[3:9])
        factors = [jnp.where(used, factor, 0.0) for factor in factors]
        slopes[c] = jnp.concatenate(factors + [jnp.zeros((2, CHUNK), F32)], axis=0)
        errors = [jnp.where(used, a - b, 0.0) for a, b in zip(colors, numbers[0:3])]
        spread(c, rows, pull(errors, factors))
        return carry

    lax.fori_loop(0, chunks, first_pass, 0)
    start_now = -collected()
    start[...] = start_now

    def applied(values):
        hold(values)
        gathered[...] = jnp.zeros(gathered.shape, F32)

        def one_pass(c, carry):
            rows = down[c].reshape(2, 1, BSIDE // 2, CHUNK)
            factors = slopes[c]
            factors = [factors[k : k + 1] for k in range(14)]
            spread(c, rows, pull(push(sample(c, rows), factors), factors))
            return carry

        lax.fori_loop(0, chunks, one_pass, 0)
        return collected() + DAMPING * values

    first_now = applied(start_now)
    first[...] = first_now
    second_now = applied(first_now)
    second[...] = second_now

    start_start = jnp.sum(start_now * start_now)
    start_first = jnp.sum(start_now * first_now)
    guess = jnp.where(start_first > 0.0, start_start / jnp.where(start_first > 0.0, start_first, 1.0), 0.0)
    rest = start_now - guess * first_now
    image = first_now - guess * second_now
    found = [
        start_start,
        start_first,
        jnp.sum(rest * rest),
        jnp.sum(rest * first_now),
        jnp.sum(first_now * first_now),
        jnp.sum(rest * image),
        jnp.sum(image * first_now),
        jnp.sum(first_now * second_now),
        guess,
    ]
    place = iota((1, 128), 1)
    line = jnp.where(place == len(found), spilled[...], 0.0)
    for k, value in enumerate(found):
        line = jnp.where(place == k, value, line)
    sums[...] = line


def steps_kernel(sums, steps, near, far, send_near, recv_near, send_far, recv_far):
    tex = lax.axis_index("tex")
    view = lax.axis_index("view")
    owners, views = near.shape[0], far.shape[0]
    barrier = pltpu.get_barrier_semaphore()
    for step in range(1, owners):
        peer = lax.rem(tex + step, owners)
        pl.semaphore_signal(barrier, inc=1, device_id=(peer, view), device_id_type=MESH)
    for step in range(1, views):
        peer = lax.rem(view + step, views)
        pl.semaphore_signal(barrier, inc=1, device_id=(tex, peer), device_id_type=MESH)
    near[tex] = sums[...]
    pl.semaphore_wait(barrier, owners + views - 2)
    copies = []
    for step in range(1, owners):
        peer = lax.rem(tex + step, owners)
        copy = pltpu.make_async_remote_copy(
            src_ref=sums,
            dst_ref=near.at[tex],
            send_sem=send_near.at[step],
            recv_sem=recv_near.at[step],
            device_id=(peer, view),
            device_id_type=MESH,
        )
        copy.start()
        copies.append(copy)
    for copy in copies:
        copy.wait()
    far[view] = near[...]
    copies = []
    for step in range(1, views):
        peer = lax.rem(view + step, views)
        copy = pltpu.make_async_remote_copy(
            src_ref=near,
            dst_ref=far.at[view],
            send_sem=send_far.at[step],
            recv_sem=recv_far.at[step],
            device_id=(tex, peer),
            device_id_type=MESH,
        )
        copy.start()
        copies.append(copy)
    for copy in copies:
        copy.wait()
    table = far[...].reshape(owners * views, 128)
    column = [table[:, k : k + 1] for k in range(10)]

    def added(values):
        return jnp.sum(values, axis=0, keepdims=True)

    start_start, start_first = added(column[0]), added(column[1])
    one = start_start / start_first
    change = column[8] - one
    norm = added(column[2] + change * (2.0 * column[3] + change * column[4]))
    turn = norm / start_start
    cross = added(column[3] + change * column[4])
    curve = added(column[5] + change * (2.0 * column[6] + change * column[7]))
    curve = curve + 2.0 * turn * cross + turn * turn * start_first
    two = norm / curve
    place = iota((1, 128), 1)
    line = jnp.where(place == 0, one + two * (1.0 + turn), 0.0)
    line = jnp.where(place == 1, one * two, line)
    steps[...] = jnp.where(place == 2, added(column[9]), line)


def in_vmem(count):
    return [pl.BlockSpec(memory_space=pltpu.VMEM)] * count


def per_device(texel_atlas, observed, geometry, block_ids, pixel_slot, corner, bilinear_frac):
    owners, views = lax.axis_size("tex"), lax.axis_size("view")
    tiles, slots = block_ids.shape[0], block_ids.shape[2]
    half_rows = CHANNELS * BSIDE // 2
    shaped = jax.ShapeDtypeStruct

    windows, spilled = pl.pallas_call(
        pack_kernel,
        out_shape=(shaped((views, ROWS, WINDOW), F32), shaped((1, 128), F32)),
        in_specs=[pl.BlockSpec(memory_space=pltpu.SMEM)] + in_vmem(5),
        out_specs=tuple(in_vmem(2)),
        scratch_shapes=[
            pltpu.VMEM((ROWS, tiles * PICKED), F32),
            pltpu.VMEM((ROWS, SORTED + WINDOW + 128), F32),
        ],
        compiler_params=pltpu.CompilerParams(vmem_limit_bytes=32 << 20),
    )(
        block_ids.reshape(tiles, slots).T,
        observed.transpose(1, 0, 2),
        geometry.transpose(1, 0, 2),
        bilinear_frac,
        pixel_slot,
        corner,
    )
    landed = pl.pallas_call(
        exchange_kernel,
        out_shape=shaped((views, ROWS, WINDOW), F32),
        in_specs=in_vmem(1),
        out_specs=in_vmem(1)[0],
        scratch_shapes=[
            pltpu.SemaphoreType.DMA,
            pltpu.SemaphoreType.DMA((views,)),
            pltpu.SemaphoreType.DMA((views,)),
        ],
        compiler_params=pltpu.CompilerParams(collective_id=0, has_side_effects=True),
    )(windows)
    most = views * WINDOW
    start, first, second, sums = pl.pallas_call(
        solve_kernel,
        out_shape=(shaped((half_rows, 128), F32),) * 3 + (shaped((1, 128), F32),),
        in_specs=in_vmem(3),
        out_specs=tuple(in_vmem(4)),
        scratch_shapes=[
            pltpu.VMEM((ROWS, most + WINDOW + 128), F32),
            pltpu.VMEM((2 * half_rows, 256), BF16),
            pltpu.VMEM((most // CHUNK, 4 * BSIDE, CHUNK), BF16),
            pltpu.VMEM((most // CHUNK, BSIDE, CHUNK), F32),
            pltpu.VMEM((most // CHUNK, ROWS, CHUNK), F32),
            pltpu.VMEM((2 * half_rows, 128), F32),
        ],
        compiler_params=pltpu.CompilerParams(vmem_limit_bytes=40 << 20),
    )(landed, spilled, texel_atlas.reshape(half_rows, 128))
    steps = pl.pallas_call(
        steps_kernel,
        out_shape=shaped((1, 128), F32),
        in_specs=in_vmem(1),
        out_specs=in_vmem(1)[0],
        scratch_shapes=[
            pltpu.VMEM((owners, 1, 128), F32),
            pltpu.VMEM((views, owners, 1, 128), F32),
            pltpu.SemaphoreType.DMA((owners,)),
            pltpu.SemaphoreType.DMA((owners,)),
            pltpu.SemaphoreType.DMA((views,)),
            pltpu.SemaphoreType.DMA((views,)),
        ],
        compiler_params=pltpu.CompilerParams(collective_id=1, has_side_effects=True),
    )(sums)

    def quick():
        update = steps[0, 0] * start - steps[0, 1] * first
        residual = start - steps[0, 0] * first + steps[0, 1] * second
        return update.reshape(texel_atlas.shape), residual.reshape(texel_atlas.shape)

    def general():
        return general_step(
            texel_atlas, observed, geometry, block_ids, pixel_slot, corner, bilinear_frac
        )

    return lax.cond(steps[0, 2] > 0.0, general, quick)


def solution(mesh):
    in_specs = (
        P(("tex", "view"), None, None),
        P("view", None, None),
        P("view", None, None),
        P("view", "tex", None),
        P("view", None),
        P("view", None),
        P("view", None, None),
    )
    out_specs = (P(("tex", "view"), None, None), P(("tex", "view"), None, None))
    return jax.shard_map(
        per_device, mesh=mesh, in_specs=in_specs, out_specs=out_specs, check_vma=False
    )
```

```python
import functools
import math

import jax
import jax.numpy as jnp
from jax import lax
from jax.experimental import pallas as pl
from jax.experimental.pallas import tpu as pltpu
from jax.sharding import PartitionSpec as P

BSIDE = 64
ITERS = 2


DAMPING = 0.1


def passed_on(values, axis):
    count = lax.axis_size(axis)
    return lax.ppermute(values, axis, [(k, (k + 1) % count) for k in range(count)])


def ring_gather(values, axis):
    count, me = lax.axis_size(axis), lax.axis_index(axis)

    def step(s, state):
        held, block = state
        block = passed_on(block, axis)
        return held.at[lax.rem(me - s + count, count)].set(block), block

    held = jnp.zeros((count,) + values.shape, values.dtype).at[me].set(values)
    return lax.fori_loop(1, count, step, (held, values))[0]


def ring_sum_scatter(values, axis):
    count, me = lax.axis_size(axis), lax.axis_index(axis)

    def step(s, total):
        return passed_on(total, axis) + values[lax.rem(me - 1 - s + 2 * count, count)]

    return lax.fori_loop(1, count, step, values[lax.rem(me - 1 + count, count)])


def grouped_by(values, count):
    return values.reshape((count, values.shape[0] // count) + values.shape[1:])


def shade(params, geometry):
    albedo = params[:, 0:3]
    specular = params[:, 3:6]
    roughness = params[:, 6]
    tilt_x = params[:, 7]
    tilt_y = params[:, 8]
    occlusion = params[:, 9]
    inverse_len = lax.rsqrt(1.0 + tilt_x * tilt_x + tilt_y * tilt_y)
    normal_x = tilt_x * inverse_len
    normal_y = tilt_y * inverse_len
    light_dir = geometry[:, 0:3]
    viewer = geometry[:, 3:6]
    halfway = light_dir + viewer
    halfway = halfway * lax.rsqrt(jnp.sum(halfway * halfway, axis=1, keepdims=True))

    def facing(vector):
        return normal_x * vector[:, 0] + normal_y * vector[:, 1] + inverse_len * vector[:, 2]

    cosine_light = facing(light_dir)
    cosine_view = facing(viewer)
    cosine_half = facing(halfway)
    view_half = jnp.sum(viewer * halfway, axis=1)
    rough_square = roughness * roughness
    rough_fourth = rough_square * rough_square
    denominator = cosine_half * cosine_half * (rough_fourth - 1.0) + 1.0
    distribution = rough_fourth / (math.pi * denominator * denominator)
    smith_k = 0.5 * rough_square
    masking = cosine_light / (cosine_light * (1.0 - smith_k) + smith_k)
    masking = masking * cosine_view / (cosine_view * (1.0 - smith_k) + smith_k)
    fresnel = specular + (1.0 - specular) * ((1.0 - view_half) ** 5)[:, None]
    reflected = (distribution * masking / (4.0 * cosine_light * cosine_view))[:, None] * fresnel
    return (occlusion * cosine_light)[:, None] * (albedo + math.pi * reflected)


def tables(slot_part, corner_part, frac_part, owner_index, slots):
    in_range = slot_part // slots == owner_index
    slot_within = slot_part % slots
    row_start = corner_part // (BSIDE - 1)
    column_start = corner_part % (BSIDE - 1)
    across = frac_part[:, 0]
    frac_down = frac_part[:, 1]
    positions = jnp.arange(BSIDE, dtype=jnp.int32)[None, :, None]
    column_weight = jnp.where(positions == column_start[:, None], (1.0 - across)[:, None], 0.0)
    column_weight = column_weight + jnp.where(
        positions == column_start[:, None] + 1, across[:, None], 0.0
    )
    row_part = jnp.where(positions == row_start[:, None], (1.0 - frac_down)[:, None], 0.0)
    row_part = row_part + jnp.where(positions == row_start[:, None] + 1, frac_down[:, None], 0.0)
    picked = (jnp.arange(slots, dtype=jnp.int32)[None, :, None] == slot_within[:, None]) & in_range[
        :, None
    ]
    row_weight = jnp.where(picked[:, :, None], row_part[:, None], 0.0)
    return (row_weight, column_weight)


def general_step(texel_atlas, observed, geometry, block_ids, pixel_slot, corner, bilinear_frac):
    tex_count = lax.axis_size("tex")
    owner_index = lax.axis_index("tex")
    own_blocks, channels, texels = texel_atlas.shape
    tiles_all = observed.shape[0]
    tiles_own = tiles_all // tex_count
    slots = block_ids.shape[2]
    groups = tiles_all // tex_count
    slot_blocks = block_ids[:, 0, :]
    slot_list = slot_blocks.reshape(-1)
    exact_mode = lax.Precision.HIGHEST

    def grouped(source):
        return source.reshape((groups, tex_count) + source.shape[1:])

    pixel_tables = (grouped(pixel_slot), grouped(corner), grouped(bilinear_frac))

    def widen(own_shard):
        return ring_gather(own_shard, "view").reshape((-1,) + own_shard.shape[1:])

    def pixels_of(whole_range):
        ranged = whole_range.shape[0]
        named = jnp.arange(ranged, dtype=jnp.int32)
        chooser = (jnp.clip(slot_list, 0, ranged - 1)[:, None] == named[None, :]).astype(jnp.float32)
        fetched = jnp.dot(chooser, whole_range.reshape(ranged, -1), precision=exact_mode)
        fetched = fetched.reshape(tiles_all, slots, channels, texels)

        def pixels_one_group(members):
            blocks, slot_part, corner_part, frac_part = members
            row_weight, column_weight = tables(
                slot_part, corner_part, frac_part, owner_index, slots
            )
            values = blocks.reshape(blocks.shape[0], slots, channels, BSIDE, BSIDE)
            middle = jnp.einsum("tjcyx,tjyp->tcxp", values, row_weight, precision=exact_mode)
            return jnp.sum(middle * column_weight[:, None], axis=2)

        partial_value = lax.map(pixels_one_group, (grouped(fetched),) + pixel_tables)
        partial_value = partial_value.reshape((tiles_all,) + partial_value.shape[2:])
        return ring_sum_scatter(grouped_by(partial_value, tex_count), "tex")

    def texel_terms(cotangent):
        gathered = ring_gather(cotangent, "tex").reshape((-1,) + cotangent.shape[1:])

        def texel_one_group(members):
            back_part, slot_part, corner_part, frac_part = members
            row_weight, column_weight = tables(
                slot_part, corner_part, frac_part, owner_index, slots
            )
            middle = back_part[:, :, None, :] * column_weight[:, None]
            values = jnp.einsum("tcxp,tjyp->tjcyx", middle, row_weight, precision=exact_mode)
            return values.reshape(values.shape[0] * slots, channels * texels)

        terms = lax.map(texel_one_group, (grouped(gathered),) + pixel_tables)
        return terms.reshape(tiles_all * slots, channels * texels)

    def owner_sums(terms):
        row_count = lax.axis_size("view") * own_blocks
        wanted = jnp.arange(row_count, dtype=jnp.int32)
        selector = (slot_list[None, :] == wanted[:, None]).astype(jnp.float32)
        summed = jnp.dot(selector, terms, precision=exact_mode, preferred_element_type=jnp.float32)
        return ring_sum_scatter(
            summed.reshape(row_count // own_blocks, own_blocks, channels, texels), "view"
        )

    atlas_range = widen(texel_atlas)
    base_params = pixels_of(atlas_range)
    geometry_own = lax.dynamic_slice_in_dim(geometry, owner_index * tiles_own, tiles_own, 0)
    observed_own = lax.dynamic_slice_in_dim(observed, owner_index * tiles_own, tiles_own, 0)

    def render(params):
        return shade(params, geometry_own)

    colors, backward = jax.vjp(render, base_params)

    def pullback(cotangent):
        return backward(cotangent)[0]

    unused, pushed = jax.vjp(pullback, jnp.zeros_like(colors))
    first_terms = texel_terms(backward(colors - observed_own)[0])
    gradient = owner_sums(first_terms)

    def inner_sums(values):
        return (jnp.sum(ring_gather(jnp.sum(ring_gather(values[0], "tex")), "view")),)

    update = jnp.zeros_like(gradient)
    residual = -gradient
    direction = residual
    norm_now = inner_sums((jnp.sum(residual * residual),))[0]
    for iteration in range(ITERS):
        applied = (
            owner_sums(texel_terms(backward(pushed(pixels_of(widen(direction)))[0])[0]))
            + DAMPING * direction
        )
        step_size = norm_now / inner_sums((jnp.sum(direction * applied),))[0]
        update = update + step_size * direction
        residual = residual - step_size * applied
        norm_next = inner_sums((jnp.sum(residual * residual),))[0]
        direction = residual + norm_next / norm_now * direction
        norm_now = norm_next
    return (update, residual)


MESH = pl.DeviceIdType.MESH
F32 = jnp.float32
BF16 = jnp.bfloat16
CHANNELS = 10
ROWS = 16
WINDOW = 384
PICKED = 256
SORTED = 1024
CHUNK = 256
DENSE = 1792
NT = (((1,), (1,)), ((), ()))


def halves(values):
    high = values.astype(BF16)
    low = (values - high.astype(F32)).astype(BF16)
    return high, low


def iota(shape, axis):
    return lax.broadcasted_iota(jnp.int32, shape, axis)


def pack(ids, obs, geo, frac, slot, corner, out, picked, ordered):
    tiles, pixels = slot.shape
    slots = ids.shape[0]
    blocks = out.shape[0]
    owner = lax.axis_index("tex")
    lanes = pixels // 128

    slot_now = slot[...]
    corner_now = corner[...]
    row = corner_now // (BSIDE - 1)
    column = (corner_now - row * (BSIDE - 1)).astype(F32)
    row = row.astype(F32)
    tile_of = iota((tiles, 128), 0)
    target = jnp.zeros((tiles, pixels), jnp.int32)
    for s in range(slots):
        named = jnp.zeros((tiles, 128), jnp.int32)
        for t in range(tiles):
            named = jnp.where(tile_of == t, ids[s, t] + 1, named)
        target = jnp.where(
            slot_now == owner * slots + s, jnp.concatenate([named] * lanes, axis=1), target
        )
    mine = jnp.where(target > 0, 1.0, 0.0)
    before = jnp.where(iota((128, 128), 0) < iota((128, 128), 1), 1.0, 0.0).astype(BF16)

    stacked = jnp.concatenate([mine[:, c * 128 : c * 128 + 128] for c in range(lanes)], axis=0)
    ahead = jnp.dot(stacked.astype(BF16), before, preferred_element_type=F32)
    base = jnp.zeros((tiles, 1), F32)
    places = []
    for c in range(lanes):
        places.append(ahead[c * tiles : c * tiles + tiles] + base)
        base = base + jnp.sum(mine[:, c * 128 : c * 128 + 128], axis=1, keepdims=True)
    place = jnp.where(target > 0, jnp.concatenate(places, axis=1), -1.0).astype(jnp.int32)
    over = jnp.max(jnp.where(base > PICKED, 1.0, 0.0))
    total = jnp.sum(base)
    over = jnp.maximum(over, jnp.where(total > SORTED, 1.0, 0.0))

    target_f = target.astype(F32)
    wanted = iota((PICKED, pixels), 0)
    for t in range(tiles):
        numbers = jnp.concatenate(
            [
                obs[:, t, :],
                geo[:, t, :],
                frac[t],
                row[t : t + 1],
                column[t : t + 1],
                target_f[t : t + 1],
                jnp.zeros((2, pixels), F32),
            ],
            axis=0,
        )
        both = jnp.concatenate(halves(numbers), axis=0)
        hot = jnp.where(wanted == place[t : t + 1], 1.0, 0.0).astype(BF16)
        got = lax.dot_general(both, hot, NT, preferred_element_type=F32)
        picked[:, t * PICKED : t * PICKED + PICKED] = got[:ROWS] + got[ROWS:]

    listed = tiles * PICKED
    groups = listed // 128
    target_row = picked[13:14, :]
    member = jnp.where(
        iota((blocks, listed), 0).astype(F32) + 1.0 == target_row, 1.0, 0.0
    )
    stacked = jnp.concatenate([member[:, c * 128 : c * 128 + 128] for c in range(groups)], axis=0)
    ahead = jnp.dot(stacked.astype(BF16), before, preferred_element_type=F32)
    base = jnp.zeros((blocks, 1), F32)
    places = []
    for c in range(groups):
        places.append(ahead[c * blocks : c * blocks + blocks] + base)
        base = base + jnp.sum(member[:, c * 128 : c * 128 + 128], axis=1, keepdims=True)
    over = jnp.maximum(over, jnp.max(jnp.where(base > WINDOW, 1.0, 0.0)))
    earlier = jnp.where(iota((blocks, blocks), 1) < iota((blocks, blocks), 0), 1.0, 0.0)
    first = jnp.dot(
        earlier,
        jnp.broadcast_to(base, (blocks, 128)),
        precision=lax.Precision.HIGHEST,
        preferred_element_type=F32,
    )
    place = jnp.concatenate(places, axis=1) + first[:, 0:1]
    place = jnp.sum(member * place, axis=0, keepdims=True)
    place = jnp.where(target_row > 0.0, place, -1.0).astype(jnp.int32)
    both = jnp.concatenate(halves(picked[...]), axis=0)
    for q in range(SORTED // 256):
        hot = jnp.where(iota((256, listed), 0) + q * 256 == place, 1.0, 0.0).astype(BF16)
        got = lax.dot_general(both, hot, NT, preferred_element_type=F32)
        ordered[:, q * 256 : q * 256 + 256] = got[:ROWS] + got[ROWS:]

    listing = ordered[...]
    turns = jnp.where(first > 0.0, jnp.maximum(float(SORTED) - first, 0.0), 0.0).astype(jnp.int32)
    for k in range(blocks):
        out[k] = pltpu.roll(listing, turns[k, 0], axis=1)[:, :WINDOW]
    return over


def greet(barrier, tex, view, owners, views):
    for step in range(1, views):
        peer = lax.rem(view + step, views)
        pl.semaphore_signal(barrier, inc=1, device_id=(tex, peer), device_id_type=MESH)
    for step in range(1, owners):
        peer = lax.rem(tex + step, owners)
        pl.semaphore_signal(barrier, inc=1, device_id=(peer, view), device_id_type=MESH)


def send_along(axis, source, target, send_sem, recv_sem):
    tex, view = lax.axis_index("tex"), lax.axis_index("view")
    count = target.shape[0]
    me = tex if axis == "tex" else view
    copies = []
    for step in range(1, count):
        peer = lax.rem(me + step, count)
        copy = pltpu.make_async_remote_copy(
            src_ref=source(peer),
            dst_ref=target.at[me],
            send_sem=send_sem.at[step],
            recv_sem=recv_sem.at[step],
            device_id=(peer, view) if axis == "tex" else (tex, peer),
            device_id_type=MESH,
        )
        copy.start()
        copies.append(copy)
    return copies


def optics(params, geometry):
    roughness, tilt_x, tilt_y, occlusion = params[6], params[7], params[8], params[9]
    light, viewer = geometry[0:3], geometry[3:6]
    inverse_len = lax.rsqrt(1.0 + tilt_x * tilt_x + tilt_y * tilt_y)
    normal_x = tilt_x * inverse_len
    normal_y = tilt_y * inverse_len
    half = [a + b for a, b in zip(light, viewer)]
    scale = lax.rsqrt(half[0] * half[0] + half[1] * half[1] + half[2] * half[2])
    half = [a * scale for a in half]

    def facing(vector):
        cosine = normal_x * vector[0] + normal_y * vector[1] + inverse_len * vector[2]
        along_x = inverse_len * (vector[0] - normal_x * cosine)
        along_y = inverse_len * (vector[1] - normal_y * cosine)
        return cosine, along_x, along_y

    light_c, light_x, light_y = facing(light)
    view_c, view_x, view_y = facing(viewer)
    half_c, half_x, half_y = facing(half)
    miss = 1.0 - (viewer[0] * half[0] + viewer[1] * half[1] + viewer[2] * half[2])
    fifth = miss * miss
    fifth = fifth * fifth * miss
    square = roughness * roughness
    fourth = square * square
    inverse_d = 1.0 / (half_c * half_c * (fourth - 1.0) + 1.0)
    smith = 0.5 * square
    inverse_l = 1.0 / (light_c * (1.0 - smith) + smith)
    inverse_v = 1.0 / (view_c * (1.0 - smith) + smith)
    shape = 0.25 * inverse_d * inverse_d * inverse_l * inverse_v
    gloss = fourth * shape
    shape_slope = -4.0 * square * half_c * half_c * inverse_d
    shape_slope = shape_slope - 0.5 * (1.0 - light_c) * inverse_l - 0.5 * (1.0 - view_c) * inverse_v
    gloss_square = 2.0 * square * shape + gloss * shape_slope
    gloss_half = -4.0 * gloss * half_c * (fourth - 1.0) * inverse_d
    gloss_light = -gloss * (1.0 - smith) * inverse_l
    gloss_view = -gloss * (1.0 - smith) * inverse_v
    gloss_x = gloss_half * half_x + gloss_light * light_x + gloss_view * view_x
    gloss_y = gloss_half * half_y + gloss_light * light_y + gloss_view * view_y
    lit = occlusion * light_c
    fresnel = [params[3 + c] + (1.0 - params[3 + c]) * fifth for c in range(3)]
    total = [params[c] + gloss * fresnel[c] for c in range(3)]
    factors = [
        lit,
        lit * gloss * (1.0 - fifth),
        lit * gloss_square * 2.0 * roughness,
        occlusion * light_x,
        lit * gloss_x,
        occlusion * light_y,
        lit * gloss_y,
        light_c,
    ]
    return factors + total + fresnel, [lit * t for t in total]


def push(tangent, factors):
    albedo, specular, rough, ex, fx, ey, fy, shine = factors[:8]
    total, fresnel = factors[8:11], factors[11:14]
    on_total = ex * tangent[7] + ey * tangent[8] + shine * tangent[9]
    on_fresnel = rough * tangent[6] + fx * tangent[7] + fy * tangent[8]
    return [
        albedo * tangent[c] + specular * tangent[3 + c] + total[c] * on_total + fresnel[c] * on_fresnel
        for c in range(3)
    ]


def pull(colors, factors):
    albedo, specular, rough, ex, fx, ey, fy, shine = factors[:8]
    total, fresnel = factors[8:11], factors[11:14]
    e = total[0] * colors[0] + total[1] * colors[1] + total[2] * colors[2]
    f = fresnel[0] * colors[0] + fresnel[1] * colors[1] + fresnel[2] * colors[2]
    return (
        [albedo * c for c in colors]
        + [specular * c for c in colors]
        + [rough * f, ex * e + fx * f, ey * e + fy * f, shine * e]
    )


def whole_kernel(
    ids, obs, geo, frac, slot, corner, atlas, update, residual, flag,
    picked, ordered, windows, landed, pixels, field, across, down, slopes, gathered, near, far,
    send_window, recv_window, send_near, recv_near, send_far, recv_far,
):
    tex, me = lax.axis_index("tex"), lax.axis_index("view")
    senders, owners = landed.shape[0], near.shape[0]
    half_rows = CHANNELS * BSIDE // 2
    lane = iota((half_rows, 128), 1)
    barrier = pltpu.get_barrier_semaphore()
    greet(barrier, tex, me, owners, senders)
    over = pack(ids, obs, geo, frac, slot, corner, windows, picked, ordered)
    pl.semaphore_wait(barrier, owners + senders - 2)
    copies = send_along("view", lambda peer: windows.at[peer], landed, send_window, recv_window)
    landed[me] = windows[me]

    def hold(values):
        high, low = halves(values)
        high, low = high.astype(F32), low.astype(F32)
        left = jnp.where(lane < BSIDE, high, pltpu.roll(low, BSIDE, axis=1)).astype(BF16)
        right = jnp.where(lane < BSIDE, pltpu.roll(high, BSIDE, axis=1), low).astype(BF16)
        field[:half_rows, :128] = left
        field[:half_rows, 128:] = left
        field[half_rows:, :128] = right
        field[half_rows:, 128:] = right

    def sample(c, rows):
        seen = jnp.dot(field[...], across[c], preferred_element_type=F32)
        seen = seen.reshape(2, CHANNELS, BSIDE // 2, CHUNK) * rows
        seen = jnp.sum(seen[0] + seen[1], axis=1)
        return [seen[k : k + 1] for k in range(CHANNELS)]

    def spread(c, rows, back):
        back = jnp.concatenate(back, axis=0)
        terms = (back.reshape(1, CHANNELS, 1, CHUNK) * rows).reshape(2 * half_rows, CHUNK)
        high, low = halves(terms)
        columns = across[c, BSIDE : 3 * BSIDE, :]
        gathered[...] += lax.dot_general(high, columns, NT, preferred_element_type=F32)
        gathered[...] += lax.dot_general(low, columns, NT, preferred_element_type=F32)

    def collected():
        left, right = gathered[:half_rows], gathered[half_rows:]
        left = left + pltpu.roll(left, BSIDE, axis=1)
        right = right + pltpu.roll(right, BSIDE, axis=1)
        return jnp.where(lane < BSIDE, left, right)

    hold(atlas[...])
    gathered[...] = jnp.zeros(gathered.shape, F32)
    for copy in copies:
        copy.wait()
    marks = landed[:, 13, :]
    live = jnp.where(marks == (me + 1).astype(F32), 1.0, 0.0)
    counts = jnp.sum(live, axis=1, keepdims=True)
    earlier = jnp.where(iota((senders, senders), 1) < iota((senders, senders), 0), 1.0, 0.0)
    begins = jnp.dot(
        earlier,
        jnp.broadcast_to(counts, (senders, 128)),
        precision=lax.Precision.HIGHEST,
        preferred_element_type=F32,
    )
    begins = jnp.minimum(begins, float(DENSE - 1)).astype(jnp.int32)
    dense = jnp.zeros((ROWS, DENSE), F32)
    for j in range(senders):
        window = jnp.where(live[j : j + 1] > 0.0, landed[j], 0.0)
        window = jnp.concatenate([window, jnp.zeros((ROWS, DENSE - WINDOW), F32)], axis=1)
        dense = dense + pltpu.roll(window, begins[j, 0], axis=1)
    pixels[...] = dense
    count = jnp.sum(counts)
    over = jnp.maximum(over, jnp.where(count > DENSE, 1.0, 0.0))
    chunks = DENSE // CHUNK

    def first_pass(c, carry):
        numbers = pixels[:, pl.ds(pl.multiple_of(c * CHUNK, CHUNK), CHUNK)]
        numbers = [numbers[k : k + 1] for k in range(ROWS)]
        used = (iota((1, CHUNK), 1) + c * CHUNK).astype(F32) < count
        frac_x, frac_y, row, column = numbers[9:13]
        at = iota((BSIDE, CHUNK), 0).astype(F32)
        weight = jnp.where(at == column, 1.0 - frac_x, jnp.where(at == column + 1.0, frac_x, 0.0))
        high, low = halves(weight)
        across[c] = jnp.concatenate([high, high, low, low], axis=0)
        at = iota((BSIDE, CHUNK), 0)
        at = jnp.where(at < BSIDE // 2, 2 * at, 2 * at - (BSIDE - 1)).astype(F32)
        weight = jnp.where(at == row, 1.0 - frac_y, jnp.where(at == row + 1.0, frac_y, 0.0))
        weight = jnp.where(used, weight, 0.0)
        down[c] = weight
        rows = weight.reshape(2, 1, BSIDE // 2, CHUNK)
        factors, colors = optics(sample(c, rows), numbers[3:9])
        factors = [jnp.where(used, factor, 0.0) for factor in factors]
        slopes[c] = jnp.concatenate(factors + [jnp.zeros((2, CHUNK), F32)], axis=0)
        errors = [jnp.where(used, a - b, 0.0) for a, b in zip(colors, numbers[0:3])]
        spread(c, rows, pull(errors, factors))
        return carry

    lax.fori_loop(0, chunks, first_pass, 0)
    start_now = -collected()

    def applied(values):
        hold(values)
        gathered[...] = jnp.zeros(gathered.shape, F32)

        def one_pass(c, carry):
            rows = down[c].reshape(2, 1, BSIDE // 2, CHUNK)
            factors = slopes[c]
            factors = [factors[k : k + 1] for k in range(14)]
            spread(c, rows, pull(push(sample(c, rows), factors), factors))
            return carry

        lax.fori_loop(0, chunks, one_pass, 0)
        return collected() + DAMPING * values

    first_now = applied(start_now)
    second_now = applied(first_now)

    start_start = jnp.sum(start_now * start_now)
    start_first = jnp.sum(start_now * first_now)
    guess = jnp.where(start_first > 0.0, start_start / jnp.where(start_first > 0.0, start_first, 1.0), 0.0)
    rest = start_now - guess * first_now
    image = first_now - guess * second_now
    found = [
        start_start,
        start_first,
        jnp.sum(rest * rest),
        jnp.sum(rest * first_now),
        jnp.sum(first_now * first_now),
        jnp.sum(rest * image),
        jnp.sum(image * first_now),
        jnp.sum(first_now * second_now),
        guess,
    ]
    place = iota((1, 128), 1)
    line = jnp.where(place == len(found), over, 0.0)
    for k, value in enumerate(found):
        line = jnp.where(place == k, value, line)
    near[tex] = line
    for copy in send_along("tex", lambda peer: near.at[tex], near, send_near, recv_near):
        copy.wait()
    far[me] = near[...]
    for copy in send_along("view", lambda peer: near, far, send_far, recv_far):
        copy.wait()
    table = far[...].reshape(owners * senders, 128)
    column = [table[:, k : k + 1] for k in range(10)]

    def added(values):
        return jnp.sum(values, axis=0, keepdims=True)

    start_start, start_first = added(column[0]), added(column[1])
    one = start_start / start_first
    change = column[8] - one
    norm = added(column[2] + change * (2.0 * column[3] + change * column[4]))
    turn = norm / start_start
    cross = added(column[3] + change * column[4])
    curve = added(column[5] + change * (2.0 * column[6] + change * column[7]))
    curve = curve + 2.0 * turn * cross + turn * turn * start_first
    two = norm / curve
    near_part = one + two * (1.0 + turn)
    update[...] = near_part * start_now - one * two * first_now
    residual[...] = start_now - near_part * first_now + one * two * second_now
    flag[...] = jnp.broadcast_to(added(column[9]), flag.shape)


def in_vmem(count):
    return [pl.BlockSpec(memory_space=pltpu.VMEM)] * count


def per_device(texel_atlas, observed, geometry, block_ids, pixel_slot, corner, bilinear_frac):
    owners, views = lax.axis_size("tex"), lax.axis_size("view")
    tiles, slots = block_ids.shape[0], block_ids.shape[2]
    half_rows = CHANNELS * BSIDE // 2
    shaped = jax.ShapeDtypeStruct

    update, residual, flag = pl.pallas_call(
        whole_kernel,
        out_shape=(shaped((half_rows, 128), F32),) * 2 + (shaped((1, 128), F32),),
        in_specs=[pl.BlockSpec(memory_space=pltpu.SMEM)] + in_vmem(6),
        out_specs=tuple(in_vmem(3)),
        scratch_shapes=[
            pltpu.VMEM((ROWS, tiles * PICKED), F32),
            pltpu.VMEM((ROWS, SORTED), F32),
            pltpu.VMEM((views, ROWS, WINDOW), F32),
            pltpu.VMEM((views, ROWS, WINDOW), F32),
            pltpu.VMEM((ROWS, DENSE), F32),
            pltpu.VMEM((2 * half_rows, 256), BF16),
            pltpu.VMEM((DENSE // CHUNK, 4 * BSIDE, CHUNK), BF16),
            pltpu.VMEM((DENSE // CHUNK, BSIDE, CHUNK), F32),
            pltpu.VMEM((DENSE // CHUNK, ROWS, CHUNK), F32),
            pltpu.VMEM((2 * half_rows, 128), F32),
            pltpu.VMEM((owners, 1, 128), F32),
            pltpu.VMEM((views, owners, 1, 128), F32),
        ]
        + [pltpu.SemaphoreType.DMA((views,))] * 2
        + [pltpu.SemaphoreType.DMA((owners,))] * 2
        + [pltpu.SemaphoreType.DMA((views,))] * 2,
        compiler_params=pltpu.CompilerParams(
            collective_id=0, has_side_effects=True, vmem_limit_bytes=56 << 20
        ),
    )(
        block_ids.reshape(tiles, slots).T,
        observed.transpose(1, 0, 2),
        geometry.transpose(1, 0, 2),
        bilinear_frac,
        pixel_slot,
        corner,
        texel_atlas.reshape(half_rows, 128),
    )

    def quick():
        return update.reshape(texel_atlas.shape), residual.reshape(texel_atlas.shape)

    def general():
        return general_step(
            texel_atlas, observed, geometry, block_ids, pixel_slot, corner, bilinear_frac
        )

    return lax.cond(flag[0, 0] > 0.0, general, quick)


def solution(mesh):
    in_specs = (
        P(("tex", "view"), None, None),
        P("view", None, None),
        P("view", None, None),
        P("view", "tex", None),
        P("view", None),
        P("view", None),
        P("view", None, None),
    )
    out_specs = (P(("tex", "view"), None, None), P(("tex", "view"), None, None))
    return jax.shard_map(
        per_device, mesh=mesh, in_specs=in_specs, out_specs=out_specs, check_vma=False
    )
```

```python
import functools
import math

import jax
import jax.numpy as jnp
from jax import lax
from jax.experimental import pallas as pl
from jax.experimental.pallas import tpu as pltpu
from jax.sharding import PartitionSpec as P

BSIDE = 64
ITERS = 2


DAMPING = 0.1


def passed_on(values, axis):
    count = lax.axis_size(axis)
    return lax.ppermute(values, axis, [(k, (k + 1) % count) for k in range(count)])


def ring_gather(values, axis):
    count, me = lax.axis_size(axis), lax.axis_index(axis)

    def step(s, state):
        held, block = state
        block = passed_on(block, axis)
        return held.at[lax.rem(me - s + count, count)].set(block), block

    held = jnp.zeros((count,) + values.shape, values.dtype).at[me].set(values)
    return lax.fori_loop(1, count, step, (held, values))[0]


def ring_sum_scatter(values, axis):
    count, me = lax.axis_size(axis), lax.axis_index(axis)

    def step(s, total):
        return passed_on(total, axis) + values[lax.rem(me - 1 - s + 2 * count, count)]

    return lax.fori_loop(1, count, step, values[lax.rem(me - 1 + count, count)])


def grouped_by(values, count):
    return values.reshape((count, values.shape[0] // count) + values.shape[1:])


def shade(params, geometry):
    albedo = params[:, 0:3]
    specular = params[:, 3:6]
    roughness = params[:, 6]
    tilt_x = params[:, 7]
    tilt_y = params[:, 8]
    occlusion = params[:, 9]
    inverse_len = lax.rsqrt(1.0 + tilt_x * tilt_x + tilt_y * tilt_y)
    normal_x = tilt_x * inverse_len
    normal_y = tilt_y * inverse_len
    light_dir = geometry[:, 0:3]
    viewer = geometry[:, 3:6]
    halfway = light_dir + viewer
    halfway = halfway * lax.rsqrt(jnp.sum(halfway * halfway, axis=1, keepdims=True))

    def facing(vector):
        return normal_x * vector[:, 0] + normal_y * vector[:, 1] + inverse_len * vector[:, 2]

    cosine_light = facing(light_dir)
    cosine_view = facing(viewer)
    cosine_half = facing(halfway)
    view_half = jnp.sum(viewer * halfway, axis=1)
    rough_square = roughness * roughness
    rough_fourth = rough_square * rough_square
    denominator = cosine_half * cosine_half * (rough_fourth - 1.0) + 1.0
    distribution = rough_fourth / (math.pi * denominator * denominator)
    smith_k = 0.5 * rough_square
    masking = cosine_light / (cosine_light * (1.0 - smith_k) + smith_k)
    masking = masking * cosine_view / (cosine_view * (1.0 - smith_k) + smith_k)
    fresnel = specular + (1.0 - specular) * ((1.0 - view_half) ** 5)[:, None]
    reflected = (distribution * masking / (4.0 * cosine_light * cosine_view))[:, None] * fresnel
    return (occlusion * cosine_light)[:, None] * (albedo + math.pi * reflected)


def tables(slot_part, corner_part, frac_part, owner_index, slots):
    in_range = slot_part // slots == owner_index
    slot_within = slot_part % slots
    row_start = corner_part // (BSIDE - 1)
    column_start = corner_part % (BSIDE - 1)
    across = frac_part[:, 0]
    frac_down = frac_part[:, 1]
    positions = jnp.arange(BSIDE, dtype=jnp.int32)[None, :, None]
    column_weight = jnp.where(positions == column_start[:, None], (1.0 - across)[:, None], 0.0)
    column_weight = column_weight + jnp.where(
        positions == column_start[:, None] + 1, across[:, None], 0.0
    )
    row_part = jnp.where(positions == row_start[:, None], (1.0 - frac_down)[:, None], 0.0)
    row_part = row_part + jnp.where(positions == row_start[:, None] + 1, frac_down[:, None], 0.0)
    picked = (jnp.arange(slots, dtype=jnp.int32)[None, :, None] == slot_within[:, None]) & in_range[
        :, None
    ]
    row_weight = jnp.where(picked[:, :, None], row_part[:, None], 0.0)
    return (row_weight, column_weight)


def general_step(texel_atlas, observed, geometry, block_ids, pixel_slot, corner, bilinear_frac):
    tex_count = lax.axis_size("tex")
    owner_index = lax.axis_index("tex")
    own_blocks, channels, texels = texel_atlas.shape
    tiles_all = observed.shape[0]
    tiles_own = tiles_all // tex_count
    slots = block_ids.shape[2]
    groups = tiles_all // tex_count
    slot_blocks = block_ids[:, 0, :]
    slot_list = slot_blocks.reshape(-1)
    exact_mode = lax.Precision.HIGHEST

    def grouped(source):
        return source.reshape((groups, tex_count) + source.shape[1:])

    pixel_tables = (grouped(pixel_slot), grouped(corner), grouped(bilinear_frac))

    def widen(own_shard):
        return ring_gather(own_shard, "view").reshape((-1,) + own_shard.shape[1:])

    def pixels_of(whole_range):
        ranged = whole_range.shape[0]
        named = jnp.arange(ranged, dtype=jnp.int32)
        chooser = (jnp.clip(slot_list, 0, ranged - 1)[:, None] == named[None, :]).astype(jnp.float32)
        fetched = jnp.dot(chooser, whole_range.reshape(ranged, -1), precision=exact_mode)
        fetched = fetched.reshape(tiles_all, slots, channels, texels)

        def pixels_one_group(members):
            blocks, slot_part, corner_part, frac_part = members
            row_weight, column_weight = tables(
                slot_part, corner_part, frac_part, owner_index, slots
            )
            values = blocks.reshape(blocks.shape[0], slots, channels, BSIDE, BSIDE)
            middle = jnp.einsum("tjcyx,tjyp->tcxp", values, row_weight, precision=exact_mode)
            return jnp.sum(middle * column_weight[:, None], axis=2)

        partial_value = lax.map(pixels_one_group, (grouped(fetched),) + pixel_tables)
        partial_value = partial_value.reshape((tiles_all,) + partial_value.shape[2:])
        return ring_sum_scatter(grouped_by(partial_value, tex_count), "tex")

    def texel_terms(cotangent):
        gathered = ring_gather(cotangent, "tex").reshape((-1,) + cotangent.shape[1:])

        def texel_one_group(members):
            back_part, slot_part, corner_part, frac_part = members
            row_weight, column_weight = tables(
                slot_part, corner_part, frac_part, owner_index, slots
            )
            middle = back_part[:, :, None, :] * column_weight[:, None]
            values = jnp.einsum("tcxp,tjyp->tjcyx", middle, row_weight, precision=exact_mode)
            return values.reshape(values.shape[0] * slots, channels * texels)

        terms = lax.map(texel_one_group, (grouped(gathered),) + pixel_tables)
        return terms.reshape(tiles_all * slots, channels * texels)

    def owner_sums(terms):
        row_count = lax.axis_size("view") * own_blocks
        wanted = jnp.arange(row_count, dtype=jnp.int32)
        selector = (slot_list[None, :] == wanted[:, None]).astype(jnp.float32)
        summed = jnp.dot(selector, terms, precision=exact_mode, preferred_element_type=jnp.float32)
        return ring_sum_scatter(
            summed.reshape(row_count // own_blocks, own_blocks, channels, texels), "view"
        )

    atlas_range = widen(texel_atlas)
    base_params = pixels_of(atlas_range)
    geometry_own = lax.dynamic_slice_in_dim(geometry, owner_index * tiles_own, tiles_own, 0)
    observed_own = lax.dynamic_slice_in_dim(observed, owner_index * tiles_own, tiles_own, 0)

    def render(params):
        return shade(params, geometry_own)

    colors, backward = jax.vjp(render, base_params)

    def pullback(cotangent):
        return backward(cotangent)[0]

    unused, pushed = jax.vjp(pullback, jnp.zeros_like(colors))
    first_terms = texel_terms(backward(colors - observed_own)[0])
    gradient = owner_sums(first_terms)

    def inner_sums(values):
        return (jnp.sum(ring_gather(jnp.sum(ring_gather(values[0], "tex")), "view")),)

    update = jnp.zeros_like(gradient)
    residual = -gradient
    direction = residual
    norm_now = inner_sums((jnp.sum(residual * residual),))[0]
    for iteration in range(ITERS):
        applied = (
            owner_sums(texel_terms(backward(pushed(pixels_of(widen(direction)))[0])[0]))
            + DAMPING * direction
        )
        step_size = norm_now / inner_sums((jnp.sum(direction * applied),))[0]
        update = update + step_size * direction
        residual = residual - step_size * applied
        norm_next = inner_sums((jnp.sum(residual * residual),))[0]
        direction = residual + norm_next / norm_now * direction
        norm_now = norm_next
    return (update, residual)


MESH = pl.DeviceIdType.MESH
F32 = jnp.float32
BF16 = jnp.bfloat16
CHANNELS = 10
ROWS = 16
WINDOW = 512
PICKED = 256
SORTED = 1024
CHUNK = 896
DENSE = 1792
NT = (((1,), (1,)), ((), ()))


def halves(values):
    high = values.astype(BF16)
    low = (values - high.astype(F32)).astype(BF16)
    return high, low


def iota(shape, axis):
    return lax.broadcasted_iota(jnp.int32, shape, axis)


def pack(ids, obs, geo, frac, slot, corner, picked, ordered):
    tiles, pixels = slot.shape
    slots = ids.shape[0]
    blocks = lax.axis_size("view")
    owner = lax.axis_index("tex")
    lanes = pixels // 128

    slot_now = slot[...]
    corner_now = corner[...].astype(F32)
    tile_of = iota((tiles, 128), 0)
    target = jnp.zeros((tiles, pixels), jnp.int32)
    for s in range(slots):
        named = jnp.zeros((tiles, 128), jnp.int32)
        for t in range(tiles):
            named = jnp.where(tile_of == t, ids[s, t] + 1, named)
        target = jnp.where(
            slot_now == owner * slots + s, jnp.concatenate([named] * lanes, axis=1), target
        )
    mine = jnp.where(target > 0, 1.0, 0.0)
    before = jnp.where(iota((128, 128), 0) < iota((128, 128), 1), 1.0, 0.0).astype(BF16)

    stacked = jnp.concatenate([mine[:, c * 128 : c * 128 + 128] for c in range(lanes)], axis=0)
    ahead = jnp.dot(stacked.astype(BF16), before, preferred_element_type=F32)
    base = jnp.zeros((tiles, 1), F32)
    places = []
    for c in range(lanes):
        places.append(ahead[c * tiles : c * tiles + tiles] + base)
        base = base + jnp.sum(mine[:, c * 128 : c * 128 + 128], axis=1, keepdims=True)
    place = jnp.where(target > 0, jnp.concatenate(places, axis=1), -1.0).astype(jnp.int32)
    over = jnp.max(jnp.where(base > PICKED, 1.0, 0.0))
    total = jnp.sum(base)
    over = jnp.maximum(over, jnp.where(total > SORTED, 1.0, 0.0))

    target_f = target.astype(F32)
    wanted = iota((PICKED, pixels), 0)
    for t in range(tiles):
        numbers = jnp.concatenate(
            [
                obs[:, t, :],
                geo[:, t, :],
                frac[t],
                corner_now[t : t + 1],
                target_f[t : t + 1],
                jnp.zeros((3, pixels), F32),
            ],
            axis=0,
        )
        both = jnp.concatenate(halves(numbers), axis=0)
        hot = jnp.where(wanted == place[t : t + 1], 1.0, 0.0).astype(BF16)
        got = lax.dot_general(both, hot, NT, preferred_element_type=F32)
        picked[:, t * PICKED : t * PICKED + PICKED] = got[:ROWS] + got[ROWS:]

    listed = tiles * PICKED
    groups = listed // 128
    target_row = picked[12:13, :]
    member = jnp.where(
        iota((blocks, listed), 0).astype(F32) + 1.0 == target_row, 1.0, 0.0
    )
    stacked = jnp.concatenate([member[:, c * 128 : c * 128 + 128] for c in range(groups)], axis=0)
    ahead = jnp.dot(stacked.astype(BF16), before, preferred_element_type=F32)
    base = jnp.zeros((blocks, 1), F32)
    places = []
    for c in range(groups):
        places.append(ahead[c * blocks : c * blocks + blocks] + base)
        base = base + jnp.sum(member[:, c * 128 : c * 128 + 128], axis=1, keepdims=True)
    over = jnp.maximum(over, jnp.max(jnp.where(base > WINDOW, 1.0, 0.0)))
    earlier = jnp.where(iota((blocks, blocks), 1) < iota((blocks, blocks), 0), 1.0, 0.0)
    first = jnp.dot(
        earlier,
        jnp.broadcast_to(base, (blocks, 128)),
        precision=lax.Precision.HIGHEST,
        preferred_element_type=F32,
    )
    place = jnp.concatenate(places, axis=1) + first[:, 0:1]
    place = jnp.sum(member * place, axis=0, keepdims=True)
    place = jnp.where(target_row > 0.0, place, -1.0).astype(jnp.int32)
    both = jnp.concatenate(halves(picked[...]), axis=0)
    for q in range(SORTED // 256):
        hot = jnp.where(iota((256, listed), 0) + q * 256 == place, 1.0, 0.0).astype(BF16)
        got = lax.dot_general(both, hot, NT, preferred_element_type=F32)
        ordered[:, q * 256 : q * 256 + 256] = got[:ROWS] + got[ROWS:]

    return over, first, jnp.broadcast_to(base, (blocks, 128))


def folded(listed, turn, size):
    window = pltpu.roll(listed, turn, axis=1)[:, :WINDOW]
    top, low = window[:8], window[8:]
    place = iota((8, WINDOW), 0)
    low = jnp.where((place == 3) & (iota((8, WINDOW), 1).astype(F32) >= size), -1.0, low)
    raised = pltpu.roll(low, 4, axis=0)
    pairs = []
    for g in range(0, WINDOW, 256):
        pairs.append(jnp.where(place[:, :128] < 4, low[:, g : g + 128], raised[:, g + 128 : g + 256]))
    return jnp.concatenate([top] + pairs, axis=1)


def unfolded(window):
    low = []
    for g in range(WINDOW, window.shape[1], 128):
        pair = window[:, g : g + 128]
        low += [pair, pltpu.roll(pair, 4, axis=0)]
    return jnp.concatenate([window[:, :WINDOW], jnp.concatenate(low, axis=1)], axis=0)


def greet(barrier, tex, view, owners, views):
    for step in range(1, views):
        peer = lax.rem(view + step, views)
        pl.semaphore_signal(barrier, inc=1, device_id=(tex, peer), device_id_type=MESH)
    for step in range(1, owners):
        peer = lax.rem(tex + step, owners)
        pl.semaphore_signal(barrier, inc=1, device_id=(peer, view), device_id_type=MESH)


def send(source, target, axis, step, send_sem, recv_sem):
    count, me = lax.axis_size(axis), lax.axis_index(axis)
    peer = lax.rem(me + step, count)
    pltpu.make_async_remote_copy(
        src_ref=source,
        dst_ref=target.at[me],
        send_sem=send_sem,
        recv_sem=recv_sem,
        device_id={axis: peer},
        device_id_type=MESH,
    ).start()


def wait_all(target, sem):
    others = target.at[pl.ds(0, target.shape[0] - 1)]
    pltpu.make_async_copy(others, others, sem).wait()


def optics(params, geometry):
    roughness, tilt_x, tilt_y, occlusion = params[6], params[7], params[8], params[9]
    light, viewer = geometry[0:3], geometry[3:6]
    inverse_len = lax.rsqrt(1.0 + tilt_x * tilt_x + tilt_y * tilt_y)
    normal_x = tilt_x * inverse_len
    normal_y = tilt_y * inverse_len
    half = [a + b for a, b in zip(light, viewer)]
    scale = lax.rsqrt(half[0] * half[0] + half[1] * half[1] + half[2] * half[2])
    half = [a * scale for a in half]

    def facing(vector):
        cosine = normal_x * vector[0] + normal_y * vector[1] + inverse_len * vector[2]
        along_x = inverse_len * (vector[0] - normal_x * cosine)
        along_y = inverse_len * (vector[1] - normal_y * cosine)
        return cosine, along_x, along_y

    light_c, light_x, light_y = facing(light)
    view_c, view_x, view_y = facing(viewer)
    half_c, half_x, half_y = facing(half)
    miss = 1.0 - (viewer[0] * half[0] + viewer[1] * half[1] + viewer[2] * half[2])
    fifth = miss * miss
    fifth = fifth * fifth * miss
    square = roughness * roughness
    fourth = square * square
    inverse_d = 1.0 / (half_c * half_c * (fourth - 1.0) + 1.0)
    smith = 0.5 * square
    inverse_l = 1.0 / (light_c * (1.0 - smith) + smith)
    inverse_v = 1.0 / (view_c * (1.0 - smith) + smith)
    shape = 0.25 * inverse_d * inverse_d * inverse_l * inverse_v
    gloss = fourth * shape
    shape_slope = -4.0 * square * half_c * half_c * inverse_d
    shape_slope = shape_slope - 0.5 * (1.0 - light_c) * inverse_l - 0.5 * (1.0 - view_c) * inverse_v
    gloss_square = 2.0 * square * shape + gloss * shape_slope
    gloss_half = -4.0 * gloss * half_c * (fourth - 1.0) * inverse_d
    gloss_light = -gloss * (1.0 - smith) * inverse_l
    gloss_view = -gloss * (1.0 - smith) * inverse_v
    gloss_x = gloss_half * half_x + gloss_light * light_x + gloss_view * view_x
    gloss_y = gloss_half * half_y + gloss_light * light_y + gloss_view * view_y
    lit = occlusion * light_c
    fresnel = [params[3 + c] + (1.0 - params[3 + c]) * fifth for c in range(3)]
    total = [params[c] + gloss * fresnel[c] for c in range(3)]
    factors = [
        lit,
        lit * gloss * (1.0 - fifth),
        lit * gloss_square * 2.0 * roughness,
        occlusion * light_x,
        lit * gloss_x,
        occlusion * light_y,
        lit * gloss_y,
        light_c,
    ]
    return factors + total + fresnel, [lit * t for t in total]


def push(tangent, factors):
    albedo, specular, rough, ex, fx, ey, fy, shine = factors[:8]
    total, fresnel = factors[8:11], factors[11:14]
    on_total = ex * tangent[7] + ey * tangent[8] + shine * tangent[9]
    on_fresnel = rough * tangent[6] + fx * tangent[7] + fy * tangent[8]
    return [
        albedo * tangent[c] + specular * tangent[3 + c] + total[c] * on_total + fresnel[c] * on_fresnel
        for c in range(3)
    ]


def pull(colors, factors):
    albedo, specular, rough, ex, fx, ey, fy, shine = factors[:8]
    total, fresnel = factors[8:11], factors[11:14]
    e = total[0] * colors[0] + total[1] * colors[1] + total[2] * colors[2]
    f = fresnel[0] * colors[0] + fresnel[1] * colors[1] + fresnel[2] * colors[2]
    return (
        [albedo * c for c in colors]
        + [specular * c for c in colors]
        + [rough * f, ex * e + fx * f, ey * e + fy * f, shine * e]
    )


def whole_kernel(
    ids, obs_in, geo_in, frac_in, slot_in, corner_in, atlas_in, update, residual, flag,
    obs, geo, frac, slot, corner, atlas, picked, ordered, windows, landed, pixels, field,
    across, down, slopes, seen_start, seen_first, gathered, near, far,
    read_sems, send_window, recv_window, send_near, recv_near, send_far, recv_far,
):
    tex, me = lax.axis_index("tex"), lax.axis_index("view")
    senders, owners = landed.shape[0], near.shape[0]
    half_rows = CHANNELS * BSIDE // 2
    lane = iota((half_rows, 128), 1)
    reads = [
        pltpu.make_async_copy(source, target, read_sems.at[k])
        for k, (source, target) in enumerate(
            [
                (slot_in, slot),
                (corner_in, corner),
                (obs_in, obs),
                (geo_in, geo),
                (frac_in, frac),
                (atlas_in, atlas),
            ]
        )
    ]
    for read in reads:
        read.start()
    barrier = pltpu.get_barrier_semaphore()
    greet(barrier, tex, me, owners, senders)
    for read in reads:
        read.wait()
    over, first, sizes = pack(ids, obs, geo, frac, slot, corner, picked, ordered)
    turns = jnp.where(first > 0.0, jnp.maximum(float(SORTED) - first, 0.0), 0.0).astype(jnp.int32)
    back_by = lax.rem(senders - me, senders)
    turns = pltpu.roll(turns, back_by, axis=0)
    sizes = pltpu.roll(sizes, back_by, axis=0)
    listed = ordered[...]
    pl.semaphore_wait(barrier, owners + senders - 2)
    for step in range(1, senders):
        windows[step] = folded(listed, turns[step, 0], sizes[step : step + 1, 0:1])
        send(windows.at[step], landed, "view", step, send_window, recv_window)
    landed[me] = folded(listed, turns[0, 0], sizes[0:1, 0:1])

    def hold(values):
        high, low = halves(values)
        high, low = high.astype(F32), low.astype(F32)
        left = jnp.where(lane < BSIDE, high, pltpu.roll(low, BSIDE, axis=1)).astype(BF16)
        right = jnp.where(lane < BSIDE, pltpu.roll(high, BSIDE, axis=1), low).astype(BF16)
        field[:half_rows, :128] = left
        field[:half_rows, 128:] = left
        field[half_rows:, :128] = right
        field[half_rows:, 128:] = right

    def sample(c, rows):
        seen = jnp.dot(field[...], across[c], preferred_element_type=F32)
        seen = seen.reshape(2, CHANNELS, BSIDE // 2, CHUNK) * rows
        seen = jnp.sum(seen[0] + seen[1], axis=1)
        return [seen[k : k + 1] for k in range(CHANNELS)]

    def spread(c, rows, back):
        back = jnp.concatenate(back, axis=0)
        terms = (back.reshape(1, CHANNELS, 1, CHUNK) * rows).reshape(2 * half_rows, CHUNK)
        high, low = halves(terms)
        columns = across[c, BSIDE : 3 * BSIDE, :]
        gathered[...] += lax.dot_general(high, columns, NT, preferred_element_type=F32)
        gathered[...] += lax.dot_general(low, columns, NT, preferred_element_type=F32)

    def collected():
        left, right = gathered[:half_rows], gathered[half_rows:]
        left = left + pltpu.roll(left, BSIDE, axis=1)
        right = right + pltpu.roll(right, BSIDE, axis=1)
        return jnp.where(lane < BSIDE, left, right)

    hold(atlas[...])
    gathered[...] = jnp.zeros(gathered.shape, F32)
    wait_all(landed, recv_window)
    arrived = [unfolded(landed[j]) for j in range(senders)]
    live = [jnp.where(window[11:12] >= 0.0, 1.0, 0.0) for window in arrived]
    counts = jnp.sum(jnp.concatenate(live, axis=0), axis=1, keepdims=True)
    earlier = jnp.where(iota((senders, senders), 1) < iota((senders, senders), 0), 1.0, 0.0)
    begins = jnp.dot(
        earlier,
        jnp.broadcast_to(counts, (senders, 128)),
        precision=lax.Precision.HIGHEST,
        preferred_element_type=F32,
    )
    begins = jnp.minimum(begins, float(DENSE - 1)).astype(jnp.int32)
    dense = jnp.zeros((ROWS, DENSE), F32)
    for j in range(senders):
        window = jnp.where(live[j] > 0.0, arrived[j], 0.0)
        window = jnp.concatenate([window, jnp.zeros((ROWS, DENSE - WINDOW), F32)], axis=1)
        dense = dense + pltpu.roll(window, begins[j, 0], axis=1)
    pixels[...] = dense
    count = jnp.sum(counts)
    over = jnp.maximum(over, jnp.where(count > DENSE, 1.0, 0.0))
    chunks = DENSE // CHUNK

    def first_pass(c, carry):
        numbers = pixels[:, pl.ds(pl.multiple_of(c * CHUNK, CHUNK), CHUNK)]
        numbers = [numbers[k : k + 1] for k in range(ROWS)]
        used = (iota((1, CHUNK), 1) + c * CHUNK).astype(F32) < count
        frac_x, frac_y, spot = numbers[9:12]
        row = jnp.floor((spot + 0.5) * (1.0 / (BSIDE - 1)))
        column = spot - row * (BSIDE - 1)
        at = iota((BSIDE, CHUNK), 0).astype(F32)
        weight = jnp.where(at == column, 1.0 - frac_x, jnp.where(at == column + 1.0, frac_x, 0.0))
        high, low = halves(weight)
        across[c] = jnp.concatenate([high, high, low, low], axis=0)
        at = iota((BSIDE, CHUNK), 0)
        at = jnp.where(at < BSIDE // 2, 2 * at, 2 * at - (BSIDE - 1)).astype(F32)
        weight = jnp.where(at == row, 1.0 - frac_y, jnp.where(at == row + 1.0, frac_y, 0.0))
        weight = jnp.where(used, weight, 0.0)
        down[c] = weight
        rows = weight.reshape(2, 1, BSIDE // 2, CHUNK)
        factors, colors = optics(sample(c, rows), numbers[3:9])
        factors = [jnp.where(used, factor, 0.0) for factor in factors]
        slopes[c] = jnp.concatenate(factors + [jnp.zeros((2, CHUNK), F32)], axis=0)
        errors = [jnp.where(used, a - b, 0.0) for a, b in zip(colors, numbers[0:3])]
        spread(c, rows, pull(errors, factors))
        return carry

    lax.fori_loop(0, chunks, first_pass, 0)
    start_now = -collected()

    def factors_of(c):
        factors = slopes[c]
        return [factors[k : k + 1] for k in range(14)]

    def seen_of(c, kept):
        rows = down[c].reshape(2, 1, BSIDE // 2, CHUNK)
        colors = push(sample(c, rows), factors_of(c))
        kept[c] = jnp.concatenate(colors + [jnp.zeros((5, CHUNK), F32)], axis=0)

    def spread_seen(c, kept):
        rows = down[c].reshape(2, 1, BSIDE // 2, CHUNK)
        colors = kept[c]
        spread(c, rows, pull([colors[k : k + 1] for k in range(3)], factors_of(c)))

    def start_pass(c, carry):
        seen_of(c, seen_start)
        spread_seen(c, seen_start)
        return carry

    def first_seen(c, carry):
        seen_of(c, seen_first)
        return carry

    hold(start_now)
    gathered[...] = jnp.zeros(gathered.shape, F32)
    lax.fori_loop(0, chunks, start_pass, 0)
    first_now = collected() + DAMPING * start_now
    hold(first_now)
    gathered[...] = jnp.zeros(gathered.shape, F32)
    lax.fori_loop(0, chunks, first_seen, 0)

    start_start = jnp.sum(start_now * start_now)
    start_first = jnp.sum(start_now * first_now)
    guess = jnp.where(start_first > 0.0, start_start / jnp.where(start_first > 0.0, start_first, 1.0), 0.0)
    rest = start_now - guess * first_now
    rest_rest = jnp.sum(rest * rest)
    rest_first = jnp.sum(rest * first_now)
    first_first = jnp.sum(first_now * first_now)
    from_start, from_first = seen_start[...], seen_first[...]
    from_rest = from_start - guess * from_first
    found = [
        start_start,
        start_first,
        rest_rest,
        rest_first,
        first_first,
        jnp.sum(from_rest * from_rest) + DAMPING * rest_rest,
        jnp.sum(from_rest * from_first) + DAMPING * rest_first,
        jnp.sum(from_first * from_first) + DAMPING * first_first,
        guess,
    ]
    place = iota((1, 128), 1)
    line = jnp.where(place == len(found), over, 0.0)
    for k, value in enumerate(found):
        line = jnp.where(place == k, value, line)
    near[tex] = line
    for step in range(1, owners):
        send(near.at[tex], near, "tex", step, send_near, recv_near)
    spread_seen(0, seen_first)
    wait_all(near, recv_near)
    far[me] = near[...]
    for step in range(1, senders):
        send(near, far, "view", step, send_far, recv_far)
    for c in range(1, chunks):
        spread_seen(c, seen_first)
    second_now = collected() + DAMPING * first_now
    wait_all(far, recv_far)
    table = far[...].reshape(owners * senders, 128)
    column = [table[:, k : k + 1] for k in range(10)]

    def added(values):
        return jnp.sum(values, axis=0, keepdims=True)

    start_start, start_first = added(column[0]), added(column[1])
    one = start_start / start_first
    change = column[8] - one
    norm = added(column[2] + change * (2.0 * column[3] + change * column[4]))
    turn = norm / start_start
    cross = added(column[3] + change * column[4])
    curve = added(column[5] + change * (2.0 * column[6] + change * column[7]))
    curve = curve + 2.0 * turn * cross + turn * turn * start_first
    two = norm / curve
    near_part = one + two * (1.0 + turn)
    update[...] = near_part * start_now - one * two * first_now
    residual[...] = start_now - near_part * first_now + one * two * second_now
    flag[...] = jnp.broadcast_to(added(column[9]), flag.shape)
    wait_all(landed, send_window)
    wait_all(near, send_near)
    wait_all(far, send_far)


def in_vmem(count):
    return [pl.BlockSpec(memory_space=pltpu.VMEM)] * count


def per_device(texel_atlas, observed, geometry, block_ids, pixel_slot, corner, bilinear_frac):
    owners, views = lax.axis_size("tex"), lax.axis_size("view")
    tiles, slots = block_ids.shape[0], block_ids.shape[2]
    half_rows = CHANNELS * BSIDE // 2
    shaped = jax.ShapeDtypeStruct

    update, residual, flag = pl.pallas_call(
        whole_kernel,
        out_shape=(shaped((half_rows, 128), F32),) * 2 + (shaped((1, 128), F32),),
        in_specs=[pl.BlockSpec(memory_space=pltpu.SMEM)] + [pl.BlockSpec(memory_space=pl.ANY)] * 6,
        out_specs=tuple(in_vmem(3)),
        scratch_shapes=[
            pltpu.VMEM((3, tiles, pixel_slot.shape[1]), F32),
            pltpu.VMEM((6, tiles, pixel_slot.shape[1]), F32),
            pltpu.VMEM(bilinear_frac.shape, F32),
            pltpu.VMEM(pixel_slot.shape, jnp.int32),
            pltpu.VMEM(pixel_slot.shape, jnp.int32),
            pltpu.VMEM((half_rows, 128), F32),
            pltpu.VMEM((ROWS, tiles * PICKED), F32),
            pltpu.VMEM((ROWS, SORTED), F32),
            pltpu.VMEM((views, 8, WINDOW * 3 // 2), F32),
            pltpu.VMEM((views, 8, WINDOW * 3 // 2), F32),
            pltpu.VMEM((ROWS, DENSE), F32),
            pltpu.VMEM((2 * half_rows, 256), BF16),
            pltpu.VMEM((DENSE // CHUNK, 4 * BSIDE, CHUNK), BF16),
            pltpu.VMEM((DENSE // CHUNK, BSIDE, CHUNK), F32),
            pltpu.VMEM((DENSE // CHUNK, ROWS, CHUNK), F32),
            pltpu.VMEM((DENSE // CHUNK, 8, CHUNK), F32),
            pltpu.VMEM((DENSE // CHUNK, 8, CHUNK), F32),
            pltpu.VMEM((2 * half_rows, 128), F32),
            pltpu.VMEM((owners, 1, 128), F32),
            pltpu.VMEM((views, owners, 1, 128), F32),
        ]
        + [pltpu.SemaphoreType.DMA((6,))]
        + [pltpu.SemaphoreType.DMA] * 6,
        compiler_params=pltpu.CompilerParams(
            collective_id=0, has_side_effects=True, vmem_limit_bytes=56 << 20
        ),
    )(
        block_ids.reshape(tiles, slots).T,
        observed.transpose(1, 0, 2),
        geometry.transpose(1, 0, 2),
        bilinear_frac,
        pixel_slot,
        corner,
        texel_atlas.reshape(half_rows, 128),
    )

    def quick():
        return update.reshape(texel_atlas.shape), residual.reshape(texel_atlas.shape)

    def general():
        return general_step(
            texel_atlas, observed, geometry, block_ids, pixel_slot, corner, bilinear_frac
        )

    return lax.cond(flag[0, 0] > 0.0, general, quick)


def solution(mesh):
    in_specs = (
        P(("tex", "view"), None, None),
        P("view", None, None),
        P("view", None, None),
        P("view", "tex", None),
        P("view", None),
        P("view", None),
        P("view", None, None),
    )
    out_specs = (P(("tex", "view"), None, None), P(("tex", "view"), None, None))
    return jax.shard_map(
        per_device, mesh=mesh, in_specs=in_specs, out_specs=out_specs, check_vma=False
    )
```

```python
import functools
import math

import jax
import jax.numpy as jnp
from jax import lax
from jax.experimental import pallas as pl
from jax.experimental.pallas import tpu as pltpu
from jax.sharding import PartitionSpec as P

BSIDE = 64
ITERS = 2


DAMPING = 0.1


def passed_on(values, axis):
    count = lax.axis_size(axis)
    return lax.ppermute(values, axis, [(k, (k + 1) % count) for k in range(count)])


def ring_gather(values, axis):
    count, me = lax.axis_size(axis), lax.axis_index(axis)

    def step(s, state):
        held, block = state
        block = passed_on(block, axis)
        return held.at[lax.rem(me - s + count, count)].set(block), block

    held = jnp.zeros((count,) + values.shape, values.dtype).at[me].set(values)
    return lax.fori_loop(1, count, step, (held, values))[0]


def ring_sum_scatter(values, axis):
    count, me = lax.axis_size(axis), lax.axis_index(axis)

    def step(s, total):
        return passed_on(total, axis) + values[lax.rem(me - 1 - s + 2 * count, count)]

    return lax.fori_loop(1, count, step, values[lax.rem(me - 1 + count, count)])


def grouped_by(values, count):
    return values.reshape((count, values.shape[0] // count) + values.shape[1:])


def shade(params, geometry):
    albedo = params[:, 0:3]
    specular = params[:, 3:6]
    roughness = params[:, 6]
    tilt_x = params[:, 7]
    tilt_y = params[:, 8]
    occlusion = params[:, 9]
    inverse_len = lax.rsqrt(1.0 + tilt_x * tilt_x + tilt_y * tilt_y)
    normal_x = tilt_x * inverse_len
    normal_y = tilt_y * inverse_len
    light_dir = geometry[:, 0:3]
    viewer = geometry[:, 3:6]
    halfway = light_dir + viewer
    halfway = halfway * lax.rsqrt(jnp.sum(halfway * halfway, axis=1, keepdims=True))

    def facing(vector):
        return normal_x * vector[:, 0] + normal_y * vector[:, 1] + inverse_len * vector[:, 2]

    cosine_light = facing(light_dir)
    cosine_view = facing(viewer)
    cosine_half = facing(halfway)
    view_half = jnp.sum(viewer * halfway, axis=1)
    rough_square = roughness * roughness
    rough_fourth = rough_square * rough_square
    denominator = cosine_half * cosine_half * (rough_fourth - 1.0) + 1.0
    distribution = rough_fourth / (math.pi * denominator * denominator)
    smith_k = 0.5 * rough_square
    masking = cosine_light / (cosine_light * (1.0 - smith_k) + smith_k)
    masking = masking * cosine_view / (cosine_view * (1.0 - smith_k) + smith_k)
    fresnel = specular + (1.0 - specular) * ((1.0 - view_half) ** 5)[:, None]
    reflected = (distribution * masking / (4.0 * cosine_light * cosine_view))[:, None] * fresnel
    return (occlusion * cosine_light)[:, None] * (albedo + math.pi * reflected)


def tables(slot_part, corner_part, frac_part, owner_index, slots):
    in_range = slot_part // slots == owner_index
    slot_within = slot_part % slots
    row_start = corner_part // (BSIDE - 1)
    column_start = corner_part % (BSIDE - 1)
    across = frac_part[:, 0]
    frac_down = frac_part[:, 1]
    positions = jnp.arange(BSIDE, dtype=jnp.int32)[None, :, None]
    column_weight = jnp.where(positions == column_start[:, None], (1.0 - across)[:, None], 0.0)
    column_weight = column_weight + jnp.where(
        positions == column_start[:, None] + 1, across[:, None], 0.0
    )
    row_part = jnp.where(positions == row_start[:, None], (1.0 - frac_down)[:, None], 0.0)
    row_part = row_part + jnp.where(positions == row_start[:, None] + 1, frac_down[:, None], 0.0)
    picked = (jnp.arange(slots, dtype=jnp.int32)[None, :, None] == slot_within[:, None]) & in_range[
        :, None
    ]
    row_weight = jnp.where(picked[:, :, None], row_part[:, None], 0.0)
    return (row_weight, column_weight)


def general_step(texel_atlas, observed, geometry, block_ids, pixel_slot, corner, bilinear_frac):
    tex_count = lax.axis_size("tex")
    owner_index = lax.axis_index("tex")
    own_blocks, channels, texels = texel_atlas.shape
    tiles_all = observed.shape[0]
    tiles_own = tiles_all // tex_count
    slots = block_ids.shape[2]
    groups = tiles_all // tex_count
    slot_blocks = block_ids[:, 0, :]
    slot_list = slot_blocks.reshape(-1)
    exact_mode = lax.Precision.HIGHEST

    def grouped(source):
        return source.reshape((groups, tex_count) + source.shape[1:])

    pixel_tables = (grouped(pixel_slot), grouped(corner), grouped(bilinear_frac))

    def widen(own_shard):
        return ring_gather(own_shard, "view").reshape((-1,) + own_shard.shape[1:])

    def pixels_of(whole_range):
        ranged = whole_range.shape[0]
        named = jnp.arange(ranged, dtype=jnp.int32)
        chooser = (jnp.clip(slot_list, 0, ranged - 1)[:, None] == named[None, :]).astype(jnp.float32)
        fetched = jnp.dot(chooser, whole_range.reshape(ranged, -1), precision=exact_mode)
        fetched = fetched.reshape(tiles_all, slots, channels, texels)

        def pixels_one_group(members):
            blocks, slot_part, corner_part, frac_part = members
            row_weight, column_weight = tables(
                slot_part, corner_part, frac_part, owner_index, slots
            )
            values = blocks.reshape(blocks.shape[0], slots, channels, BSIDE, BSIDE)
            middle = jnp.einsum("tjcyx,tjyp->tcxp", values, row_weight, precision=exact_mode)
            return jnp.sum(middle * column_weight[:, None], axis=2)

        partial_value = lax.map(pixels_one_group, (grouped(fetched),) + pixel_tables)
        partial_value = partial_value.reshape((tiles_all,) + partial_value.shape[2:])
        return ring_sum_scatter(grouped_by(partial_value, tex_count), "tex")

    def texel_terms(cotangent):
        gathered = ring_gather(cotangent, "tex").reshape((-1,) + cotangent.shape[1:])

        def texel_one_group(members):
            back_part, slot_part, corner_part, frac_part = members
            row_weight, column_weight = tables(
                slot_part, corner_part, frac_part, owner_index, slots
            )
            middle = back_part[:, :, None, :] * column_weight[:, None]
            values = jnp.einsum("tcxp,tjyp->tjcyx", middle, row_weight, precision=exact_mode)
            return values.reshape(values.shape[0] * slots, channels * texels)

        terms = lax.map(texel_one_group, (grouped(gathered),) + pixel_tables)
        return terms.reshape(tiles_all * slots, channels * texels)

    def owner_sums(terms):
        row_count = lax.axis_size("view") * own_blocks
        wanted = jnp.arange(row_count, dtype=jnp.int32)
        selector = (slot_list[None, :] == wanted[:, None]).astype(jnp.float32)
        summed = jnp.dot(selector, terms, precision=exact_mode, preferred_element_type=jnp.float32)
        return ring_sum_scatter(
            summed.reshape(row_count // own_blocks, own_blocks, channels, texels), "view"
        )

    atlas_range = widen(texel_atlas)
    base_params = pixels_of(atlas_range)
    geometry_own = lax.dynamic_slice_in_dim(geometry, owner_index * tiles_own, tiles_own, 0)
    observed_own = lax.dynamic_slice_in_dim(observed, owner_index * tiles_own, tiles_own, 0)

    def render(params):
        return shade(params, geometry_own)

    colors, backward = jax.vjp(render, base_params)

    def pullback(cotangent):
        return backward(cotangent)[0]

    unused, pushed = jax.vjp(pullback, jnp.zeros_like(colors))
    first_terms = texel_terms(backward(colors - observed_own)[0])
    gradient = owner_sums(first_terms)

    def inner_sums(values):
        return (jnp.sum(ring_gather(jnp.sum(ring_gather(values[0], "tex")), "view")),)

    update = jnp.zeros_like(gradient)
    residual = -gradient
    direction = residual
    norm_now = inner_sums((jnp.sum(residual * residual),))[0]
    for iteration in range(ITERS):
        applied = (
            owner_sums(texel_terms(backward(pushed(pixels_of(widen(direction)))[0])[0]))
            + DAMPING * direction
        )
        step_size = norm_now / inner_sums((jnp.sum(direction * applied),))[0]
        update = update + step_size * direction
        residual = residual - step_size * applied
        norm_next = inner_sums((jnp.sum(residual * residual),))[0]
        direction = residual + norm_next / norm_now * direction
        norm_now = norm_next
    return (update, residual)


MESH = pl.DeviceIdType.MESH
F32 = jnp.float32
BF16 = jnp.bfloat16
CHANNELS = 10
ROWS = 16
WINDOW = 512
PICKED = 256
SORTED = 1024
CHUNK = 896
TALL = CHUNK // 128
DENSE = 1792
NT = (((1,), (1,)), ((), ()))


def halves(values):
    high = values.astype(BF16)
    low = (values - high.astype(F32)).astype(BF16)
    return high, low


def iota(shape, axis):
    return lax.broadcasted_iota(jnp.int32, shape, axis)


def pack(ids, obs, geo, frac, slot, corner, picked, ordered):
    tiles, pixels = slot.shape
    slots = ids.shape[0]
    blocks = lax.axis_size("view")
    owner = lax.axis_index("tex")
    lanes = pixels // 128

    slot_now = slot[...]
    corner_now = corner[...].astype(F32)
    tile_of = iota((tiles, 128), 0)
    target = jnp.zeros((tiles, pixels), jnp.int32)
    for s in range(slots):
        named = jnp.zeros((tiles, 128), jnp.int32)
        for t in range(tiles):
            named = jnp.where(tile_of == t, ids[s, t] + 1, named)
        target = jnp.where(
            slot_now == owner * slots + s, jnp.concatenate([named] * lanes, axis=1), target
        )
    mine = jnp.where(target > 0, 1.0, 0.0)
    before = jnp.where(iota((128, 128), 0) < iota((128, 128), 1), 1.0, 0.0).astype(BF16)

    stacked = jnp.concatenate([mine[:, c * 128 : c * 128 + 128] for c in range(lanes)], axis=0)
    ahead = jnp.dot(stacked.astype(BF16), before, preferred_element_type=F32)
    base = jnp.zeros((tiles, 1), F32)
    places = []
    for c in range(lanes):
        places.append(ahead[c * tiles : c * tiles + tiles] + base)
        base = base + jnp.sum(mine[:, c * 128 : c * 128 + 128], axis=1, keepdims=True)
    place = jnp.where(target > 0, jnp.concatenate(places, axis=1), -1.0).astype(jnp.int32)
    over = jnp.max(jnp.where(base > PICKED, 1.0, 0.0))
    total = jnp.sum(base)
    over = jnp.maximum(over, jnp.where(total > SORTED, 1.0, 0.0))

    target_f = target.astype(F32)
    wanted = iota((PICKED, pixels), 0)
    for t in range(tiles):
        numbers = jnp.concatenate(
            [
                obs[:, t, :],
                geo[:, t, :],
                frac[t],
                corner_now[t : t + 1],
                target_f[t : t + 1],
                jnp.zeros((3, pixels), F32),
            ],
            axis=0,
        )
        both = jnp.concatenate(halves(numbers), axis=0)
        hot = jnp.where(wanted == place[t : t + 1], 1.0, 0.0).astype(BF16)
        got = lax.dot_general(both, hot, NT, preferred_element_type=F32)
        picked[:, t * PICKED : t * PICKED + PICKED] = got[:ROWS] + got[ROWS:]

    listed = tiles * PICKED
    groups = listed // 128
    target_row = picked[12:13, :]
    member = jnp.where(
        iota((blocks, listed), 0).astype(F32) + 1.0 == target_row, 1.0, 0.0
    )
    stacked = jnp.concatenate([member[:, c * 128 : c * 128 + 128] for c in range(groups)], axis=0)
    ahead = jnp.dot(stacked.astype(BF16), before, preferred_element_type=F32)
    base = jnp.zeros((blocks, 1), F32)
    places = []
    for c in range(groups):
        places.append(ahead[c * blocks : c * blocks + blocks] + base)
        base = base + jnp.sum(member[:, c * 128 : c * 128 + 128], axis=1, keepdims=True)
    over = jnp.maximum(over, jnp.max(jnp.where(base > WINDOW, 1.0, 0.0)))
    earlier = jnp.where(iota((blocks, blocks), 1) < iota((blocks, blocks), 0), 1.0, 0.0)
    first = jnp.dot(
        earlier,
        jnp.broadcast_to(base, (blocks, 128)),
        precision=lax.Precision.HIGHEST,
        preferred_element_type=F32,
    )
    place = jnp.concatenate(places, axis=1) + first[:, 0:1]
    place = jnp.sum(member * place, axis=0, keepdims=True)
    place = jnp.where(target_row > 0.0, place, -1.0).astype(jnp.int32)
    both = jnp.concatenate(halves(picked[...]), axis=0)
    for q in range(SORTED // 256):
        hot = jnp.where(iota((256, listed), 0) + q * 256 == place, 1.0, 0.0).astype(BF16)
        got = lax.dot_general(both, hot, NT, preferred_element_type=F32)
        ordered[:, q * 256 : q * 256 + 256] = got[:ROWS] + got[ROWS:]

    return over, first, jnp.broadcast_to(base, (blocks, 128))


def folded(listed, turn, size):
    window = pltpu.roll(listed, turn, axis=1)[:, :WINDOW]
    top, low = window[:8], window[8:]
    place = iota((8, WINDOW), 0)
    low = jnp.where((place == 3) & (iota((8, WINDOW), 1).astype(F32) >= size), -1.0, low)
    raised = pltpu.roll(low, 4, axis=0)
    pairs = []
    for g in range(0, WINDOW, 256):
        pairs.append(jnp.where(place[:, :128] < 4, low[:, g : g + 128], raised[:, g + 128 : g + 256]))
    return jnp.concatenate([top] + pairs, axis=1)


def unfolded(window):
    low = []
    for g in range(WINDOW, window.shape[1], 128):
        pair = window[:, g : g + 128]
        low += [pair, pltpu.roll(pair, 4, axis=0)]
    return jnp.concatenate([window[:, :WINDOW], jnp.concatenate(low, axis=1)], axis=0)


def greet(barrier, tex, view, owners, views):
    for step in range(1, views):
        peer = lax.rem(view + step, views)
        pl.semaphore_signal(barrier, inc=1, device_id=(tex, peer), device_id_type=MESH)
    for step in range(1, owners):
        peer = lax.rem(tex + step, owners)
        pl.semaphore_signal(barrier, inc=1, device_id=(peer, view), device_id_type=MESH)


def send(source, target, axis, step, send_sem, recv_sem):
    count, me = lax.axis_size(axis), lax.axis_index(axis)
    peer = lax.rem(me + step, count)
    pltpu.make_async_remote_copy(
        src_ref=source,
        dst_ref=target.at[me],
        send_sem=send_sem,
        recv_sem=recv_sem,
        device_id={axis: peer},
        device_id_type=MESH,
    ).start()


def wait_all(target, sem):
    others = target.at[pl.ds(0, target.shape[0] - 1)]
    pltpu.make_async_copy(others, others, sem).wait()


def optics(params, geometry):
    roughness, tilt_x, tilt_y, occlusion = params[6], params[7], params[8], params[9]
    light, viewer = geometry[0:3], geometry[3:6]
    inverse_len = lax.rsqrt(1.0 + tilt_x * tilt_x + tilt_y * tilt_y)
    normal_x = tilt_x * inverse_len
    normal_y = tilt_y * inverse_len
    half = [a + b for a, b in zip(light, viewer)]
    scale = lax.rsqrt(half[0] * half[0] + half[1] * half[1] + half[2] * half[2])
    half = [a * scale for a in half]

    def facing(vector):
        cosine = normal_x * vector[0] + normal_y * vector[1] + inverse_len * vector[2]
        along_x = inverse_len * (vector[0] - normal_x * cosine)
        along_y = inverse_len * (vector[1] - normal_y * cosine)
        return cosine, along_x, along_y

    light_c, light_x, light_y = facing(light)
    view_c, view_x, view_y = facing(viewer)
    half_c, half_x, half_y = facing(half)
    miss = 1.0 - (viewer[0] * half[0] + viewer[1] * half[1] + viewer[2] * half[2])
    fifth = miss * miss
    fifth = fifth * fifth * miss
    square = roughness * roughness
    fourth = square * square
    inverse_d = 1.0 / (half_c * half_c * (fourth - 1.0) + 1.0)
    smith = 0.5 * square
    inverse_l = 1.0 / (light_c * (1.0 - smith) + smith)
    inverse_v = 1.0 / (view_c * (1.0 - smith) + smith)
    shape = 0.25 * inverse_d * inverse_d * inverse_l * inverse_v
    gloss = fourth * shape
    shape_slope = -4.0 * square * half_c * half_c * inverse_d
    shape_slope = shape_slope - 0.5 * (1.0 - light_c) * inverse_l - 0.5 * (1.0 - view_c) * inverse_v
    gloss_square = 2.0 * square * shape + gloss * shape_slope
    gloss_half = -4.0 * gloss * half_c * (fourth - 1.0) * inverse_d
    gloss_light = -gloss * (1.0 - smith) * inverse_l
    gloss_view = -gloss * (1.0 - smith) * inverse_v
    gloss_x = gloss_half * half_x + gloss_light * light_x + gloss_view * view_x
    gloss_y = gloss_half * half_y + gloss_light * light_y + gloss_view * view_y
    lit = occlusion * light_c
    fresnel = [params[3 + c] + (1.0 - params[3 + c]) * fifth for c in range(3)]
    total = [params[c] + gloss * fresnel[c] for c in range(3)]
    factors = [
        lit,
        lit * gloss * (1.0 - fifth),
        lit * gloss_square * 2.0 * roughness,
        occlusion * light_x,
        lit * gloss_x,
        occlusion * light_y,
        lit * gloss_y,
        light_c,
    ]
    return factors + total + fresnel, [lit * t for t in total]


def push(tangent, factors):
    albedo, specular, rough, ex, fx, ey, fy, shine = factors[:8]
    total, fresnel = factors[8:11], factors[11:14]
    on_total = ex * tangent[7] + ey * tangent[8] + shine * tangent[9]
    on_fresnel = rough * tangent[6] + fx * tangent[7] + fy * tangent[8]
    return [
        albedo * tangent[c] + specular * tangent[3 + c] + total[c] * on_total + fresnel[c] * on_fresnel
        for c in range(3)
    ]


def pull(colors, factors):
    albedo, specular, rough, ex, fx, ey, fy, shine = factors[:8]
    total, fresnel = factors[8:11], factors[11:14]
    e = total[0] * colors[0] + total[1] * colors[1] + total[2] * colors[2]
    f = fresnel[0] * colors[0] + fresnel[1] * colors[1] + fresnel[2] * colors[2]
    return (
        [albedo * c for c in colors]
        + [specular * c for c in colors]
        + [rough * f, ex * e + fx * f, ey * e + fy * f, shine * e]
    )


def whole_kernel(
    ids, obs_in, geo_in, frac_in, slot_in, corner_in, atlas_in, update, residual, flag,
    obs, geo, frac, slot, corner, atlas, picked, ordered, windows, landed, pixels, field,
    across, down, turned, stood, slopes, seen_start, seen_first, gathered, near, far,
    read_sems, send_window, recv_window, send_near, recv_near, send_far, recv_far,
):
    tex, me = lax.axis_index("tex"), lax.axis_index("view")
    senders, owners = landed.shape[0], near.shape[0]
    half_rows = CHANNELS * BSIDE // 2
    lane = iota((half_rows, 128), 1)
    reads = [
        pltpu.make_async_copy(source, target, read_sems.at[k])
        for k, (source, target) in enumerate(
            [
                (slot_in, slot),
                (corner_in, corner),
                (obs_in, obs),
                (geo_in, geo),
                (frac_in, frac),
                (atlas_in, atlas),
            ]
        )
    ]
    for read in reads:
        read.start()
    barrier = pltpu.get_barrier_semaphore()
    greet(barrier, tex, me, owners, senders)
    for read in reads:
        read.wait()
    over, first, sizes = pack(ids, obs, geo, frac, slot, corner, picked, ordered)
    turns = jnp.where(first > 0.0, jnp.maximum(float(SORTED) - first, 0.0), 0.0).astype(jnp.int32)
    deep = math.isqrt(senders)
    up, side = me // deep, lax.rem(me, deep)
    listed = ordered[...]
    pl.semaphore_wait(barrier, owners + senders - 2)

    def window_for(peer):
        named = iota(turns.shape, 0) == peer
        turn = jnp.sum(jnp.where(named, turns, 0)[:, 0:1])
        size = jnp.sum(jnp.where(named, sizes, 0.0)[:, 0:1], axis=0, keepdims=True)
        return folded(listed, turn, size)

    apart = [(min(a, deep - a) + min(b, deep - b), a, b) for a in range(deep) for b in range(deep)]
    for _, a, b in sorted(apart, reverse=True)[:-1]:
        step = a * deep + b
        peer = lax.rem(up + a, deep) * deep + lax.rem(side + b, deep)
        windows[step] = window_for(peer)
        pltpu.make_async_remote_copy(
            src_ref=windows.at[step],
            dst_ref=landed.at[me],
            send_sem=send_window,
            recv_sem=recv_window,
            device_id=(tex, peer),
            device_id_type=MESH,
        ).start()
    landed[me] = window_for(me)


    def hold(values):
        high, low = halves(values)
        high, low = high.astype(F32), low.astype(F32)
        left = jnp.where(lane < BSIDE, high, pltpu.roll(low, BSIDE, axis=1)).astype(BF16)
        right = jnp.where(lane < BSIDE, pltpu.roll(high, BSIDE, axis=1), low).astype(BF16)
        field[:half_rows, :128] = left
        field[:half_rows, 128:] = left
        field[half_rows:, :128] = right
        field[half_rows:, 128:] = right

    def sample(c, rows):
        seen = jnp.dot(field[...], across[c], preferred_element_type=F32)
        seen = seen.reshape(2, CHANNELS, BSIDE // 2, CHUNK) * rows
        seen = jnp.sum(seen[0] + seen[1], axis=1)
        for j in range(TALL):
            turned[:, j, :] = seen[:, j * 128 : j * 128 + 128]
        return [turned[k] for k in range(CHANNELS)]

    def spread(c, rows, back):
        for k in range(CHANNELS):
            turned[k] = back[k]
        back = jnp.concatenate([turned[:, j, :] for j in range(TALL)], axis=1)
        terms = (back.reshape(1, CHANNELS, 1, CHUNK) * rows).reshape(2 * half_rows, CHUNK)
        high, low = halves(terms)
        columns = across[c, BSIDE : 3 * BSIDE, :]
        gathered[...] += lax.dot_general(high, columns, NT, preferred_element_type=F32)
        gathered[...] += lax.dot_general(low, columns, NT, preferred_element_type=F32)

    def collected():
        left, right = gathered[:half_rows], gathered[half_rows:]
        left = left + pltpu.roll(left, BSIDE, axis=1)
        right = right + pltpu.roll(right, BSIDE, axis=1)
        return jnp.where(lane < BSIDE, left, right)

    hold(atlas[...])
    gathered[...] = jnp.zeros(gathered.shape, F32)
    wait_all(landed, recv_window)
    arrived = [unfolded(landed[j]) for j in range(senders)]
    live = [jnp.where(window[11:12] >= 0.0, 1.0, 0.0) for window in arrived]
    counts = jnp.sum(jnp.concatenate(live, axis=0), axis=1, keepdims=True)
    earlier = jnp.where(iota((senders, senders), 1) < iota((senders, senders), 0), 1.0, 0.0)
    begins = jnp.dot(
        earlier,
        jnp.broadcast_to(counts, (senders, 128)),
        precision=lax.Precision.HIGHEST,
        preferred_element_type=F32,
    )
    begins = jnp.minimum(begins, float(DENSE - 1)).astype(jnp.int32)
    dense = jnp.zeros((ROWS, DENSE), F32)
    for j in range(senders):
        window = jnp.where(live[j] > 0.0, arrived[j], 0.0)
        window = jnp.concatenate([window, jnp.zeros((ROWS, DENSE - WINDOW), F32)], axis=1)
        dense = dense + pltpu.roll(window, begins[j, 0], axis=1)
    pixels[...] = dense
    for c in range(DENSE // CHUNK):
        for j in range(TALL):
            at = c * CHUNK + j * 128
            stood[c, :, j, :] = dense[:, at : at + 128]
    count = jnp.sum(counts)
    over = jnp.maximum(over, jnp.where(count > DENSE, 1.0, 0.0))
    chunks = DENSE // CHUNK

    def first_pass(c, carry):
        numbers = pixels[:, pl.ds(pl.multiple_of(c * CHUNK, CHUNK), CHUNK)]
        numbers = [numbers[k : k + 1] for k in range(ROWS)]
        used = (iota((1, CHUNK), 1) + c * CHUNK).astype(F32) < count
        frac_x, frac_y, spot = numbers[9:12]
        row = jnp.floor((spot + 0.5) * (1.0 / (BSIDE - 1)))
        column = spot - row * (BSIDE - 1)
        at = iota((BSIDE, CHUNK), 0).astype(F32)
        weight = jnp.where(at == column, 1.0 - frac_x, jnp.where(at == column + 1.0, frac_x, 0.0))
        high, low = halves(weight)
        across[c] = jnp.concatenate([high, high, low, low], axis=0)
        at = iota((BSIDE, CHUNK), 0)
        at = jnp.where(at < BSIDE // 2, 2 * at, 2 * at - (BSIDE - 1)).astype(F32)
        weight = jnp.where(at == row, 1.0 - frac_y, jnp.where(at == row + 1.0, frac_y, 0.0))
        weight = jnp.where(used, weight, 0.0)
        down[c] = weight
        rows = weight.reshape(2, 1, BSIDE // 2, CHUNK)
        standing = [stood[c, k] for k in range(9)]
        factors, colors = optics(sample(c, rows), standing[3:9])
        place = iota((TALL, 128), 0) * 128 + iota((TALL, 128), 1) + c * CHUNK
        used = place.astype(F32) < count
        factors = [jnp.where(used, factor, 0.0) for factor in factors]
        for k, factor in enumerate(factors):
            slopes[c, k] = factor
        errors = [jnp.where(used, a - b, 0.0) for a, b in zip(colors, standing[0:3])]
        spread(c, rows, pull(errors, factors))
        return carry

    lax.fori_loop(0, chunks, first_pass, 0)
    start_now = -collected()

    def factors_of(c):
        return [slopes[c, k] for k in range(14)]

    def seen_of(c, kept):
        rows = down[c].reshape(2, 1, BSIDE // 2, CHUNK)
        colors = push(sample(c, rows), factors_of(c))
        for k in range(3):
            kept[c, k] = colors[k]

    def spread_seen(c, kept):
        rows = down[c].reshape(2, 1, BSIDE // 2, CHUNK)
        spread(c, rows, pull([kept[c, k] for k in range(3)], factors_of(c)))

    def start_pass(c, carry):
        seen_of(c, seen_start)
        spread_seen(c, seen_start)
        return carry

    def first_seen(c, carry):
        seen_of(c, seen_first)
        return carry

    hold(start_now)
    gathered[...] = jnp.zeros(gathered.shape, F32)
    lax.fori_loop(0, chunks, start_pass, 0)
    first_now = collected() + DAMPING * start_now
    hold(first_now)
    gathered[...] = jnp.zeros(gathered.shape, F32)
    lax.fori_loop(0, chunks, first_seen, 0)

    start_start = jnp.sum(start_now * start_now)
    start_first = jnp.sum(start_now * first_now)
    guess = jnp.where(start_first > 0.0, start_start / jnp.where(start_first > 0.0, start_first, 1.0), 0.0)
    rest = start_now - guess * first_now
    rest_rest = jnp.sum(rest * rest)
    rest_first = jnp.sum(rest * first_now)
    first_first = jnp.sum(first_now * first_now)
    from_start, from_first = seen_start[...], seen_first[...]
    from_rest = from_start - guess * from_first
    found = [
        start_start,
        start_first,
        rest_rest,
        rest_first,
        first_first,
        jnp.sum(from_rest * from_rest) + DAMPING * rest_rest,
        jnp.sum(from_rest * from_first) + DAMPING * rest_first,
        jnp.sum(from_first * from_first) + DAMPING * first_first,
        guess,
    ]
    place = iota((1, 128), 1)
    line = jnp.where(place == len(found), over, 0.0)
    for k, value in enumerate(found):
        line = jnp.where(place == k, value, line)
    near[tex] = line
    for step in range(1, owners):
        send(near.at[tex], near, "tex", step, send_near, recv_near)
    spread_seen(0, seen_first)
    wait_all(near, recv_near)
    far[me] = near[...]
    for step in range(1, senders):
        send(near, far, "view", step, send_far, recv_far)
    for c in range(1, chunks):
        spread_seen(c, seen_first)
    second_now = collected() + DAMPING * first_now
    wait_all(far, recv_far)
    table = far[...].reshape(owners * senders, 128)
    column = [table[:, k : k + 1] for k in range(10)]

    def added(values):
        return jnp.sum(values, axis=0, keepdims=True)

    start_start, start_first = added(column[0]), added(column[1])
    one = start_start / start_first
    change = column[8] - one
    norm = added(column[2] + change * (2.0 * column[3] + change * column[4]))
    turn = norm / start_start
    cross = added(column[3] + change * column[4])
    curve = added(column[5] + change * (2.0 * column[6] + change * column[7]))
    curve = curve + 2.0 * turn * cross + turn * turn * start_first
    two = norm / curve
    near_part = one + two * (1.0 + turn)
    update[...] = near_part * start_now - one * two * first_now
    residual[...] = start_now - near_part * first_now + one * two * second_now
    flag[...] = jnp.broadcast_to(added(column[9]), flag.shape)
    wait_all(landed, send_window)
    wait_all(near, send_near)
    wait_all(far, send_far)


def hand_on_kernel(update, residual, update_out, residual_out, sems):
    copies = [
        pltpu.make_async_copy(update, update_out, sems.at[0]),
        pltpu.make_async_copy(residual, residual_out, sems.at[1]),
    ]
    for copy in copies:
        copy.start()
    for copy in copies:
        copy.wait()


def in_vmem(count):
    return [pl.BlockSpec(memory_space=pltpu.VMEM)] * count


def per_device(texel_atlas, observed, geometry, block_ids, pixel_slot, corner, bilinear_frac):
    owners, views = lax.axis_size("tex"), lax.axis_size("view")
    tiles, slots = block_ids.shape[0], block_ids.shape[2]
    half_rows = CHANNELS * BSIDE // 2
    shaped = jax.ShapeDtypeStruct

    update, residual, flag = pl.pallas_call(
        whole_kernel,
        out_shape=(shaped((half_rows, 128), F32),) * 2 + (shaped((1, 128), F32),),
        in_specs=[pl.BlockSpec(memory_space=pltpu.SMEM)] + [pl.BlockSpec(memory_space=pl.ANY)] * 6,
        out_specs=tuple(in_vmem(3)),
        scratch_shapes=[
            pltpu.VMEM((3, tiles, pixel_slot.shape[1]), F32),
            pltpu.VMEM((6, tiles, pixel_slot.shape[1]), F32),
            pltpu.VMEM(bilinear_frac.shape, F32),
            pltpu.VMEM(pixel_slot.shape, jnp.int32),
            pltpu.VMEM(pixel_slot.shape, jnp.int32),
            pltpu.VMEM((half_rows, 128), F32),
            pltpu.VMEM((ROWS, tiles * PICKED), F32),
            pltpu.VMEM((ROWS, SORTED), F32),
            pltpu.VMEM((views, 8, WINDOW * 3 // 2), F32),
            pltpu.VMEM((views, 8, WINDOW * 3 // 2), F32),
            pltpu.VMEM((ROWS, DENSE), F32),
            pltpu.VMEM((2 * half_rows, 256), BF16),
            pltpu.VMEM((DENSE // CHUNK, 4 * BSIDE, CHUNK), BF16),
            pltpu.VMEM((DENSE // CHUNK, BSIDE, CHUNK), F32),
            pltpu.VMEM((CHANNELS, TALL, 128), F32),
            pltpu.VMEM((DENSE // CHUNK, ROWS, TALL, 128), F32),
            pltpu.VMEM((DENSE // CHUNK, 14, TALL, 128), F32),
            pltpu.VMEM((DENSE // CHUNK, 3, TALL, 128), F32),
            pltpu.VMEM((DENSE // CHUNK, 3, TALL, 128), F32),
            pltpu.VMEM((2 * half_rows, 128), F32),
            pltpu.VMEM((owners, 1, 128), F32),
            pltpu.VMEM((views, owners, 1, 128), F32),
        ]
        + [pltpu.SemaphoreType.DMA((6,))]
        + [pltpu.SemaphoreType.DMA] * 6,
        compiler_params=pltpu.CompilerParams(
            collective_id=0, has_side_effects=True, vmem_limit_bytes=56 << 20
        ),
    )(
        block_ids.reshape(tiles, slots).T,
        observed.transpose(1, 0, 2),
        geometry.transpose(1, 0, 2),
        bilinear_frac,
        pixel_slot,
        corner,
        texel_atlas.reshape(half_rows, 128),
    )

    def quick():
        handed = pl.pallas_call(
            hand_on_kernel,
            out_shape=(shaped((half_rows, 128), F32),) * 2,
            in_specs=[pl.BlockSpec(memory_space=pl.ANY)] * 2,
            out_specs=(pl.BlockSpec(memory_space=pl.ANY),) * 2,
            scratch_shapes=[pltpu.SemaphoreType.DMA((2,))],
        )(update, residual)
        return tuple(part.reshape(texel_atlas.shape) for part in handed)

    def general():
        return general_step(
            texel_atlas, observed, geometry, block_ids, pixel_slot, corner, bilinear_frac
        )

    return lax.cond(flag[0, 0] > 0.0, general, quick)


def solution(mesh):
    in_specs = (
        P(("tex", "view"), None, None),
        P("view", None, None),
        P("view", None, None),
        P("view", "tex", None),
        P("view", None),
        P("view", None),
        P("view", None, None),
    )
    out_specs = (P(("tex", "view"), None, None), P(("tex", "view"), None, None))
    return jax.shard_map(
        per_device, mesh=mesh, in_specs=in_specs, out_specs=out_specs, check_vma=False
    )
```

```python
import functools
import math

import jax
import jax.numpy as jnp
from jax import lax
from jax.experimental import pallas as pl
from jax.experimental.pallas import tpu as pltpu
from jax.sharding import PartitionSpec as P

BSIDE = 64
ITERS = 2


DAMPING = 0.1


def passed_on(values, axis):
    count = lax.axis_size(axis)
    return lax.ppermute(values, axis, [(k, (k + 1) % count) for k in range(count)])


def ring_gather(values, axis):
    count, me = lax.axis_size(axis), lax.axis_index(axis)

    def step(s, state):
        held, block = state
        block = passed_on(block, axis)
        return held.at[lax.rem(me - s + count, count)].set(block), block

    held = jnp.zeros((count,) + values.shape, values.dtype).at[me].set(values)
    return lax.fori_loop(1, count, step, (held, values))[0]


def ring_sum_scatter(values, axis):
    count, me = lax.axis_size(axis), lax.axis_index(axis)

    def step(s, total):
        return passed_on(total, axis) + values[lax.rem(me - 1 - s + 2 * count, count)]

    return lax.fori_loop(1, count, step, values[lax.rem(me - 1 + count, count)])


def grouped_by(values, count):
    return values.reshape((count, values.shape[0] // count) + values.shape[1:])


def shade(params, geometry):
    albedo = params[:, 0:3]
    specular = params[:, 3:6]
    roughness = params[:, 6]
    tilt_x = params[:, 7]
    tilt_y = params[:, 8]
    occlusion = params[:, 9]
    inverse_len = lax.rsqrt(1.0 + tilt_x * tilt_x + tilt_y * tilt_y)
    normal_x = tilt_x * inverse_len
    normal_y = tilt_y * inverse_len
    light_dir = geometry[:, 0:3]
    viewer = geometry[:, 3:6]
    halfway = light_dir + viewer
    halfway = halfway * lax.rsqrt(jnp.sum(halfway * halfway, axis=1, keepdims=True))

    def facing(vector):
        return normal_x * vector[:, 0] + normal_y * vector[:, 1] + inverse_len * vector[:, 2]

    cosine_light = facing(light_dir)
    cosine_view = facing(viewer)
    cosine_half = facing(halfway)
    view_half = jnp.sum(viewer * halfway, axis=1)
    rough_square = roughness * roughness
    rough_fourth = rough_square * rough_square
    denominator = cosine_half * cosine_half * (rough_fourth - 1.0) + 1.0
    distribution = rough_fourth / (math.pi * denominator * denominator)
    smith_k = 0.5 * rough_square
    masking = cosine_light / (cosine_light * (1.0 - smith_k) + smith_k)
    masking = masking * cosine_view / (cosine_view * (1.0 - smith_k) + smith_k)
    fresnel = specular + (1.0 - specular) * ((1.0 - view_half) ** 5)[:, None]
    reflected = (distribution * masking / (4.0 * cosine_light * cosine_view))[:, None] * fresnel
    return (occlusion * cosine_light)[:, None] * (albedo + math.pi * reflected)


def tables(slot_part, corner_part, frac_part, owner_index, slots):
    in_range = slot_part // slots == owner_index
    slot_within = slot_part % slots
    row_start = corner_part // (BSIDE - 1)
    column_start = corner_part % (BSIDE - 1)
    across = frac_part[:, 0]
    frac_down = frac_part[:, 1]
    positions = jnp.arange(BSIDE, dtype=jnp.int32)[None, :, None]
    column_weight = jnp.where(positions == column_start[:, None], (1.0 - across)[:, None], 0.0)
    column_weight = column_weight + jnp.where(
        positions == column_start[:, None] + 1, across[:, None], 0.0
    )
    row_part = jnp.where(positions == row_start[:, None], (1.0 - frac_down)[:, None], 0.0)
    row_part = row_part + jnp.where(positions == row_start[:, None] + 1, frac_down[:, None], 0.0)
    picked = (jnp.arange(slots, dtype=jnp.int32)[None, :, None] == slot_within[:, None]) & in_range[
        :, None
    ]
    row_weight = jnp.where(picked[:, :, None], row_part[:, None], 0.0)
    return (row_weight, column_weight)


def general_step(texel_atlas, observed, geometry, block_ids, pixel_slot, corner, bilinear_frac):
    tex_count = lax.axis_size("tex")
    owner_index = lax.axis_index("tex")
    own_blocks, channels, texels = texel_atlas.shape
    tiles_all = observed.shape[0]
    tiles_own = tiles_all // tex_count
    slots = block_ids.shape[2]
    groups = tiles_all // tex_count
    slot_blocks = block_ids[:, 0, :]
    slot_list = slot_blocks.reshape(-1)
    exact_mode = lax.Precision.HIGHEST

    def grouped(source):
        return source.reshape((groups, tex_count) + source.shape[1:])

    pixel_tables = (grouped(pixel_slot), grouped(corner), grouped(bilinear_frac))

    def widen(own_shard):
        return ring_gather(own_shard, "view").reshape((-1,) + own_shard.shape[1:])

    def pixels_of(whole_range):
        ranged = whole_range.shape[0]
        named = jnp.arange(ranged, dtype=jnp.int32)
        chooser = (jnp.clip(slot_list, 0, ranged - 1)[:, None] == named[None, :]).astype(jnp.float32)
        fetched = jnp.dot(chooser, whole_range.reshape(ranged, -1), precision=exact_mode)
        fetched = fetched.reshape(tiles_all, slots, channels, texels)

        def pixels_one_group(members):
            blocks, slot_part, corner_part, frac_part = members
            row_weight, column_weight = tables(
                slot_part, corner_part, frac_part, owner_index, slots
            )
            values = blocks.reshape(blocks.shape[0], slots, channels, BSIDE, BSIDE)
            middle = jnp.einsum("tjcyx,tjyp->tcxp", values, row_weight, precision=exact_mode)
            return jnp.sum(middle * column_weight[:, None], axis=2)

        partial_value = lax.map(pixels_one_group, (grouped(fetched),) + pixel_tables)
        partial_value = partial_value.reshape((tiles_all,) + partial_value.shape[2:])
        return ring_sum_scatter(grouped_by(partial_value, tex_count), "tex")

    def texel_terms(cotangent):
        gathered = ring_gather(cotangent, "tex").reshape((-1,) + cotangent.shape[1:])

        def texel_one_group(members):
            back_part, slot_part, corner_part, frac_part = members
            row_weight, column_weight = tables(
                slot_part, corner_part, frac_part, owner_index, slots
            )
            middle = back_part[:, :, None, :] * column_weight[:, None]
            values = jnp.einsum("tcxp,tjyp->tjcyx", middle, row_weight, precision=exact_mode)
            return values.reshape(values.shape[0] * slots, channels * texels)

        terms = lax.map(texel_one_group, (grouped(gathered),) + pixel_tables)
        return terms.reshape(tiles_all * slots, channels * texels)

    def owner_sums(terms):
        row_count = lax.axis_size("view") * own_blocks
        wanted = jnp.arange(row_count, dtype=jnp.int32)
        selector = (slot_list[None, :] == wanted[:, None]).astype(jnp.float32)
        summed = jnp.dot(selector, terms, precision=exact_mode, preferred_element_type=jnp.float32)
        return ring_sum_scatter(
            summed.reshape(row_count // own_blocks, own_blocks, channels, texels), "view"
        )

    atlas_range = widen(texel_atlas)
    base_params = pixels_of(atlas_range)
    geometry_own = lax.dynamic_slice_in_dim(geometry, owner_index * tiles_own, tiles_own, 0)
    observed_own = lax.dynamic_slice_in_dim(observed, owner_index * tiles_own, tiles_own, 0)

    def render(params):
        return shade(params, geometry_own)

    colors, backward = jax.vjp(render, base_params)

    def pullback(cotangent):
        return backward(cotangent)[0]

    unused, pushed = jax.vjp(pullback, jnp.zeros_like(colors))
    first_terms = texel_terms(backward(colors - observed_own)[0])
    gradient = owner_sums(first_terms)

    def inner_sums(values):
        return (jnp.sum(ring_gather(jnp.sum(ring_gather(values[0], "tex")), "view")),)

    update = jnp.zeros_like(gradient)
    residual = -gradient
    direction = residual
    norm_now = inner_sums((jnp.sum(residual * residual),))[0]
    for iteration in range(ITERS):
        applied = (
            owner_sums(texel_terms(backward(pushed(pixels_of(widen(direction)))[0])[0]))
            + DAMPING * direction
        )
        step_size = norm_now / inner_sums((jnp.sum(direction * applied),))[0]
        update = update + step_size * direction
        residual = residual - step_size * applied
        norm_next = inner_sums((jnp.sum(residual * residual),))[0]
        direction = residual + norm_next / norm_now * direction
        norm_now = norm_next
    return (update, residual)


MESH = pl.DeviceIdType.MESH
F32 = jnp.float32
BF16 = jnp.bfloat16
CHANNELS = 10
ROWS = 16
WINDOW = 512
PICKED = 256
SORTED = 1024
CHUNK = 896
TALL = CHUNK // 128
DENSE = 1792
NT = (((1,), (1,)), ((), ()))


def halves(values):
    high = values.astype(BF16)
    low = (values - high.astype(F32)).astype(BF16)
    return high, low


def iota(shape, axis):
    return lax.broadcasted_iota(jnp.int32, shape, axis)


def pack(ids, obs, geo, frac, slot, corner, picked, ordered):
    tiles, pixels = slot.shape
    slots = ids.shape[0]
    blocks = lax.axis_size("view")
    owner = lax.axis_index("tex")
    lanes = pixels // 128

    slot_now = slot[...]
    corner_now = corner[...].astype(F32)
    tile_of = iota((tiles, 128), 0)
    target = jnp.zeros((tiles, pixels), jnp.int32)
    for s in range(slots):
        named = jnp.zeros((tiles, 128), jnp.int32)
        for t in range(tiles):
            named = jnp.where(tile_of == t, ids[s, t] + 1, named)
        target = jnp.where(
            slot_now == owner * slots + s, jnp.concatenate([named] * lanes, axis=1), target
        )
    mine = jnp.where(target > 0, 1.0, 0.0)
    before = jnp.where(iota((128, 128), 0) < iota((128, 128), 1), 1.0, 0.0).astype(BF16)

    stacked = jnp.concatenate([mine[:, c * 128 : c * 128 + 128] for c in range(lanes)], axis=0)
    ahead = jnp.dot(stacked.astype(BF16), before, preferred_element_type=F32)
    base = jnp.zeros((tiles, 1), F32)
    places = []
    for c in range(lanes):
        places.append(ahead[c * tiles : c * tiles + tiles] + base)
        base = base + jnp.sum(mine[:, c * 128 : c * 128 + 128], axis=1, keepdims=True)
    place = jnp.where(target > 0, jnp.concatenate(places, axis=1), -1.0).astype(jnp.int32)
    over = jnp.max(jnp.where(base > PICKED, 1.0, 0.0))
    total = jnp.sum(base)
    over = jnp.maximum(over, jnp.where(total > SORTED, 1.0, 0.0))

    target_f = target.astype(F32)
    wanted = iota((PICKED, pixels), 0)
    for t in range(tiles):
        numbers = jnp.concatenate(
            [
                obs[:, t, :],
                geo[:, t, :],
                frac[t],
                corner_now[t : t + 1],
                target_f[t : t + 1],
                jnp.zeros((3, pixels), F32),
            ],
            axis=0,
        )
        both = jnp.concatenate(halves(numbers), axis=0)
        hot = jnp.where(wanted == place[t : t + 1], 1.0, 0.0).astype(BF16)
        got = lax.dot_general(both, hot, NT, preferred_element_type=F32)
        picked[:, t * PICKED : t * PICKED + PICKED] = got[:ROWS] + got[ROWS:]

    listed = tiles * PICKED
    groups = listed // 128
    target_row = picked[12:13, :]
    member = jnp.where(
        iota((blocks, listed), 0).astype(F32) + 1.0 == target_row, 1.0, 0.0
    )
    stacked = jnp.concatenate([member[:, c * 128 : c * 128 + 128] for c in range(groups)], axis=0)
    ahead = jnp.dot(stacked.astype(BF16), before, preferred_element_type=F32)
    base = jnp.zeros((blocks, 1), F32)
    places = []
    for c in range(groups):
        places.append(ahead[c * blocks : c * blocks + blocks] + base)
        base = base + jnp.sum(member[:, c * 128 : c * 128 + 128], axis=1, keepdims=True)
    over = jnp.maximum(over, jnp.max(jnp.where(base > WINDOW, 1.0, 0.0)))
    earlier = jnp.where(iota((blocks, blocks), 1) < iota((blocks, blocks), 0), 1.0, 0.0)
    first = jnp.dot(
        earlier,
        jnp.broadcast_to(base, (blocks, 128)),
        precision=lax.Precision.HIGHEST,
        preferred_element_type=F32,
    )
    place = jnp.concatenate(places, axis=1) + first[:, 0:1]
    place = jnp.sum(member * place, axis=0, keepdims=True)
    place = jnp.where(target_row > 0.0, place, -1.0).astype(jnp.int32)
    both = jnp.concatenate(halves(picked[...]), axis=0)
    for q in range(SORTED // 256):
        hot = jnp.where(iota((256, listed), 0) + q * 256 == place, 1.0, 0.0).astype(BF16)
        got = lax.dot_general(both, hot, NT, preferred_element_type=F32)
        ordered[:, q * 256 : q * 256 + 256] = got[:ROWS] + got[ROWS:]

    return over, first, jnp.broadcast_to(base, (blocks, 128))


def folded(listed, turn, size):
    window = pltpu.roll(listed, turn, axis=1)[:, :WINDOW]
    top, low = window[:8], window[8:]
    place = iota((8, WINDOW), 0)
    low = jnp.where((place == 3) & (iota((8, WINDOW), 1).astype(F32) >= size), -1.0, low)
    raised = pltpu.roll(low, 4, axis=0)
    pairs = []
    for g in range(0, WINDOW, 256):
        pairs.append(jnp.where(place[:, :128] < 4, low[:, g : g + 128], raised[:, g + 128 : g + 256]))
    return jnp.concatenate([top] + pairs, axis=1)


def unfolded(window):
    low = []
    for g in range(WINDOW, window.shape[1], 128):
        pair = window[:, g : g + 128]
        low += [pair, pltpu.roll(pair, 4, axis=0)]
    return jnp.concatenate([window[:, :WINDOW], jnp.concatenate(low, axis=1)], axis=0)


def greet(barrier, tex, view, owners, views):
    for step in range(1, views):
        peer = lax.rem(view + step, views)
        pl.semaphore_signal(barrier, inc=1, device_id=(tex, peer), device_id_type=MESH)
    for step in range(1, owners):
        peer = lax.rem(tex + step, owners)
        pl.semaphore_signal(barrier, inc=1, device_id=(peer, view), device_id_type=MESH)


def send(source, target, axis, step, send_sem, recv_sem):
    count, me = lax.axis_size(axis), lax.axis_index(axis)
    peer = lax.rem(me + step, count)
    pltpu.make_async_remote_copy(
        src_ref=source,
        dst_ref=target.at[me],
        send_sem=send_sem,
        recv_sem=recv_sem,
        device_id={axis: peer},
        device_id_type=MESH,
    ).start()


def wait_all(target, sem):
    others = target.at[pl.ds(0, target.shape[0] - 1)]
    pltpu.make_async_copy(others, others, sem).wait()


def optics(params, geometry):
    roughness, tilt_x, tilt_y, occlusion = params[6], params[7], params[8], params[9]
    light, viewer = geometry[0:3], geometry[3:6]
    inverse_len = lax.rsqrt(1.0 + tilt_x * tilt_x + tilt_y * tilt_y)
    normal_x = tilt_x * inverse_len
    normal_y = tilt_y * inverse_len
    half = [a + b for a, b in zip(light, viewer)]
    scale = lax.rsqrt(half[0] * half[0] + half[1] * half[1] + half[2] * half[2])
    half = [a * scale for a in half]

    def facing(vector):
        cosine = normal_x * vector[0] + normal_y * vector[1] + inverse_len * vector[2]
        along_x = inverse_len * (vector[0] - normal_x * cosine)
        along_y = inverse_len * (vector[1] - normal_y * cosine)
        return cosine, along_x, along_y

    light_c, light_x, light_y = facing(light)
    view_c, view_x, view_y = facing(viewer)
    half_c, half_x, half_y = facing(half)
    miss = 1.0 - (viewer[0] * half[0] + viewer[1] * half[1] + viewer[2] * half[2])
    fifth = miss * miss
    fifth = fifth * fifth * miss
    square = roughness * roughness
    fourth = square * square
    inverse_d = 1.0 / (half_c * half_c * (fourth - 1.0) + 1.0)
    smith = 0.5 * square
    inverse_l = 1.0 / (light_c * (1.0 - smith) + smith)
    inverse_v = 1.0 / (view_c * (1.0 - smith) + smith)
    shape = 0.25 * inverse_d * inverse_d * inverse_l * inverse_v
    gloss = fourth * shape
    shape_slope = -4.0 * square * half_c * half_c * inverse_d
    shape_slope = shape_slope - 0.5 * (1.0 - light_c) * inverse_l - 0.5 * (1.0 - view_c) * inverse_v
    gloss_square = 2.0 * square * shape + gloss * shape_slope
    gloss_half = -4.0 * gloss * half_c * (fourth - 1.0) * inverse_d
    gloss_light = -gloss * (1.0 - smith) * inverse_l
    gloss_view = -gloss * (1.0 - smith) * inverse_v
    gloss_x = gloss_half * half_x + gloss_light * light_x + gloss_view * view_x
    gloss_y = gloss_half * half_y + gloss_light * light_y + gloss_view * view_y
    lit = occlusion * light_c
    fresnel = [params[3 + c] + (1.0 - params[3 + c]) * fifth for c in range(3)]
    total = [params[c] + gloss * fresnel[c] for c in range(3)]
    factors = [
        lit,
        lit * gloss * (1.0 - fifth),
        lit * gloss_square * 2.0 * roughness,
        occlusion * light_x,
        lit * gloss_x,
        occlusion * light_y,
        lit * gloss_y,
        light_c,
    ]
    return factors + total + fresnel, [lit * t for t in total]


def push(tangent, factors):
    albedo, specular, rough, ex, fx, ey, fy, shine = factors[:8]
    total, fresnel = factors[8:11], factors[11:14]
    on_total = ex * tangent[7] + ey * tangent[8] + shine * tangent[9]
    on_fresnel = rough * tangent[6] + fx * tangent[7] + fy * tangent[8]
    return [
        albedo * tangent[c] + specular * tangent[3 + c] + total[c] * on_total + fresnel[c] * on_fresnel
        for c in range(3)
    ]


def pull(colors, factors):
    albedo, specular, rough, ex, fx, ey, fy, shine = factors[:8]
    total, fresnel = factors[8:11], factors[11:14]
    e = total[0] * colors[0] + total[1] * colors[1] + total[2] * colors[2]
    f = fresnel[0] * colors[0] + fresnel[1] * colors[1] + fresnel[2] * colors[2]
    return (
        [albedo * c for c in colors]
        + [specular * c for c in colors]
        + [rough * f, ex * e + fx * f, ey * e + fy * f, shine * e]
    )


def whole_kernel(
    ids, obs_in, geo_in, frac_in, slot_in, corner_in, atlas_in, update, residual, flag,
    obs, geo, frac, slot, corner, atlas, picked, ordered, windows, landed, pixels, field,
    across, down, turned, stood, slopes, seen_start, seen_first, gathered, near, far,
    read_sems, send_window, recv_window, send_near, recv_near, send_far, recv_far,
):
    tex, me = lax.axis_index("tex"), lax.axis_index("view")
    senders, owners = landed.shape[0], near.shape[0]
    half_rows = CHANNELS * BSIDE // 2
    lane = iota((half_rows, 128), 1)
    reads = [
        pltpu.make_async_copy(source, target, read_sems.at[k])
        for k, (source, target) in enumerate(
            [
                (slot_in, slot),
                (corner_in, corner),
                (obs_in, obs),
                (geo_in, geo),
                (frac_in, frac),
                (atlas_in, atlas),
            ]
        )
    ]
    for read in reads:
        read.start()
    barrier = pltpu.get_barrier_semaphore()
    greet(barrier, tex, me, owners, senders)
    for read in reads:
        read.wait()
    over, first, sizes = pack(ids, obs, geo, frac, slot, corner, picked, ordered)
    turns = jnp.where(first > 0.0, jnp.maximum(float(SORTED) - first, 0.0), 0.0).astype(jnp.int32)
    deep = math.isqrt(senders)
    up, side = me // deep, lax.rem(me, deep)
    listed = ordered[...]
    pl.semaphore_wait(barrier, owners + senders - 2)

    def window_for(peer):
        named = iota(turns.shape, 0) == peer
        turn = jnp.sum(jnp.where(named, turns, 0)[:, 0:1])
        size = jnp.sum(jnp.where(named, sizes, 0.0)[:, 0:1], axis=0, keepdims=True)
        return folded(listed, turn, size)

    apart = [(min(a, deep - a) + min(b, deep - b), a, b) for a in range(deep) for b in range(deep)]
    for _, a, b in sorted(apart, reverse=True)[:-1]:
        step = a * deep + b
        peer = lax.rem(up + a, deep) * deep + lax.rem(side + b, deep)
        windows[step] = window_for(peer)
        pltpu.make_async_remote_copy(
            src_ref=windows.at[step],
            dst_ref=landed.at[me],
            send_sem=send_window,
            recv_sem=recv_window,
            device_id=(tex, peer),
            device_id_type=MESH,
        ).start()
    landed[me] = window_for(me)


    def hold(values):
        high, low = halves(values)
        high, low = high.astype(F32), low.astype(F32)
        left = jnp.where(lane < BSIDE, high, pltpu.roll(low, BSIDE, axis=1)).astype(BF16)
        right = jnp.where(lane < BSIDE, pltpu.roll(high, BSIDE, axis=1), low).astype(BF16)
        field[:half_rows, :128] = left
        field[:half_rows, 128:] = left
        field[half_rows:, :128] = right
        field[half_rows:, 128:] = right

    def sample(c, rows):
        seen = jnp.dot(field[...], across[c], preferred_element_type=F32)
        seen = seen.reshape(2, CHANNELS, BSIDE // 2, CHUNK) * rows
        seen = jnp.sum(seen[0] + seen[1], axis=1)
        for j in range(TALL):
            turned[2 * c, :, j, :] = seen[:, j * 128 : j * 128 + 128]
        return [turned[2 * c, k] for k in range(CHANNELS)]

    def spread(c, rows, back):
        for k in range(CHANNELS):
            turned[2 * c + 1, k] = back[k]
        back = jnp.concatenate([turned[2 * c + 1, :, j, :] for j in range(TALL)], axis=1)
        terms = (back.reshape(1, CHANNELS, 1, CHUNK) * rows).reshape(2 * half_rows, CHUNK)
        high, low = halves(terms)
        columns = across[c, BSIDE : 3 * BSIDE, :]
        gathered[...] += lax.dot_general(high, columns, NT, preferred_element_type=F32)
        gathered[...] += lax.dot_general(low, columns, NT, preferred_element_type=F32)

    def collected():
        left, right = gathered[:half_rows], gathered[half_rows:]
        left = left + pltpu.roll(left, BSIDE, axis=1)
        right = right + pltpu.roll(right, BSIDE, axis=1)
        return jnp.where(lane < BSIDE, left, right)

    hold(atlas[...])
    gathered[...] = jnp.zeros(gathered.shape, F32)
    wait_all(landed, recv_window)
    arrived = [unfolded(landed[j]) for j in range(senders)]
    live = [jnp.where(window[11:12] >= 0.0, 1.0, 0.0) for window in arrived]
    counts = jnp.sum(jnp.concatenate(live, axis=0), axis=1, keepdims=True)
    earlier = jnp.where(iota((senders, senders), 1) < iota((senders, senders), 0), 1.0, 0.0)
    begins = jnp.dot(
        earlier,
        jnp.broadcast_to(counts, (senders, 128)),
        precision=lax.Precision.HIGHEST,
        preferred_element_type=F32,
    )
    begins = jnp.minimum(begins, float(DENSE - 1)).astype(jnp.int32)
    dense = jnp.zeros((ROWS, DENSE), F32)
    for j in range(senders):
        window = jnp.where(live[j] > 0.0, arrived[j], 0.0)
        window = jnp.concatenate([window, jnp.zeros((ROWS, DENSE - WINDOW), F32)], axis=1)
        dense = dense + pltpu.roll(window, begins[j, 0], axis=1)
    pixels[...] = dense
    for c in range(DENSE // CHUNK):
        for j in range(TALL):
            at = c * CHUNK + j * 128
            stood[c, :, j, :] = dense[:, at : at + 128]
    count = jnp.sum(counts)
    over = jnp.maximum(over, jnp.where(count > DENSE, 1.0, 0.0))
    chunks = DENSE // CHUNK

    def first_pass(c):
        numbers = pixels[:, c * CHUNK : c * CHUNK + CHUNK]
        numbers = [numbers[k : k + 1] for k in range(ROWS)]
        used = (iota((1, CHUNK), 1) + c * CHUNK).astype(F32) < count
        frac_x, frac_y, spot = numbers[9:12]
        row = jnp.floor((spot + 0.5) * (1.0 / (BSIDE - 1)))
        column = spot - row * (BSIDE - 1)
        at = iota((BSIDE, CHUNK), 0).astype(F32)
        weight = jnp.where(at == column, 1.0 - frac_x, jnp.where(at == column + 1.0, frac_x, 0.0))
        high, low = halves(weight)
        across[c] = jnp.concatenate([high, high, low, low], axis=0)
        at = iota((BSIDE, CHUNK), 0)
        at = jnp.where(at < BSIDE // 2, 2 * at, 2 * at - (BSIDE - 1)).astype(F32)
        weight = jnp.where(at == row, 1.0 - frac_y, jnp.where(at == row + 1.0, frac_y, 0.0))
        weight = jnp.where(used, weight, 0.0)
        down[c] = weight
        rows = weight.reshape(2, 1, BSIDE // 2, CHUNK)
        standing = [stood[c, k] for k in range(9)]
        factors, colors = optics(sample(c, rows), standing[3:9])
        place = iota((TALL, 128), 0) * 128 + iota((TALL, 128), 1) + c * CHUNK
        used = place.astype(F32) < count
        factors = [jnp.where(used, factor, 0.0) for factor in factors]
        for k, factor in enumerate(factors):
            slopes[c, k] = factor
        errors = [jnp.where(used, a - b, 0.0) for a, b in zip(colors, standing[0:3])]
        spread(c, rows, pull(errors, factors))

    for c in range(chunks):
        first_pass(c)
    start_now = -collected()

    def factors_of(c):
        return [slopes[c, k] for k in range(14)]

    def seen_of(c, kept):
        rows = down[c].reshape(2, 1, BSIDE // 2, CHUNK)
        colors = push(sample(c, rows), factors_of(c))
        for k in range(3):
            kept[c, k] = colors[k]

    def spread_seen(c, kept):
        rows = down[c].reshape(2, 1, BSIDE // 2, CHUNK)
        spread(c, rows, pull([kept[c, k] for k in range(3)], factors_of(c)))

    def start_pass(c):
        seen_of(c, seen_start)
        spread_seen(c, seen_start)

    def first_seen(c):
        seen_of(c, seen_first)

    hold(start_now)
    gathered[...] = jnp.zeros(gathered.shape, F32)
    for c in range(chunks):
        start_pass(c)
    first_now = collected() + DAMPING * start_now
    hold(first_now)
    gathered[...] = jnp.zeros(gathered.shape, F32)
    for c in range(chunks):
        first_seen(c)

    start_start = jnp.sum(start_now * start_now)
    start_first = jnp.sum(start_now * first_now)
    guess = jnp.where(start_first > 0.0, start_start / jnp.where(start_first > 0.0, start_first, 1.0), 0.0)
    rest = start_now - guess * first_now
    rest_rest = jnp.sum(rest * rest)
    rest_first = jnp.sum(rest * first_now)
    first_first = jnp.sum(first_now * first_now)
    from_start, from_first = seen_start[...], seen_first[...]
    from_rest = from_start - guess * from_first
    found = [
        start_start,
        start_first,
        rest_rest,
        rest_first,
        first_first,
        jnp.sum(from_rest * from_rest) + DAMPING * rest_rest,
        jnp.sum(from_rest * from_first) + DAMPING * rest_first,
        jnp.sum(from_first * from_first) + DAMPING * first_first,
        guess,
    ]
    place = iota((1, 128), 1)
    line = jnp.where(place == len(found), over, 0.0)
    for k, value in enumerate(found):
        line = jnp.where(place == k, value, line)
    near[tex] = line
    for step in range(1, owners):
        send(near.at[tex], near, "tex", step, send_near, recv_near)
    spread_seen(0, seen_first)
    wait_all(near, recv_near)
    far[me] = near[...]
    for step in range(1, senders):
        send(near, far, "view", step, send_far, recv_far)
    for c in range(1, chunks):
        spread_seen(c, seen_first)
    second_now = collected() + DAMPING * first_now
    wait_all(far, recv_far)
    table = far[...].reshape(owners * senders, 128)
    column = [table[:, k : k + 1] for k in range(10)]

    def added(values):
        return jnp.sum(values, axis=0, keepdims=True)

    start_start, start_first = added(column[0]), added(column[1])
    one = start_start / start_first
    change = column[8] - one
    norm = added(column[2] + change * (2.0 * column[3] + change * column[4]))
    turn = norm / start_start
    cross = added(column[3] + change * column[4])
    curve = added(column[5] + change * (2.0 * column[6] + change * column[7]))
    curve = curve + 2.0 * turn * cross + turn * turn * start_first
    two = norm / curve
    near_part = one + two * (1.0 + turn)
    update[...] = near_part * start_now - one * two * first_now
    residual[...] = start_now - near_part * first_now + one * two * second_now
    flag[...] = jnp.broadcast_to(added(column[9]), flag.shape)
    wait_all(landed, send_window)
    wait_all(near, send_near)
    wait_all(far, send_far)


def hand_on_kernel(update, residual, update_out, residual_out, sems):
    copies = [
        pltpu.make_async_copy(update, update_out, sems.at[0]),
        pltpu.make_async_copy(residual, residual_out, sems.at[1]),
    ]
    for copy in copies:
        copy.start()
    for copy in copies:
        copy.wait()


def in_vmem(count):
    return [pl.BlockSpec(memory_space=pltpu.VMEM)] * count


def per_device(texel_atlas, observed, geometry, block_ids, pixel_slot, corner, bilinear_frac):
    owners, views = lax.axis_size("tex"), lax.axis_size("view")
    tiles, slots = block_ids.shape[0], block_ids.shape[2]
    half_rows = CHANNELS * BSIDE // 2
    shaped = jax.ShapeDtypeStruct

    update, residual, flag = pl.pallas_call(
        whole_kernel,
        out_shape=(shaped((half_rows, 128), F32),) * 2 + (shaped((1, 128), F32),),
        in_specs=[pl.BlockSpec(memory_space=pltpu.SMEM)] + [pl.BlockSpec(memory_space=pl.ANY)] * 6,
        out_specs=tuple(in_vmem(3)),
        scratch_shapes=[
            pltpu.VMEM((3, tiles, pixel_slot.shape[1]), F32),
            pltpu.VMEM((6, tiles, pixel_slot.shape[1]), F32),
            pltpu.VMEM(bilinear_frac.shape, F32),
            pltpu.VMEM(pixel_slot.shape, jnp.int32),
            pltpu.VMEM(pixel_slot.shape, jnp.int32),
            pltpu.VMEM((half_rows, 128), F32),
            pltpu.VMEM((ROWS, tiles * PICKED), F32),
            pltpu.VMEM((ROWS, SORTED), F32),
            pltpu.VMEM((views, 8, WINDOW * 3 // 2), F32),
            pltpu.VMEM((views, 8, WINDOW * 3 // 2), F32),
            pltpu.VMEM((ROWS, DENSE), F32),
            pltpu.VMEM((2 * half_rows, 256), BF16),
            pltpu.VMEM((DENSE // CHUNK, 4 * BSIDE, CHUNK), BF16),
            pltpu.VMEM((DENSE // CHUNK, BSIDE, CHUNK), F32),
            pltpu.VMEM((2 * DENSE // CHUNK, CHANNELS, TALL, 128), F32),
            pltpu.VMEM((DENSE // CHUNK, ROWS, TALL, 128), F32),
            pltpu.VMEM((DENSE // CHUNK, 14, TALL, 128), F32),
            pltpu.VMEM((DENSE // CHUNK, 3, TALL, 128), F32),
            pltpu.VMEM((DENSE // CHUNK, 3, TALL, 128), F32),
            pltpu.VMEM((2 * half_rows, 128), F32),
            pltpu.VMEM((owners, 1, 128), F32),
            pltpu.VMEM((views, owners, 1, 128), F32),
        ]
        + [pltpu.SemaphoreType.DMA((6,))]
        + [pltpu.SemaphoreType.DMA] * 6,
        compiler_params=pltpu.CompilerParams(
            collective_id=0, has_side_effects=True, vmem_limit_bytes=56 << 20
        ),
    )(
        block_ids.reshape(tiles, slots).T,
        observed.transpose(1, 0, 2),
        geometry.transpose(1, 0, 2),
        bilinear_frac,
        pixel_slot,
        corner,
        texel_atlas.reshape(half_rows, 128),
    )

    def quick():
        handed = pl.pallas_call(
            hand_on_kernel,
            out_shape=(shaped((half_rows, 128), F32),) * 2,
            in_specs=[pl.BlockSpec(memory_space=pl.ANY)] * 2,
            out_specs=(pl.BlockSpec(memory_space=pl.ANY),) * 2,
            scratch_shapes=[pltpu.SemaphoreType.DMA((2,))],
        )(update, residual)
        return tuple(part.reshape(texel_atlas.shape) for part in handed)

    def general():
        return general_step(
            texel_atlas, observed, geometry, block_ids, pixel_slot, corner, bilinear_frac
        )

    return lax.cond(flag[0, 0] > 0.0, general, quick)


def solution(mesh):
    in_specs = (
        P(("tex", "view"), None, None),
        P("view", None, None),
        P("view", None, None),
        P("view", "tex", None),
        P("view", None),
        P("view", None),
        P("view", None, None),
    )
    out_specs = (P(("tex", "view"), None, None), P(("tex", "view"), None, None))
    return jax.shard_map(
        per_device, mesh=mesh, in_specs=in_specs, out_specs=out_specs, check_vma=False
    )
```

```python
import functools
import math

import jax
import jax.numpy as jnp
from jax import lax
from jax.experimental import pallas as pl
from jax.experimental.pallas import tpu as pltpu
from jax.sharding import PartitionSpec as P

BSIDE = 64
ITERS = 2


DAMPING = 0.1


def passed_on(values, axis):
    count = lax.axis_size(axis)
    return lax.ppermute(values, axis, [(k, (k + 1) % count) for k in range(count)])


def ring_gather(values, axis):
    count, me = lax.axis_size(axis), lax.axis_index(axis)

    def step(s, state):
        held, block = state
        block = passed_on(block, axis)
        return held.at[lax.rem(me - s + count, count)].set(block), block

    held = jnp.zeros((count,) + values.shape, values.dtype).at[me].set(values)
    return lax.fori_loop(1, count, step, (held, values))[0]


def ring_sum_scatter(values, axis):
    count, me = lax.axis_size(axis), lax.axis_index(axis)

    def step(s, total):
        return passed_on(total, axis) + values[lax.rem(me - 1 - s + 2 * count, count)]

    return lax.fori_loop(1, count, step, values[lax.rem(me - 1 + count, count)])


def grouped_by(values, count):
    return values.reshape((count, values.shape[0] // count) + values.shape[1:])


def shade(params, geometry):
    albedo = params[:, 0:3]
    specular = params[:, 3:6]
    roughness = params[:, 6]
    tilt_x = params[:, 7]
    tilt_y = params[:, 8]
    occlusion = params[:, 9]
    inverse_len = lax.rsqrt(1.0 + tilt_x * tilt_x + tilt_y * tilt_y)
    normal_x = tilt_x * inverse_len
    normal_y = tilt_y * inverse_len
    light_dir = geometry[:, 0:3]
    viewer = geometry[:, 3:6]
    halfway = light_dir + viewer
    halfway = halfway * lax.rsqrt(jnp.sum(halfway * halfway, axis=1, keepdims=True))

    def facing(vector):
        return normal_x * vector[:, 0] + normal_y * vector[:, 1] + inverse_len * vector[:, 2]

    cosine_light = facing(light_dir)
    cosine_view = facing(viewer)
    cosine_half = facing(halfway)
    view_half = jnp.sum(viewer * halfway, axis=1)
    rough_square = roughness * roughness
    rough_fourth = rough_square * rough_square
    denominator = cosine_half * cosine_half * (rough_fourth - 1.0) + 1.0
    distribution = rough_fourth / (math.pi * denominator * denominator)
    smith_k = 0.5 * rough_square
    masking = cosine_light / (cosine_light * (1.0 - smith_k) + smith_k)
    masking = masking * cosine_view / (cosine_view * (1.0 - smith_k) + smith_k)
    fresnel = specular + (1.0 - specular) * ((1.0 - view_half) ** 5)[:, None]
    reflected = (distribution * masking / (4.0 * cosine_light * cosine_view))[:, None] * fresnel
    return (occlusion * cosine_light)[:, None] * (albedo + math.pi * reflected)


def tables(slot_part, corner_part, frac_part, owner_index, slots):
    in_range = slot_part // slots == owner_index
    slot_within = slot_part % slots
    row_start = corner_part // (BSIDE - 1)
    column_start = corner_part % (BSIDE - 1)
    across = frac_part[:, 0]
    frac_down = frac_part[:, 1]
    positions = jnp.arange(BSIDE, dtype=jnp.int32)[None, :, None]
    column_weight = jnp.where(positions == column_start[:, None], (1.0 - across)[:, None], 0.0)
    column_weight = column_weight + jnp.where(
        positions == column_start[:, None] + 1, across[:, None], 0.0
    )
    row_part = jnp.where(positions == row_start[:, None], (1.0 - frac_down)[:, None], 0.0)
    row_part = row_part + jnp.where(positions == row_start[:, None] + 1, frac_down[:, None], 0.0)
    picked = (jnp.arange(slots, dtype=jnp.int32)[None, :, None] == slot_within[:, None]) & in_range[
        :, None
    ]
    row_weight = jnp.where(picked[:, :, None], row_part[:, None], 0.0)
    return (row_weight, column_weight)


def general_step(texel_atlas, observed, geometry, block_ids, pixel_slot, corner, bilinear_frac):
    tex_count = lax.axis_size("tex")
    owner_index = lax.axis_index("tex")
    own_blocks, channels, texels = texel_atlas.shape
    tiles_all = observed.shape[0]
    tiles_own = tiles_all // tex_count
    slots = block_ids.shape[2]
    groups = tiles_all // tex_count
    slot_blocks = block_ids[:, 0, :]
    slot_list = slot_blocks.reshape(-1)
    exact_mode = lax.Precision.HIGHEST

    def grouped(source):
        return source.reshape((groups, tex_count) + source.shape[1:])

    pixel_tables = (grouped(pixel_slot), grouped(corner), grouped(bilinear_frac))

    def widen(own_shard):
        return ring_gather(own_shard, "view").reshape((-1,) + own_shard.shape[1:])

    def pixels_of(whole_range):
        ranged = whole_range.shape[0]
        named = jnp.arange(ranged, dtype=jnp.int32)
        chooser = (jnp.clip(slot_list, 0, ranged - 1)[:, None] == named[None, :]).astype(jnp.float32)
        fetched = jnp.dot(chooser, whole_range.reshape(ranged, -1), precision=exact_mode)
        fetched = fetched.reshape(tiles_all, slots, channels, texels)

        def pixels_one_group(members):
            blocks, slot_part, corner_part, frac_part = members
            row_weight, column_weight = tables(
                slot_part, corner_part, frac_part, owner_index, slots
            )
            values = blocks.reshape(blocks.shape[0], slots, channels, BSIDE, BSIDE)
            middle = jnp.einsum("tjcyx,tjyp->tcxp", values, row_weight, precision=exact_mode)
            return jnp.sum(middle * column_weight[:, None], axis=2)

        partial_value = lax.map(pixels_one_group, (grouped(fetched),) + pixel_tables)
        partial_value = partial_value.reshape((tiles_all,) + partial_value.shape[2:])
        return ring_sum_scatter(grouped_by(partial_value, tex_count), "tex")

    def texel_terms(cotangent):
        gathered = ring_gather(cotangent, "tex").reshape((-1,) + cotangent.shape[1:])

        def texel_one_group(members):
            back_part, slot_part, corner_part, frac_part = members
            row_weight, column_weight = tables(
                slot_part, corner_part, frac_part, owner_index, slots
            )
            middle = back_part[:, :, None, :] * column_weight[:, None]
            values = jnp.einsum("tcxp,tjyp->tjcyx", middle, row_weight, precision=exact_mode)
            return values.reshape(values.shape[0] * slots, channels * texels)

        terms = lax.map(texel_one_group, (grouped(gathered),) + pixel_tables)
        return terms.reshape(tiles_all * slots, channels * texels)

    def owner_sums(terms):
        row_count = lax.axis_size("view") * own_blocks
        wanted = jnp.arange(row_count, dtype=jnp.int32)
        selector = (slot_list[None, :] == wanted[:, None]).astype(jnp.float32)
        summed = jnp.dot(selector, terms, precision=exact_mode, preferred_element_type=jnp.float32)
        return ring_sum_scatter(
            summed.reshape(row_count // own_blocks, own_blocks, channels, texels), "view"
        )

    atlas_range = widen(texel_atlas)
    base_params = pixels_of(atlas_range)
    geometry_own = lax.dynamic_slice_in_dim(geometry, owner_index * tiles_own, tiles_own, 0)
    observed_own = lax.dynamic_slice_in_dim(observed, owner_index * tiles_own, tiles_own, 0)

    def render(params):
        return shade(params, geometry_own)

    colors, backward = jax.vjp(render, base_params)

    def pullback(cotangent):
        return backward(cotangent)[0]

    unused, pushed = jax.vjp(pullback, jnp.zeros_like(colors))
    first_terms = texel_terms(backward(colors - observed_own)[0])
    gradient = owner_sums(first_terms)

    def inner_sums(values):
        return (jnp.sum(ring_gather(jnp.sum(ring_gather(values[0], "tex")), "view")),)

    update = jnp.zeros_like(gradient)
    residual = -gradient
    direction = residual
    norm_now = inner_sums((jnp.sum(residual * residual),))[0]
    for iteration in range(ITERS):
        applied = (
            owner_sums(texel_terms(backward(pushed(pixels_of(widen(direction)))[0])[0]))
            + DAMPING * direction
        )
        step_size = norm_now / inner_sums((jnp.sum(direction * applied),))[0]
        update = update + step_size * direction
        residual = residual - step_size * applied
        norm_next = inner_sums((jnp.sum(residual * residual),))[0]
        direction = residual + norm_next / norm_now * direction
        norm_now = norm_next
    return (update, residual)


MESH = pl.DeviceIdType.MESH
F32 = jnp.float32
BF16 = jnp.bfloat16
CHANNELS = 10
ROWS = 16
WINDOW = 512
PICKED = 256
SORTED = 1024
CHUNK = 896
TALL = CHUNK // 128
DENSE = 1792
NT = (((1,), (1,)), ((), ()))


def halves(values):
    high = values.astype(BF16)
    low = (values - high.astype(F32)).astype(BF16)
    return high, low


def iota(shape, axis):
    return lax.broadcasted_iota(jnp.int32, shape, axis)


def pack(ids, obs, geo, frac, slot, corner, picked, ordered):
    tiles, pixels = slot.shape
    slots = ids.shape[0]
    blocks = lax.axis_size("view")
    owner = lax.axis_index("tex")
    lanes = pixels // 128

    slot_now = slot[...]
    corner_now = corner[...].astype(F32)
    tile_of = iota((tiles, 128), 0)
    target = jnp.zeros((tiles, pixels), jnp.int32)
    for s in range(slots):
        named = jnp.zeros((tiles, 128), jnp.int32)
        for t in range(tiles):
            named = jnp.where(tile_of == t, ids[s, t] + 1, named)
        target = jnp.where(
            slot_now == owner * slots + s, jnp.concatenate([named] * lanes, axis=1), target
        )
    mine = jnp.where(target > 0, 1.0, 0.0)
    before = jnp.where(iota((128, 128), 0) < iota((128, 128), 1), 1.0, 0.0).astype(BF16)

    stacked = jnp.concatenate([mine[:, c * 128 : c * 128 + 128] for c in range(lanes)], axis=0)
    ahead = jnp.dot(stacked.astype(BF16), before, preferred_element_type=F32)
    base = jnp.zeros((tiles, 1), F32)
    places = []
    for c in range(lanes):
        places.append(ahead[c * tiles : c * tiles + tiles] + base)
        base = base + jnp.sum(mine[:, c * 128 : c * 128 + 128], axis=1, keepdims=True)
    place = jnp.where(target > 0, jnp.concatenate(places, axis=1), -1.0).astype(jnp.int32)
    over = jnp.max(jnp.where(base > PICKED, 1.0, 0.0))
    total = jnp.sum(base)
    over = jnp.maximum(over, jnp.where(total > SORTED, 1.0, 0.0))

    target_f = target.astype(F32)
    wanted = iota((PICKED, pixels), 0)
    for t in range(tiles):
        numbers = jnp.concatenate(
            [
                obs[:, t, :],
                geo[:, t, :],
                frac[t],
                corner_now[t : t + 1],
                target_f[t : t + 1],
                jnp.zeros((3, pixels), F32),
            ],
            axis=0,
        )
        both = jnp.concatenate(halves(numbers), axis=0)
        hot = jnp.where(wanted == place[t : t + 1], 1.0, 0.0).astype(BF16)
        got = lax.dot_general(both, hot, NT, preferred_element_type=F32)
        picked[:, t * PICKED : t * PICKED + PICKED] = got[:ROWS] + got[ROWS:]

    listed = tiles * PICKED
    groups = listed // 128
    target_row = picked[12:13, :]
    member = jnp.where(
        iota((blocks, listed), 0).astype(F32) + 1.0 == target_row, 1.0, 0.0
    )
    stacked = jnp.concatenate([member[:, c * 128 : c * 128 + 128] for c in range(groups)], axis=0)
    ahead = jnp.dot(stacked.astype(BF16), before, preferred_element_type=F32)
    base = jnp.zeros((blocks, 1), F32)
    places = []
    for c in range(groups):
        places.append(ahead[c * blocks : c * blocks + blocks] + base)
        base = base + jnp.sum(member[:, c * 128 : c * 128 + 128], axis=1, keepdims=True)
    over = jnp.maximum(over, jnp.max(jnp.where(base > WINDOW, 1.0, 0.0)))
    earlier = jnp.where(iota((blocks, blocks), 1) < iota((blocks, blocks), 0), 1.0, 0.0)
    first = jnp.dot(
        earlier,
        jnp.broadcast_to(base, (blocks, 128)),
        precision=lax.Precision.HIGHEST,
        preferred_element_type=F32,
    )
    place = jnp.concatenate(places, axis=1) + first[:, 0:1]
    place = jnp.sum(member * place, axis=0, keepdims=True)
    place = jnp.where(target_row > 0.0, place, -1.0).astype(jnp.int32)
    both = jnp.concatenate(halves(picked[...]), axis=0)
    for q in range(SORTED // 256):
        hot = jnp.where(iota((256, listed), 0) + q * 256 == place, 1.0, 0.0).astype(BF16)
        got = lax.dot_general(both, hot, NT, preferred_element_type=F32)
        ordered[:, q * 256 : q * 256 + 256] = got[:ROWS] + got[ROWS:]

    return over, first, jnp.broadcast_to(base, (blocks, 128))


def folded(listed, turn, size):
    window = pltpu.roll(listed, turn, axis=1)[:, :WINDOW]
    top, low = window[:8], window[8:]
    place = iota((8, WINDOW), 0)
    low = jnp.where((place == 3) & (iota((8, WINDOW), 1).astype(F32) >= size), -1.0, low)
    raised = pltpu.roll(low, 4, axis=0)
    pairs = []
    for g in range(0, WINDOW, 256):
        pairs.append(jnp.where(place[:, :128] < 4, low[:, g : g + 128], raised[:, g + 128 : g + 256]))
    return jnp.concatenate([top] + pairs, axis=1)


def unfolded(window):
    low = []
    for g in range(WINDOW, window.shape[1], 128):
        pair = window[:, g : g + 128]
        low += [pair, pltpu.roll(pair, 4, axis=0)]
    return jnp.concatenate([window[:, :WINDOW], jnp.concatenate(low, axis=1)], axis=0)


def far_first(me, count):
    deep = math.isqrt(count)
    apart = [(min(a, deep - a) + min(b, deep - b), a, b) for a in range(deep) for b in range(deep)]
    up, side = me // deep, lax.rem(me, deep)
    for _, a, b in sorted(apart, reverse=True)[:-1]:
        yield a * deep + b, lax.rem(up + a, deep) * deep + lax.rem(side + b, deep)


def greet(barrier, tex, view, owners, views):
    for _, peer in far_first(view, views):
        pl.semaphore_signal(barrier, inc=1, device_id=(tex, peer), device_id_type=MESH)
    for step in range(1, owners):
        peer = lax.rem(tex + step, owners)
        pl.semaphore_signal(barrier, inc=1, device_id=(peer, view), device_id_type=MESH)


def send(source, target, axis, peer, send_sem, recv_sem):
    me = lax.axis_index(axis)
    pltpu.make_async_remote_copy(
        src_ref=source,
        dst_ref=target.at[me],
        send_sem=send_sem,
        recv_sem=recv_sem,
        device_id={axis: peer},
        device_id_type=MESH,
    ).start()


def wait_all(target, sem):
    others = target.at[pl.ds(0, target.shape[0] - 1)]
    pltpu.make_async_copy(others, others, sem).wait()


def optics(params, geometry):
    roughness, tilt_x, tilt_y, occlusion = params[6], params[7], params[8], params[9]
    light, viewer = geometry[0:3], geometry[3:6]
    inverse_len = lax.rsqrt(1.0 + tilt_x * tilt_x + tilt_y * tilt_y)
    normal_x = tilt_x * inverse_len
    normal_y = tilt_y * inverse_len
    half = [a + b for a, b in zip(light, viewer)]
    scale = lax.rsqrt(half[0] * half[0] + half[1] * half[1] + half[2] * half[2])
    half = [a * scale for a in half]

    def facing(vector):
        cosine = normal_x * vector[0] + normal_y * vector[1] + inverse_len * vector[2]
        along_x = inverse_len * (vector[0] - normal_x * cosine)
        along_y = inverse_len * (vector[1] - normal_y * cosine)
        return cosine, along_x, along_y

    light_c, light_x, light_y = facing(light)
    view_c, view_x, view_y = facing(viewer)
    half_c, half_x, half_y = facing(half)
    miss = 1.0 - (viewer[0] * half[0] + viewer[1] * half[1] + viewer[2] * half[2])
    fifth = miss * miss
    fifth = fifth * fifth * miss
    square = roughness * roughness
    fourth = square * square
    inverse_d = 1.0 / (half_c * half_c * (fourth - 1.0) + 1.0)
    smith = 0.5 * square
    inverse_l = 1.0 / (light_c * (1.0 - smith) + smith)
    inverse_v = 1.0 / (view_c * (1.0 - smith) + smith)
    shape = 0.25 * inverse_d * inverse_d * inverse_l * inverse_v
    gloss = fourth * shape
    shape_slope = -4.0 * square * half_c * half_c * inverse_d
    shape_slope = shape_slope - 0.5 * (1.0 - light_c) * inverse_l - 0.5 * (1.0 - view_c) * inverse_v
    gloss_square = 2.0 * square * shape + gloss * shape_slope
    gloss_half = -4.0 * gloss * half_c * (fourth - 1.0) * inverse_d
    gloss_light = -gloss * (1.0 - smith) * inverse_l
    gloss_view = -gloss * (1.0 - smith) * inverse_v
    gloss_x = gloss_half * half_x + gloss_light * light_x + gloss_view * view_x
    gloss_y = gloss_half * half_y + gloss_light * light_y + gloss_view * view_y
    lit = occlusion * light_c
    fresnel = [params[3 + c] + (1.0 - params[3 + c]) * fifth for c in range(3)]
    total = [params[c] + gloss * fresnel[c] for c in range(3)]
    factors = [
        lit,
        lit * gloss * (1.0 - fifth),
        lit * gloss_square * 2.0 * roughness,
        occlusion * light_x,
        lit * gloss_x,
        occlusion * light_y,
        lit * gloss_y,
        light_c,
    ]
    return factors + total + fresnel, [lit * t for t in total]


def push(tangent, factors):
    albedo, specular, rough, ex, fx, ey, fy, shine = factors[:8]
    total, fresnel = factors[8:11], factors[11:14]
    on_total = ex * tangent[7] + ey * tangent[8] + shine * tangent[9]
    on_fresnel = rough * tangent[6] + fx * tangent[7] + fy * tangent[8]
    return [
        albedo * tangent[c] + specular * tangent[3 + c] + total[c] * on_total + fresnel[c] * on_fresnel
        for c in range(3)
    ]


def pull(colors, factors):
    albedo, specular, rough, ex, fx, ey, fy, shine = factors[:8]
    total, fresnel = factors[8:11], factors[11:14]
    e = total[0] * colors[0] + total[1] * colors[1] + total[2] * colors[2]
    f = fresnel[0] * colors[0] + fresnel[1] * colors[1] + fresnel[2] * colors[2]
    return (
        [albedo * c for c in colors]
        + [specular * c for c in colors]
        + [rough * f, ex * e + fx * f, ey * e + fy * f, shine * e]
    )


def whole_kernel(
    ids, obs_in, geo_in, frac_in, slot_in, corner_in, atlas_in, update, residual, flag,
    obs, geo, frac, slot, corner, atlas, picked, ordered, windows, landed, pixels, field,
    across, down, turned, stood, slopes, seen_start, seen_first, gathered, near, far,
    read_sems, send_window, recv_window, send_near, recv_near, send_far, recv_far,
):
    tex, me = lax.axis_index("tex"), lax.axis_index("view")
    senders, owners = landed.shape[0], near.shape[0]
    half_rows = CHANNELS * BSIDE // 2
    lane = iota((half_rows, 128), 1)
    reads = [
        pltpu.make_async_copy(source, target, read_sems.at[k])
        for k, (source, target) in enumerate(
            [
                (slot_in, slot),
                (corner_in, corner),
                (obs_in, obs),
                (geo_in, geo),
                (frac_in, frac),
                (atlas_in, atlas),
            ]
        )
    ]
    for read in reads:
        read.start()
    barrier = pltpu.get_barrier_semaphore()
    greet(barrier, tex, me, owners, senders)
    for read in reads:
        read.wait()
    over, first, sizes = pack(ids, obs, geo, frac, slot, corner, picked, ordered)
    turns = jnp.where(first > 0.0, jnp.maximum(float(SORTED) - first, 0.0), 0.0).astype(jnp.int32)
    listed = ordered[...]
    pl.semaphore_wait(barrier, owners + senders - 2)

    def window_for(peer):
        named = iota(turns.shape, 0) == peer
        turn = jnp.sum(jnp.where(named, turns, 0)[:, 0:1])
        size = jnp.sum(jnp.where(named, sizes, 0.0)[:, 0:1], axis=0, keepdims=True)
        return folded(listed, turn, size)

    for step, peer in far_first(me, senders):
        windows[step] = window_for(peer)
        send(windows.at[step], landed, "view", peer, send_window, recv_window)
    landed[me] = window_for(me)


    def hold(values):
        high, low = halves(values)
        high, low = high.astype(F32), low.astype(F32)
        left = jnp.where(lane < BSIDE, high, pltpu.roll(low, BSIDE, axis=1)).astype(BF16)
        right = jnp.where(lane < BSIDE, pltpu.roll(high, BSIDE, axis=1), low).astype(BF16)
        field[:half_rows, :128] = left
        field[:half_rows, 128:] = left
        field[half_rows:, :128] = right
        field[half_rows:, 128:] = right

    def sample(c, rows):
        seen = jnp.dot(field[...], across[c], preferred_element_type=F32)
        seen = seen.reshape(2, CHANNELS, BSIDE // 2, CHUNK) * rows
        seen = jnp.sum(seen[0] + seen[1], axis=1)
        for j in range(TALL):
            turned[2 * c, :, j, :] = seen[:, j * 128 : j * 128 + 128]
        return [turned[2 * c, k] for k in range(CHANNELS)]

    def spread(c, rows, back):
        for k in range(CHANNELS):
            turned[2 * c + 1, k] = back[k]
        back = jnp.concatenate([turned[2 * c + 1, :, j, :] for j in range(TALL)], axis=1)
        terms = (back.reshape(1, CHANNELS, 1, CHUNK) * rows).reshape(2 * half_rows, CHUNK)
        high, low = halves(terms)
        columns = across[c, BSIDE : 3 * BSIDE, :]
        gathered[...] += lax.dot_general(high, columns, NT, preferred_element_type=F32)
        gathered[...] += lax.dot_general(low, columns, NT, preferred_element_type=F32)

    def collected():
        left, right = gathered[:half_rows], gathered[half_rows:]
        left = left + pltpu.roll(left, BSIDE, axis=1)
        right = right + pltpu.roll(right, BSIDE, axis=1)
        return jnp.where(lane < BSIDE, left, right)

    hold(atlas[...])
    gathered[...] = jnp.zeros(gathered.shape, F32)
    wait_all(landed, recv_window)
    arrived = [unfolded(landed[j]) for j in range(senders)]
    live = [jnp.where(window[11:12] >= 0.0, 1.0, 0.0) for window in arrived]
    counts = jnp.sum(jnp.concatenate(live, axis=0), axis=1, keepdims=True)
    earlier = jnp.where(iota((senders, senders), 1) < iota((senders, senders), 0), 1.0, 0.0)
    begins = jnp.dot(
        earlier,
        jnp.broadcast_to(counts, (senders, 128)),
        precision=lax.Precision.HIGHEST,
        preferred_element_type=F32,
    )
    begins = jnp.minimum(begins, float(DENSE - 1)).astype(jnp.int32)
    dense = jnp.zeros((ROWS, DENSE), F32)
    for j in range(senders):
        window = jnp.where(live[j] > 0.0, arrived[j], 0.0)
        window = jnp.concatenate([window, jnp.zeros((ROWS, DENSE - WINDOW), F32)], axis=1)
        dense = dense + pltpu.roll(window, begins[j, 0], axis=1)
    pixels[...] = dense
    for c in range(DENSE // CHUNK):
        for j in range(TALL):
            at = c * CHUNK + j * 128
            stood[c, :, j, :] = dense[:, at : at + 128]
    count = jnp.sum(counts)
    over = jnp.maximum(over, jnp.where(count > DENSE, 1.0, 0.0))
    chunks = DENSE // CHUNK

    def first_pass(c):
        numbers = pixels[:, c * CHUNK : c * CHUNK + CHUNK]
        numbers = [numbers[k : k + 1] for k in range(ROWS)]
        used = (iota((1, CHUNK), 1) + c * CHUNK).astype(F32) < count
        frac_x, frac_y, spot = numbers[9:12]
        row = jnp.floor((spot + 0.5) * (1.0 / (BSIDE - 1)))
        column = spot - row * (BSIDE - 1)
        at = iota((BSIDE, CHUNK), 0).astype(F32)
        weight = jnp.where(at == column, 1.0 - frac_x, jnp.where(at == column + 1.0, frac_x, 0.0))
        high, low = halves(weight)
        across[c] = jnp.concatenate([high, high, low, low], axis=0)
        at = iota((BSIDE, CHUNK), 0)
        at = jnp.where(at < BSIDE // 2, 2 * at, 2 * at - (BSIDE - 1)).astype(F32)
        weight = jnp.where(at == row, 1.0 - frac_y, jnp.where(at == row + 1.0, frac_y, 0.0))
        weight = jnp.where(used, weight, 0.0)
        down[c] = weight
        rows = weight.reshape(2, 1, BSIDE // 2, CHUNK)
        standing = [stood[c, k] for k in range(9)]
        factors, colors = optics(sample(c, rows), standing[3:9])
        place = iota((TALL, 128), 0) * 128 + iota((TALL, 128), 1) + c * CHUNK
        used = place.astype(F32) < count
        factors = [jnp.where(used, factor, 0.0) for factor in factors]
        for k, factor in enumerate(factors):
            slopes[c, k] = factor
        errors = [jnp.where(used, a - b, 0.0) for a, b in zip(colors, standing[0:3])]
        spread(c, rows, pull(errors, factors))

    for c in range(chunks):
        first_pass(c)
    start_now = -collected()

    def factors_of(c):
        return [slopes[c, k] for k in range(14)]

    def seen_of(c, kept):
        rows = down[c].reshape(2, 1, BSIDE // 2, CHUNK)
        colors = push(sample(c, rows), factors_of(c))
        for k in range(3):
            kept[c, k] = colors[k]

    def spread_seen(c, kept):
        rows = down[c].reshape(2, 1, BSIDE // 2, CHUNK)
        spread(c, rows, pull([kept[c, k] for k in range(3)], factors_of(c)))

    def start_pass(c):
        seen_of(c, seen_start)
        spread_seen(c, seen_start)

    def first_seen(c):
        seen_of(c, seen_first)

    hold(start_now)
    gathered[...] = jnp.zeros(gathered.shape, F32)
    for c in range(chunks):
        start_pass(c)
    first_now = collected() + DAMPING * start_now
    hold(first_now)
    gathered[...] = jnp.zeros(gathered.shape, F32)
    for c in range(chunks):
        first_seen(c)

    start_start = jnp.sum(start_now * start_now)
    start_first = jnp.sum(start_now * first_now)
    guess = jnp.where(start_first > 0.0, start_start / jnp.where(start_first > 0.0, start_first, 1.0), 0.0)
    rest = start_now - guess * first_now
    rest_rest = jnp.sum(rest * rest)
    rest_first = jnp.sum(rest * first_now)
    first_first = jnp.sum(first_now * first_now)
    from_start, from_first = seen_start[...], seen_first[...]
    from_rest = from_start - guess * from_first
    found = [
        start_start,
        start_first,
        rest_rest,
        rest_first,
        first_first,
        jnp.sum(from_rest * from_rest) + DAMPING * rest_rest,
        jnp.sum(from_rest * from_first) + DAMPING * rest_first,
        jnp.sum(from_first * from_first) + DAMPING * first_first,
        guess,
    ]
    place = iota((1, 128), 1)
    line = jnp.where(place == len(found), over, 0.0)
    for k, value in enumerate(found):
        line = jnp.where(place == k, value, line)
    near[tex] = line
    for step in range(1, owners):
        send(near.at[tex], near, "tex", lax.rem(tex + step, owners), send_near, recv_near)
    spread_seen(0, seen_first)
    wait_all(near, recv_near)
    far[me] = near[...]
    for _, peer in far_first(me, senders):
        send(near, far, "view", peer, send_far, recv_far)
    for c in range(1, chunks):
        spread_seen(c, seen_first)
    second_now = collected() + DAMPING * first_now
    wait_all(far, recv_far)
    table = far[...].reshape(owners * senders, 128)
    column = [table[:, k : k + 1] for k in range(10)]

    def added(values):
        return jnp.sum(values, axis=0, keepdims=True)

    start_start, start_first = added(column[0]), added(column[1])
    one = start_start / start_first
    change = column[8] - one
    norm = added(column[2] + change * (2.0 * column[3] + change * column[4]))
    turn = norm / start_start
    cross = added(column[3] + change * column[4])
    curve = added(column[5] + change * (2.0 * column[6] + change * column[7]))
    curve = curve + 2.0 * turn * cross + turn * turn * start_first
    two = norm / curve
    near_part = one + two * (1.0 + turn)
    update[...] = near_part * start_now - one * two * first_now
    residual[...] = start_now - near_part * first_now + one * two * second_now
    flag[...] = jnp.broadcast_to(added(column[9]), flag.shape)
    wait_all(landed, send_window)
    wait_all(near, send_near)
    wait_all(far, send_far)


def hand_on_kernel(update, residual, update_out, residual_out, sems):
    copies = [
        pltpu.make_async_copy(update, update_out, sems.at[0]),
        pltpu.make_async_copy(residual, residual_out, sems.at[1]),
    ]
    for copy in copies:
        copy.start()
    for copy in copies:
        copy.wait()


def in_vmem(count):
    return [pl.BlockSpec(memory_space=pltpu.VMEM)] * count


def per_device(texel_atlas, observed, geometry, block_ids, pixel_slot, corner, bilinear_frac):
    owners, views = lax.axis_size("tex"), lax.axis_size("view")
    tiles, slots = block_ids.shape[0], block_ids.shape[2]
    half_rows = CHANNELS * BSIDE // 2
    shaped = jax.ShapeDtypeStruct

    update, residual, flag = pl.pallas_call(
        whole_kernel,
        out_shape=(shaped((half_rows, 128), F32),) * 2 + (shaped((1, 128), F32),),
        in_specs=[pl.BlockSpec(memory_space=pltpu.SMEM)] + [pl.BlockSpec(memory_space=pl.ANY)] * 6,
        out_specs=tuple(in_vmem(3)),
        scratch_shapes=[
            pltpu.VMEM((3, tiles, pixel_slot.shape[1]), F32),
            pltpu.VMEM((6, tiles, pixel_slot.shape[1]), F32),
            pltpu.VMEM(bilinear_frac.shape, F32),
            pltpu.VMEM(pixel_slot.shape, jnp.int32),
            pltpu.VMEM(pixel_slot.shape, jnp.int32),
            pltpu.VMEM((half_rows, 128), F32),
            pltpu.VMEM((ROWS, tiles * PICKED), F32),
            pltpu.VMEM((ROWS, SORTED), F32),
            pltpu.VMEM((views, 8, WINDOW * 3 // 2), F32),
            pltpu.VMEM((views, 8, WINDOW * 3 // 2), F32),
            pltpu.VMEM((ROWS, DENSE), F32),
            pltpu.VMEM((2 * half_rows, 256), BF16),
            pltpu.VMEM((DENSE // CHUNK, 4 * BSIDE, CHUNK), BF16),
            pltpu.VMEM((DENSE // CHUNK, BSIDE, CHUNK), F32),
            pltpu.VMEM((2 * DENSE // CHUNK, CHANNELS, TALL, 128), F32),
            pltpu.VMEM((DENSE // CHUNK, ROWS, TALL, 128), F32),
            pltpu.VMEM((DENSE // CHUNK, 14, TALL, 128), F32),
            pltpu.VMEM((DENSE // CHUNK, 3, TALL, 128), F32),
            pltpu.VMEM((DENSE // CHUNK, 3, TALL, 128), F32),
            pltpu.VMEM((2 * half_rows, 128), F32),
            pltpu.VMEM((owners, 1, 128), F32),
            pltpu.VMEM((views, owners, 1, 128), F32),
        ]
        + [pltpu.SemaphoreType.DMA((6,))]
        + [pltpu.SemaphoreType.DMA] * 6,
        compiler_params=pltpu.CompilerParams(
            collective_id=0, has_side_effects=True, vmem_limit_bytes=56 << 20
        ),
    )(
        block_ids.reshape(tiles, slots).T,
        observed.transpose(1, 0, 2),
        geometry.transpose(1, 0, 2),
        bilinear_frac,
        pixel_slot,
        corner,
        texel_atlas.reshape(half_rows, 128),
    )

    def quick():
        handed = pl.pallas_call(
            hand_on_kernel,
            out_shape=(shaped((half_rows, 128), F32),) * 2,
            in_specs=[pl.BlockSpec(memory_space=pl.ANY)] * 2,
            out_specs=(pl.BlockSpec(memory_space=pl.ANY),) * 2,
            scratch_shapes=[pltpu.SemaphoreType.DMA((2,))],
        )(update, residual)
        return tuple(part.reshape(texel_atlas.shape) for part in handed)

    def general():
        return general_step(
            texel_atlas, observed, geometry, block_ids, pixel_slot, corner, bilinear_frac
        )

    return lax.cond(flag[0, 0] > 0.0, general, quick)


def solution(mesh):
    in_specs = (
        P(("tex", "view"), None, None),
        P("view", None, None),
        P("view", None, None),
        P("view", "tex", None),
        P("view", None),
        P("view", None),
        P("view", None, None),
    )
    out_specs = (P(("tex", "view"), None, None), P(("tex", "view"), None, None))
    return jax.shard_map(
        per_device, mesh=mesh, in_specs=in_specs, out_specs=out_specs, check_vma=False
    )
```
